32 devices in a mesh: wide: 8 (over y, x, core), narrow: 4 (over z).
Axes of the slice: x: 2, y: 2, z: 4, core: 2. Of those that a mesh axis runs over, the one named last changes fastest.
Arguments:
- tokens: bfloat16 [8192, 768], P(('wide', 'narrow')), may hold values from -6 to 6
- cotangent: bfloat16 [8192, 768], P(('wide', 'narrow')), may hold values from -6 to 6
- horizons: int32 [8], P('wide'), may hold values from 1024 to 2048
- qkv_weight: bfloat16 [2, 768, 2304], replicated, may hold values from -0.21875 to 0.21875
- out_weight: bfloat16 [2, 768, 768], replicated, may hold values from -1.75 to 1.75
- ffn_in_weight: bfloat16 [2, 768, 3072], replicated, may hold values from -0.21875 to 0.21875
- ffn_out_weight: bfloat16 [2, 3072, 768], replicated, may hold values from -0.109375 to 0.109375
- qkv_bias: bfloat16 [2, 2304], replicated, may hold values from -1 to 1
- ffn_in_bias: bfloat16 [2, 3072], replicated, may hold values from -1.5 to 1.5
- model_biases: bfloat16 [2, 4, 768], replicated, may hold values from -1.5 to 1.5
- norm_gains: bfloat16 [2, 2, 768], replicated, may hold values from 0.5 to 1.5
Outputs:
- output: bfloat16 [8192, 768], P(('wide', 'narrow'))
- input_grad: float32 [8192, 768], P(('wide', 'narrow'))
- grad_qkv_weight: float32 [2, 768, 2304], P(None, 'wide', 'narrow')
- grad_out_weight: float32 [2, 768, 768], P(None, 'wide', 'narrow')
- grad_ffn_in_weight: float32 [2, 768, 3072], P(None, 'wide', 'narrow')
- grad_ffn_out_weight: float32 [2, 3072, 768], P(None, 'wide', 'narrow')
- grad_qkv_bias: float32 [2, 2304], P(None, 'narrow')
- grad_ffn_in_bias: float32 [2, 3072], P(None, 'narrow')
- grad_model_biases: float32 [2, 4, 768], P(None, None, 'narrow')
- grad_norm_gains: float32 [2, 2, 768], P(None, None, 'narrow')
The draws below stay inside these ranges and needn't reach their ends.
All inputs are finite; a program needn't handle non-finite values.
Results may differ from the reference program's by a relative error of at most 0.014.
Values may be sent and summed in bfloat16 or wider, within the bound.
No kernel may reach another device: no remote copies, remote signals or barrier semaphores. Data moves between devices by JAX's collectives and lax.ppermute only.
A program may use at most 576 MiB of HBM per device.

```python
import math
import jax
import jax.numpy as jnp
from jax import lax

D = 768
HEADS = 12
HEAD_DIM = 64
FF = 3072
LAYERS = 2
SEQ_LEN = 1024
STRETCH = 64
SEQ_GROUP = 1
SEQUENCES = 8
TOKENS = 8192
N_WIDE = 8


def touch_ends(entries, stream_key, least, high):
    dims = entries.shape
    index_at = [jax.random.randint(jax.random.fold_in(stream_key, axis), (), 0, dims[axis]) for axis in range(len(dims))]
    entries = entries.at[tuple(index_at)].set(least)
    longest = dims.index(max(dims))
    index_at[longest] = (index_at[longest] + 1) % dims[longest]
    return entries.at[tuple(index_at)].set(high)


def shard_levels(own_key, extent, pieces, low, top_value):
    def one(position, blocks):
        steps = jax.random.uniform(jax.random.fold_in(jax.random.fold_in(own_key, 6), position), (blocks,), jnp.float32, low / len(pieces), top_value / len(pieces))
        return jnp.repeat(jnp.exp(steps), extent[position] // blocks).reshape((-1,) + (1,) * (len(extent) - position - 1))

    level = one(*pieces[0])
    for cut in pieces[1:]:
        level = level * one(*cut)
    return level


def scatter_about(key, extent, spread, reach, pieces=(), held_as=jnp.bfloat16):
    array = spread * jax.random.normal(key, extent, jnp.float32)
    if pieces:
        array = array * shard_levels(key, extent, pieces, -0.22, 0.18)
    return jnp.clip(array, -reach, reach).astype(held_as)


def setup_inputs(seed: int = 0) -> dict:
    splits = jax.random.split(jax.random.key(seed), 12)
    return {
        "tokens": scatter_about(splits[0], (TOKENS, D), 1.0, 6.0, ((0, 32),)),
        "cotangent": scatter_about(splits[1], (TOKENS, D), 1.0, 6.0, ((0, 32),)),
        "horizons": touch_ends(jax.random.randint(splits[2], (SEQUENCES,), SEQ_LEN, 2 * SEQ_LEN + 1), jax.random.fold_in(splits[2], 1), SEQ_LEN, 2 * SEQ_LEN).astype(jnp.int32),
        "qkv_weight": scatter_about(splits[3], (LAYERS, D, 3 * D), D ** -0.5, 0.21875),
        "out_weight": scatter_about(splits[4], (LAYERS, D, D), (max(1, 16 * D // SEQ_LEN)) ** -0.5, 1.75),
        "ffn_in_weight": scatter_about(splits[5], (LAYERS, D, FF), D ** -0.5, 0.21875),
        "ffn_out_weight": scatter_about(splits[6], (LAYERS, FF, D), FF ** -0.5, 0.109375),
        "qkv_bias": scatter_about(splits[7], (LAYERS, 3 * D), 0.2, 1.0),
        "ffn_in_bias": scatter_about(splits[8], (LAYERS, FF), 0.3, 1.5),
        "model_biases": scatter_about(splits[9], (LAYERS, 4, D), 0.3, 1.5),
        "norm_gains": jnp.clip(1.0 + 0.1 * jax.random.normal(splits[10], (LAYERS, 2, D), jnp.float32), 0.5, 1.5).astype(jnp.bfloat16),
    }


@jax.custom_vjp
def low(v):
    return lax.optimization_barrier(v.astype(jnp.bfloat16)).astype(jnp.float32)

@jax.custom_vjp
def low_back(v):
    return v

def low_keep(v):
    return (low(v), None)

def low_pass(kept, grad):
    return (grad,)

def back_keep(v):
    return (v, None)

def back_low(kept, grad):
    return (low(grad),)
low.defvjp(low_keep, low_pass)
low_back.defvjp(back_keep, back_low)
PRECISE = lax.Precision.HIGHEST
NORM_EPS = 1e-05

def linear_mix(query, key_in, value_in, horizon_block):
    seq_count = query.shape[0]
    length = query.shape[1]
    head_count = query.shape[2]
    head_width = query.shape[3]
    block_count = length // STRETCH
    places = jnp.arange(length, dtype=jnp.float32)
    angles = 0.5 * math.pi * places[None, :] / horizon_block.astype(jnp.float32)[:, None]
    cosine = jnp.cos(angles)[:, :, None, None]
    sine = jnp.sin(angles)[:, :, None, None]
    query_feat = jax.nn.softplus(query)
    key_feat = jax.nn.softplus(key_in)
    query_both = jnp.concatenate([query_feat * cosine, query_feat * sine], axis=-1)
    key_both = jnp.concatenate([key_feat * cosine, key_feat * sine], axis=-1)
    block_shape = (seq_count, block_count, STRETCH, head_count, 2 * head_width)
    query_both = query_both.reshape(block_shape)
    key_both = key_both.reshape(block_shape)
    value_blocks = value_in.reshape(seq_count, block_count, STRETCH, head_count, head_width)
    states = jnp.einsum('sbjhf,sbjhe->sbhfe', key_both, value_blocks, precision=PRECISE)
    totals = lax.optimization_barrier(jnp.sum(key_both, axis=2))
    states_before = jnp.cumsum(jnp.concatenate([jnp.zeros_like(states[:, :1]), states[:, :-1]], axis=1), axis=1)
    totals_before = jnp.cumsum(jnp.concatenate([jnp.zeros_like(totals[:, :1]), totals[:, :-1]], axis=1), axis=1)
    inter_num = jnp.einsum('sbihf,sbhfe->sbihe', query_both, states_before, precision=PRECISE)
    inter_den = jnp.einsum('sbihf,sbhf->sbih', query_both, totals_before, precision=PRECISE)
    scores = jnp.einsum('sbihf,sbjhf->sbhij', query_both, key_both, precision=PRECISE)
    causal = jnp.arange(STRETCH)[:, None] >= jnp.arange(STRETCH)[None, :]
    scores = jnp.where(causal, scores, 0.0)
    intra_num = jnp.einsum('sbhij,sbjhe->sbihe', scores, value_blocks, precision=PRECISE)
    intra_den = jnp.einsum('sbhij->sbih', scores)
    numerator = inter_num + intra_num
    denominator = inter_den + intra_den
    return (numerator / denominator[..., None]).reshape(seq_count, length, head_count, head_width)

def matmul_high(left, right):
    return jnp.dot(left, right, precision=PRECISE, preferred_element_type=jnp.float32)

def layer_norm(total, gain_vec, bias_vec):
    row_mean = lax.optimization_barrier(jnp.mean(total, axis=-1, keepdims=True))
    centred = total - row_mean
    variance = lax.optimization_barrier(jnp.mean(centred * centred, axis=-1, keepdims=True))
    return centred * lax.rsqrt(variance + NORM_EPS) * gain_vec + bias_vec

def block_forward(current, params, horizon_block):
    qkv_weight, out_weight, ffn_in_weight, ffn_out_weight, qkv_bias, ffn_in_bias, model_biases, norm_gains = params
    row_count = current.shape[0]
    for layer_at in range(LAYERS):
        packed = matmul_high(low(current), qkv_weight[layer_at]) + qkv_bias[layer_at]
        packed = low(low_back(packed)).reshape(SEQ_GROUP, SEQ_LEN, HEADS, 3, HEAD_DIM)
        mixed_seq = linear_mix(packed[:, :, :, 0], packed[:, :, :, 1], packed[:, :, :, 2], horizon_block)
        mixed_tok = low(low_back(mixed_seq.reshape(row_count, D)))
        branch = low_back(matmul_high(mixed_tok, out_weight[layer_at]) + model_biases[layer_at, 0])
        middle = layer_norm(current + branch, norm_gains[layer_at, 0], model_biases[layer_at, 2])
        pre_act = low_back(matmul_high(low(middle), ffn_in_weight[layer_at]) + ffn_in_bias[layer_at])
        hidden = low(jax.nn.gelu(pre_act, approximate=False))
        branch_two = low_back(matmul_high(hidden, ffn_out_weight[layer_at]) + model_biases[layer_at, 1])
        current = layer_norm(middle + branch_two, norm_gains[layer_at, 1], model_biases[layer_at, 3])
    return current

def reference(tokens, cotangent, horizons, qkv_weight, out_weight, ffn_in_weight, ffn_out_weight, qkv_bias, ffn_in_bias, model_biases, norm_gains):
    params = (qkv_weight.astype(jnp.float32), out_weight.astype(jnp.float32), ffn_in_weight.astype(jnp.float32), ffn_out_weight.astype(jnp.float32), qkv_bias.astype(jnp.float32), ffn_in_bias.astype(jnp.float32), model_biases.astype(jnp.float32), norm_gains.astype(jnp.float32))
    group_rows = SEQ_GROUP * SEQ_LEN
    token_blocks = tokens.astype(jnp.float32).reshape(N_WIDE, group_rows, D)
    cot_blocks = cotangent.astype(jnp.float32).reshape(N_WIDE, group_rows, D)
    horizon_blocks = horizons.astype(jnp.int32).reshape(N_WIDE, SEQ_GROUP)

    def visit(totals, block):
        block_tokens, block_cot, horizon_block = block

        def forward(current, weights):
            return block_forward(current, weights, horizon_block)
        result, pullback = jax.vjp(forward, block_tokens, params)
        grad_rows, grad_params = pullback(block_cot)
        totals = jax.tree.map(jnp.add, totals, grad_params)
        return (totals, (result.astype(jnp.bfloat16), grad_rows))
    zeros_init = jax.tree.map(jnp.zeros_like, params)
    totals, stacked = lax.scan(visit, zeros_init, (token_blocks, cot_blocks, horizon_blocks))
    output = stacked[0].reshape(TOKENS, D)
    input_grad = stacked[1].reshape(TOKENS, D)
    return (output, input_grad, totals[0], totals[1], totals[2], totals[3], totals[4], totals[5], totals[6], totals[7])
```

```python
import functools
import math

import jax
import jax.numpy as jnp
from jax import lax
from jax.experimental import pallas as pl
from jax.experimental.pallas import tpu as pltpu
from jax.sharding import PartitionSpec as P

D = 768
HEADS = 12
HEAD_DIM = 64
FF = 3072
LAYERS = 2
PAIRS = HEADS // 2
NORM_EPS = 1e-05
LANES = 128
STATE_ROWS = PAIRS * LANES + LANES

BF = jnp.bfloat16
F32 = jnp.float32
VMEM = pl.BlockSpec(memory_space=pltpu.VMEM)
SMEM = pl.BlockSpec(memory_space=pltpu.SMEM)
ANY = pl.BlockSpec(memory_space=pl.ANY)


def nn(a, b):
    return lax.dot_general(a, b, (((1,), (0,)), ((), ())), preferred_element_type=F32)


def nt(a, b):
    return lax.dot_general(a, b, (((1,), (1,)), ((), ())), preferred_element_type=F32)


def tn(a, b):
    return lax.dot_general(a, b, (((0,), (0,)), ((), ())), preferred_element_type=F32)


def low(v):
    return v.astype(BF)


def softplus(u):
    return jnp.maximum(u, 0.0) + jnp.log1p(jnp.exp(-jnp.abs(u)))


def sigmoid(u):
    return 1.0 / (1.0 + jnp.exp(-u))


def swap(v):
    return pltpu.roll(v, HEAD_DIM, 1)


def left_half(rows):
    return lax.broadcasted_iota(jnp.int32, (rows, LANES), 1) < HEAD_DIM


def tile(v, at):
    return v[:, at * LANES : (at + 1) * LANES]


def row_mean(v):
    return jnp.mean(v, axis=-1, keepdims=True)


def norm_apply(total, gain, shift):
    centred = total - row_mean(total)
    scale = lax.rsqrt(row_mean(centred * centred) + NORM_EPS)
    normal = centred * scale
    return normal * gain + shift, normal, scale


def norm_back(upstream, normal, scale, gain):
    grad = upstream * gain
    return scale * (grad - row_mean(grad) - normal * row_mean(grad * normal))


def column_sum(v):
    return jnp.sum(v, axis=0, keepdims=True)


def spread(v, rows):
    return jnp.broadcast_to(v, (rows, LANES))


def vector(ref, layer, row=None):
    if row is None:
        return ref[...].astype(F32)[layer : layer + 1]
    return ref[layer].astype(F32)[row : row + 1]


def call(kernel, outs, in_specs, scratch, flops, byte_count, **more):
    return pl.pallas_call(
        kernel,
        out_shape=outs,
        in_specs=in_specs,
        out_specs=jax.tree.map(lambda _: VMEM, outs),
        scratch_shapes=scratch,
        compiler_params=pltpu.CompilerParams(vmem_limit_bytes=48 * 1024 * 1024),
        cost_estimate=pl.CostEstimate(
            flops=int(flops), bytes_accessed=int(byte_count), transcendentals=0
        ),
        **more,
    )


def shape(*dims, dtype=F32):
    return jax.ShapeDtypeStruct(dims, dtype)


def project_kernel(layer, x_ref, w_hbm, b_ref, cs_ref, packed_ref, xt_ref, st_ref, wbuf, sems):
    parts = wbuf.shape[0]
    copies = [
        pltpu.make_async_copy(w_hbm.at[layer, :, pl.ds(D * j, D)], wbuf.at[j], sems.at[j])
        for j in range(parts)
    ]
    for copy in copies:
        copy.start()
    rows = x_ref.shape[0]
    x = x_ref[...].astype(F32)
    xb = low(x)
    xt_ref[...] = low(x.T)
    cs = cs_ref[...]
    lo = left_half(rows)
    lo_state = left_half(LANES)
    lane = lax.broadcasted_iota(jnp.int32, (LANES, LANES), 1)
    bias = vector(b_ref, layer)
    totals = jnp.zeros((LANES, LANES), F32)
    for j in range(parts):
        copies[j].wait()
        pk = low(nn(xb, wbuf[j]) + bias[:, D * j : D * (j + 1)])
        packed_ref[:, D * j : D * (j + 1)] = pk
        pf = pk.astype(F32)
        for p in range(2):
            t0, t1, t2 = (tile(pf, 3 * p + i) for i in range(3))
            sp0 = softplus(t0)
            sp2 = softplus(t2)
            kf0 = low(jnp.where(lo, swap(sp0), sp0) * cs)
            kf1 = low(jnp.where(lo, sp2, swap(sp2)) * cs)
            s0 = tn(kf0, low(jnp.where(lo, t1, 1.0)))
            s1 = tn(kf1, low(jnp.where(lo, 1.0, t2)))
            pair = 2 * j + p
            st_ref[pair * LANES : (pair + 1) * LANES, :] = low(jnp.where(lo_state, s0, s1))
            totals = jnp.where(lane == HEAD_DIM + 2 * pair, s0, totals)
            totals = jnp.where(lane == 2 * pair + 1, s1, totals)
    st_ref[PAIRS * LANES :, :] = low(totals)


def project(layer, x, w, b, cs):
    rows = x.shape[0]
    return call(
        functools.partial(project_kernel, layer),
        (
            shape(rows, 3 * D, dtype=BF),
            shape(D, rows, dtype=BF),
            shape(STATE_ROWS, LANES, dtype=BF),
        ),
        [VMEM, ANY, VMEM, VMEM],
        [pltpu.VMEM((3, D, D), BF), pltpu.SemaphoreType.DMA((3,))],
        2 * rows * D * 3 * D,
        2 * D * 3 * D,
    )(x, w, b, cs)


def inside_kernel(packed_ref, cm_ref, num_ref, den_ref, sq_ref):
    rows = packed_ref.shape[0]
    lo = left_half(rows)
    cm = cm_ref[...]
    for pair in range(PAIRS):
        at = pair * 3 * LANES
        t0, t1, t2 = (
            packed_ref[:, at + i * LANES : at + (i + 1) * LANES].astype(F32) for i in range(3)
        )
        sp0, sp1, sp2 = softplus(t0), softplus(t1), softplus(t2)
        a0 = nt(low(jnp.where(lo, sp0, 0.0)), low(swap(sp0)))
        a1 = nt(low(jnp.where(lo, 0.0, sp1)), low(swap(sp2)))
        n0 = nn(low(a0 * cm), low(jnp.where(lo, t1, 1.0)))
        n1 = nn(low(a1 * cm), low(jnp.where(lo, 1.0, t2)))
        here = slice(pair * LANES, (pair + 1) * LANES)
        num_ref[:, here] = jnp.where(lo, n0, n1)
        den_ref[:, here] = swap(jnp.where(lo, n1, n0))
        sq_ref[:, here] = low(jnp.where(lo, sp0, sp1))


def inside(packed, cm):
    rows = packed.shape[0]
    return call(
        inside_kernel,
        (shape(rows, D), shape(rows, D), shape(rows, D, dtype=BF)),
        [VMEM, VMEM],
        [],
        4 * HEADS * rows * rows * LANES,
        rows * D * 16,
    )(packed, cm)


def totals_column(totals, head, rows):
    at = head + (HEAD_DIM if head % 2 == 0 else 0)
    return jnp.broadcast_to(totals[:, at : at + 1], (rows, LANES))


def layer_kernel(
    layer,
    shifts,
    *refs,
):
    recv = refs[:shifts]
    (
        x_ref,
        num_ref,
        den_ref,
        sq_ref,
        cs_ref,
        wo_hbm,
        w1_hbm,
        w2_hbm,
        bf_ref,
        mb_ref,
        ng_ref,
        before_ref,
        mixed_ref,
        mixt_ref,
        inv_ref,
        n1_ref,
        r1_ref,
        midt_ref,
        hid_ref,
        slope_ref,
        n2_ref,
        r2_ref,
        s_ref,
        wo,
        w1,
        w2,
        sems,
    ) = refs[shifts:]
    parts = w1.shape[0]
    co = pltpu.make_async_copy(wo_hbm.at[layer], wo, sems.at[2 * parts])
    c1 = [
        pltpu.make_async_copy(w1_hbm.at[layer, :, pl.ds(D * j, D)], w1.at[j], sems.at[j])
        for j in range(parts)
    ]
    c2 = [
        pltpu.make_async_copy(
            w2_hbm.at[layer, pl.ds(D * j, D), :], w2.at[j], sems.at[parts + j]
        )
        for j in range(parts)
    ]
    co.start()
    for j in range(parts):
        c1[j].start()
        c2[j].start()
    rows = x_ref.shape[0]
    lo = left_half(rows)
    lo_state = left_half(LANES)
    cs = cs_ref[...]
    before = recv[0][...].astype(F32)
    for other in recv[1:]:
        before = before + other[...].astype(F32)
    before_ref[...] = low(before)
    totals = before[PAIRS * LANES :]
    for pair in range(PAIRS):
        here = slice(pair * LANES, (pair + 1) * LANES)
        sq = sq_ref[:, here].astype(F32)
        other = swap(sq)
        state = before[here]
        n0 = nn(
            low(jnp.where(lo, sq, other) * cs),
            low(jnp.where(lo_state, state, totals_column(totals, 2 * pair, LANES))),
        )
        n1 = nn(
            low(jnp.where(lo, other, sq) * cs),
            low(jnp.where(lo_state, totals_column(totals, 2 * pair + 1, LANES), state)),
        )
        num = num_ref[:, here] + jnp.where(lo, n0, n1)
        inv = 1.0 / (den_ref[:, here] + swap(jnp.where(lo, n1, n0)))
        mixed = num * inv
        inv_ref[:, here] = inv
        mixed_ref[:, here] = low(mixed)
        mixt_ref[here, :] = low(mixed.T)
    co.wait()
    x = x_ref[...].astype(F32)
    branch = nn(mixed_ref[...], wo[...]) + vector(mb_ref, layer, 0)
    middle, n1, r1 = norm_apply(x + branch, vector(ng_ref, layer, 0), vector(mb_ref, layer, 2))
    n1_ref[...] = n1
    r1_ref[...] = spread(r1, rows)
    midt_ref[...] = low(middle.T)
    mid = low(middle)
    bias = vector(bf_ref, layer)
    total = middle + vector(mb_ref, layer, 1)
    for j in range(parts):
        here = slice(D * j, D * (j + 1))
        c1[j].wait()
        pre = nn(mid, w1[j]) + bias[:, here]
        cdf = 0.5 * (1.0 + lax.erf(pre * (1.0 / math.sqrt(2.0))))
        hid = low(pre * cdf)
        hid_ref[:, here] = hid
        slope_ref[:, here] = low(
            cdf + pre * jnp.exp(-0.5 * pre * pre) * (1.0 / math.sqrt(2.0 * math.pi))
        )
        c2[j].wait()
        total = total + nn(hid, w2[j])
    s_next, n2, r2 = norm_apply(total, vector(ng_ref, layer, 1), vector(mb_ref, layer, 3))
    n2_ref[...] = n2
    r2_ref[...] = spread(r2, rows)
    s_ref[...] = s_next.astype(s_ref.dtype)


def layer_forward(layer, recv, x, num, den, sq, cs, wo, w1, w2, bf, mb, ng, out_type):
    rows = x.shape[0]
    parts = FF // D
    return call(
        functools.partial(layer_kernel, layer, len(recv)),
        (
            shape(STATE_ROWS, LANES, dtype=BF),
            shape(rows, D, dtype=BF),
            shape(D, rows, dtype=BF),
            shape(rows, D),
            shape(rows, D),
            shape(rows, LANES),
            shape(D, rows, dtype=BF),
            shape(rows, FF, dtype=BF),
            shape(rows, FF, dtype=BF),
            shape(rows, D),
            shape(rows, LANES),
            shape(rows, D, dtype=out_type),
        ),
        [VMEM] * (len(recv) + 5) + [ANY] * 3 + [VMEM] * 3,
        [
            pltpu.VMEM((D, D), BF),
            pltpu.VMEM((parts, D, D), BF),
            pltpu.VMEM((parts, D, D), BF),
            pltpu.SemaphoreType.DMA((2 * parts + 1,)),
        ],
        2 * rows * D * (D + 2 * FF),
        2 * D * (D + 2 * FF),
    )(*recv, x, num, den, sq, cs, wo, w1, w2, bf, mb, ng)


def back_kernel(
    layer,
    gs_ref,
    n2_ref,
    r2_ref,
    slope_ref,
    n1_ref,
    r1_ref,
    mixed_ref,
    inv_ref,
    sq_ref,
    cs_ref,
    wo_hbm,
    w1_hbm,
    w2_hbm,
    ng_ref,
    gb2t_ref,
    gpre_ref,
    gb1_ref,
    gz1_ref,
    u_ref,
    dd_ref,
    st_ref,
    sums_ref,
    wo,
    w1,
    w2,
    sems,
):
    parts = w1.shape[0]
    co = pltpu.make_async_copy(wo_hbm.at[layer], wo, sems.at[2 * parts])
    c1 = [
        pltpu.make_async_copy(w1_hbm.at[layer, :, pl.ds(D * j, D)], w1.at[j], sems.at[j])
        for j in range(parts)
    ]
    c2 = [
        pltpu.make_async_copy(
            w2_hbm.at[layer, pl.ds(D * j, D), :], w2.at[j], sems.at[parts + j]
        )
        for j in range(parts)
    ]
    for j in range(parts):
        c2[j].start()
        c1[j].start()
    co.start()
    rows = gs_ref.shape[0]
    lo = left_half(rows)
    lo_state = left_half(LANES)
    cs = cs_ref[...]
    lane = lax.broadcasted_iota(jnp.int32, (LANES, LANES), 1)
    sublane = lax.broadcasted_iota(jnp.int32, (LANES, LANES), 0)
    same = low(jnp.where((lane < HEAD_DIM) == (sublane < HEAD_DIM), 1.0, 0.0))
    gs = gs_ref[...].astype(F32)
    n2 = n2_ref[...]
    gz2 = norm_back(gs, n2, r2_ref[:, :1], vector(ng_ref, layer, 1))
    gb2 = low(gz2)
    gb2t_ref[...] = low(gz2.T)
    sums_ref[...] = jnp.zeros(sums_ref.shape, F32)
    sums_ref[5:6, :] = column_sum(gb2.astype(F32))
    sums_ref[7:8, :] = column_sum(gs)
    sums_ref[9:10, :] = column_sum(gs * n2)
    gmid = gz2
    for j in range(parts):
        here = slice(D * j, D * (j + 1))
        c2[j].wait()
        gpre = low(nt(gb2, w2[j]) * slope_ref[:, here].astype(F32))
        gpre_ref[:, here] = gpre
        sums_ref[j : j + 1, :] = column_sum(gpre.astype(F32))
        c1[j].wait()
        gmid = gmid + nt(gpre, w1[j])
    n1 = n1_ref[...]
    gz1 = norm_back(gmid, n1, r1_ref[:, :1], vector(ng_ref, layer, 0))
    gb1 = low(gz1)
    gz1_ref[...] = gz1
    gb1_ref[...] = gb1
    sums_ref[4:5, :] = column_sum(gb1.astype(F32))
    sums_ref[6:7, :] = column_sum(gmid)
    sums_ref[8:9, :] = column_sum(gmid * n1)
    co.wait()
    gmixed = low(nt(gb1, wo[...])).astype(F32)
    totals = jnp.zeros((LANES, LANES), F32)
    for pair in range(PAIRS):
        here = slice(pair * LANES, (pair + 1) * LANES)
        u = gmixed[:, here] * inv_ref[:, here]
        dd = -nn(low(u * mixed_ref[:, here].astype(F32)), same)
        u_ref[:, here] = low(u)
        dd_ref[:, here] = low(dd)
        ds = swap(dd)
        sq = sq_ref[:, here].astype(F32)
        other = swap(sq)
        s0 = tn(low(jnp.where(lo, sq, other) * cs), low(jnp.where(lo, u, ds)))
        s1 = tn(low(jnp.where(lo, other, sq) * cs), low(jnp.where(lo, ds, u)))
        st_ref[here, :] = low(jnp.where(lo_state, s0, s1))
        totals = jnp.where(lane == HEAD_DIM + 2 * pair, s0, totals)
        totals = jnp.where(lane == 2 * pair + 1, s1, totals)
    st_ref[PAIRS * LANES :, :] = low(totals)


def layer_back(layer, gs, n2, r2, slope, n1, r1, mixed, inv, sq, cs, wo, w1, w2, ng):
    rows = gs.shape[0]
    parts = FF // D
    return call(
        functools.partial(back_kernel, layer),
        (
            shape(D, rows, dtype=BF),
            shape(rows, FF, dtype=BF),
            shape(rows, D, dtype=BF),
            shape(rows, D),
            shape(rows, D, dtype=BF),
            shape(rows, D, dtype=BF),
            shape(STATE_ROWS, LANES, dtype=BF),
            shape(16, D),
        ),
        [VMEM] * 10 + [ANY] * 3 + [VMEM],
        [
            pltpu.VMEM((D, D), BF),
            pltpu.VMEM((parts, D, D), BF),
            pltpu.VMEM((parts, D, D), BF),
            pltpu.SemaphoreType.DMA((2 * parts + 1,)),
        ],
        2 * rows * D * (D + 2 * FF),
        2 * D * (D + 2 * FF),
    )(gs, n2, r2, slope, n1, r1, mixed, inv, sq, cs, wo, w1, w2, ng)


def mix_back_kernel(layer, shifts, *refs):
    recv = refs[:shifts]
    (
        spot_ref,
        packed_ref,
        u_ref,
        dd_ref,
        before_ref,
        cs_ref,
        cm_ref,
        gb1_ref,
        gz1_ref,
        w_hbm,
        gpk_ref,
        gcol_ref,
        gs_ref,
        sums_ref,
        wbuf,
        sems,
    ) = refs[shifts:]
    parts = wbuf.shape[0]
    copies = [
        pltpu.make_async_copy(w_hbm.at[layer, :, pl.ds(D * j, D)], wbuf.at[j], sems.at[j])
        for j in range(parts)
    ]
    for copy in copies:
        copy.start()
    rows = packed_ref.shape[0]
    lo = left_half(rows)
    lo_state = left_half(LANES)
    one_left = lax.broadcasted_iota(jnp.int32, (rows, LANES), 1) == 0
    one_right = lax.broadcasted_iota(jnp.int32, (rows, LANES), 1) == HEAD_DIM
    col_left = lax.broadcasted_iota(jnp.int32, (LANES, LANES), 1) == 0
    col_right = lax.broadcasted_iota(jnp.int32, (LANES, LANES), 1) == HEAD_DIM
    cs = cs_ref[...]
    cm = cm_ref[...]
    later = recv[0][...].astype(F32)
    for other in recv[1:]:
        later = later + other[...].astype(F32)
    before = before_ref[...].astype(F32)
    before_totals = before[PAIRS * LANES :]
    later_totals = later[PAIRS * LANES :]
    for pair in range(PAIRS):
        here = slice(pair * LANES, (pair + 1) * LANES)
        at = pair * 3 * LANES
        t0, t1, t2 = (
            packed_ref[:, at + i * LANES : at + (i + 1) * LANES].astype(F32) for i in range(3)
        )
        sp0, sp1, sp2 = softplus(t0), softplus(t1), softplus(t2)
        sw0 = swap(sp0)
        sw1 = swap(sp1)
        sw2 = swap(sp2)
        q0 = low(jnp.where(lo, sp0, 0.0))
        k0 = low(jnp.where(lo, sw0, 0.0))
        q1 = low(jnp.where(lo, 0.0, sp1))
        k1 = low(jnp.where(lo, 0.0, sw2))
        kf0 = low(jnp.where(lo, sw0, sp0) * cs)
        kf1 = low(jnp.where(lo, sp2, sw2) * cs)
        v0 = low(jnp.where(lo, t1, jnp.where(one_right, 1.0, 0.0)))
        v1 = low(jnp.where(lo, jnp.where(one_left, 1.0, 0.0), t2))
        u = u_ref[:, here]
        uf = u.astype(F32)
        ds = swap(dd_ref[:, here].astype(F32))
        u0 = low(jnp.where(lo, uf, ds))
        u1 = low(jnp.where(lo, ds, uf))
        p0 = low(nt(q0, k0) * cm)
        p1 = low(nt(q1, k1) * cm)
        d0 = low(nt(u0, v0) * cm)
        d1 = low(nt(u1, v1) * cm)
        state = before[here]
        after = later[here]
        after_low = low(after)
        s0 = low(
            jnp.where(
                lo_state,
                state,
                jnp.where(col_right, totals_column(before_totals, 2 * pair, LANES), 0.0),
            )
        )
        s1 = low(
            jnp.where(
                lo_state,
                jnp.where(col_left, totals_column(before_totals, 2 * pair + 1, LANES), 0.0),
                state,
            )
        )
        r0 = low(
            jnp.where(
                lo_state,
                after,
                jnp.where(col_right, totals_column(later_totals, 2 * pair, LANES), 0.0),
            )
        )
        r1 = low(
            jnp.where(
                lo_state,
                jnp.where(col_left, totals_column(later_totals, 2 * pair + 1, LANES), 0.0),
                after,
            )
        )
        eq0 = nt(u0, s0) * cs
        eq1 = nt(u1, s1) * cs
        ek0 = nt(v0, r0) * cs
        ek1 = nt(v1, r1) * cs
        eq0 = eq0 + swap(eq0)
        eq1 = eq1 + swap(eq1)
        ek0 = ek0 + swap(ek0)
        ek1 = ek1 + swap(ek1)
        dq = jnp.where(lo, eq0 + nn(d0, k0), eq1 + nn(d1, k1))
        dk = jnp.where(lo, ek0 + tn(d0, q0), ek1 + tn(d1, q1))
        dv = jnp.where(
            lo,
            tn(p0, u) + nn(kf0, after_low),
            tn(p1, u) + nn(kf1, after_low),
        )
        dks = swap(dk)
        gpk_ref[:, at : at + LANES] = low(jnp.where(lo, dq, dks) * sigmoid(t0))
        gpk_ref[:, at + LANES : at + 2 * LANES] = low(jnp.where(lo, dv, dq * sigmoid(t1)))
        gpk_ref[:, at + 2 * LANES : at + 3 * LANES] = low(
            jnp.where(lo, dks * sigmoid(t2), dv)
        )
    grad = gz1_ref[...]
    for j in range(parts):
        here = slice(D * j, D * (j + 1))
        copies[j].wait()
        gpk = gpk_ref[:, here]
        sums_ref[j : j + 1, :] = column_sum(gpk.astype(F32))
        grad = grad + nt(gpk, wbuf[j])
    gs_ref[...] = grad
    near = spot_ref[3]
    far = spot_ref[4]
    gpk = gpk_ref[...].astype(F32)
    gb1 = gb1_ref[...].astype(F32)
    for low_bit in range(2):
        slot = low_bit ^ near
        for source, start in ((gb1, 0), (gpk, D // 2)):
            width = source.shape[1] // 4
            first = source[:, low_bit * width : (low_bit + 1) * width]
            second = source[:, (low_bit + 2) * width : (low_bit + 3) * width]
            both = jnp.concatenate(
                [jnp.where(far == 0, first, second), jnp.where(far == 0, second, first)], axis=1
            )
            gcol_ref[slot, :, start : start + 2 * width] = low(both)


def mix_back(layer, recv, spot, packed, u, dd, before, cs, cm, gb1, gz1, w):
    rows = packed.shape[0]
    return call(
        functools.partial(mix_back_kernel, layer, len(recv)),
        (
            shape(rows, 3 * D, dtype=BF),
            shape(2, rows, 2 * D, dtype=BF),
            shape(rows, D),
            shape(3, D),
        ),
        [VMEM] * len(recv) + [SMEM] + [VMEM] * 8 + [ANY],
        [pltpu.VMEM((3, D, D), BF), pltpu.SemaphoreType.DMA((3,))],
        2 * rows * D * 3 * D + 12 * HEADS * rows * rows * LANES,
        2 * D * 3 * D,
    )(*recv, spot, packed, u, dd, before, cs, cm, gb1, gz1, w)


def ffn_block(spot, midt, gpre, gb2t, hid, put):
    near = spot[3]
    far = spot[4]
    grad_in = nn(midt[0], gpre[...])
    grad_out = nn(gb2t[...], hid[...])
    for n in range(4):
        slot = (n % 2) ^ near
        half = (n // 2) ^ far
        put(0, slot, half, grad_in[:, D * n : D * (n + 1)])
        put(1, slot, half, grad_out[(D // 4) * n : (D // 4) * (n + 1)])


def ffn_send_kernel(spot, midt, gpre, gb2t, hid, out):
    def put(kind, slot, half, value):
        if kind == 0:
            out[0, slot, pl.ds(half * 96, 96), :] = low(value)
        else:
            out[0, slot, pl.ds(192, 192), pl.ds(half * 384, 384)] = low(value)

    ffn_block(spot, midt, gpre, gb2t, hid, put)


def ffn_keep_kernel(spot, midt, gpre, gb2t, hid, got, send0, keep0, send1, keep1):
    across = pl.program_id(0)
    along = pl.program_id(1)
    near = spot[3]
    far = spot[4]
    grad_in = nn(midt[0], gpre[...])
    grad_out = nn(gb2t[...], hid[...])

    def fill_in(target):
        for n in range(4):
            slot = (n % 2) ^ near
            rows = pl.ds(((n // 2) ^ far) * 96, 96)
            target[0, slot, rows, :] = low(
                grad_in[:, D * n : D * (n + 1)] + got[0, slot, rows, :].astype(F32)
            )

    def fill_out(target):
        for n in range(4):
            slot = (n % 2) ^ near
            lanes = pl.ds(pl.multiple_of(((n // 2) ^ far) * 384, 384), 384)
            target[0, slot, :, lanes] = low(
                grad_out[192 * n : 192 * (n + 1)] + got[0, slot, pl.ds(192, 192), lanes].astype(F32)
            )

    @pl.when(across == 0)
    def _():
        fill_in(keep0)

    @pl.when(across == 1)
    def _():
        fill_in(send0)

    @pl.when(along == 0)
    def _():
        fill_out(keep1)

    @pl.when(along == 1)
    def _():
        fill_out(send1)


def mix_send_kernel(spot, xt, mixt, gcol, out):
    for slot in range(2):
        out[0, slot, :, : D // 2] = low(nn(mixt[0], gcol[slot, :, : D // 2]))
        out[0, slot, :, D // 2 :] = low(nn(xt[0], gcol[slot, :, D // 2 :]))


def mix_keep_kernel(spot, xt, mixt, gcol, got, send0, keep0, send1, keep1):
    across = pl.program_id(0)
    along = pl.program_id(1)
    half = send0.shape[2]
    full = [
        (
            nn(mixt[0], gcol[slot, :, : D // 2]) + got[0, slot, :, : D // 2].astype(F32),
            nn(xt[0], gcol[slot, :, D // 2 :]) + got[0, slot, :, D // 2 :].astype(F32),
        )
        for slot in range(2)
    ]

    def fill(target, rows):
        for slot in range(2):
            target[0, slot, :, : D // 2] = low(full[slot][0][rows])
            target[0, slot, :, D // 2 :] = low(full[slot][1][rows])

    first = slice(0, half)
    second = slice(half, 2 * half)

    @pl.when(across == 0)
    def _():
        fill(keep0, first)

    @pl.when(across == 1)
    def _():
        fill(send0, first)

    @pl.when(along == 0)
    def _():
        fill(keep1, second)

    @pl.when(along == 1)
    def _():
        fill(send1, second)


def owner(same_core):
    def index(across, along, spot):
        core = spot[0] if same_core else 1 - spot[0]
        return ((spot[1] ^ along) * 2 + (spot[2] ^ across)) * 2 + core

    return index


def grad_specs(block, index):
    def rows_of(_):
        return pl.BlockSpec((1, D // 8, _), lambda a, b, s: (index(a, b, s), 0, 0))

    def whole(*dims):
        return pl.BlockSpec(dims, lambda a, b, s: (0,) * len(dims))

    return rows_of, whole


def grad_call(kind, spot, operands, got):
    keep = got is not None
    index = owner(keep)
    rows_of, whole = grad_specs(None, index)
    tokens = operands[0].shape[1]
    if kind == "ffn":
        midt, gpre, gb2t, hid = operands
        operands = (midt.reshape(8, D // 8, tokens), gpre, gb2t, hid)
        in_specs = [
            rows_of(tokens),
            whole(tokens, FF),
            whole(D, tokens),
            pl.BlockSpec((tokens, FF // 8), lambda a, b, s: (0, index(a, b, s))),
        ]
        rows, columns = 384, D
        kernel = ffn_keep_kernel if keep else ffn_send_kernel
        flops = 2 * tokens * D * FF
    else:
        xt, mixt, gcol = operands
        operands = (xt.reshape(8, D // 8, tokens), mixt.reshape(8, D // 8, tokens), gcol)
        in_specs = [rows_of(tokens), rows_of(tokens), whole(2, tokens, 2 * D)]
        rows, columns = 96, 2 * D
        kernel = mix_keep_kernel if keep else mix_send_kernel
        flops = 2 * tokens * D * 2 * D
    block = pl.BlockSpec((1, 2, rows, columns), lambda a, b, s: (2 * a + b, 0, 0, 0))
    if keep:
        in_specs.append(block)
        operands = operands + (got,)

        def half(at):
            return pl.BlockSpec(
                (1, 2, rows // 2, columns), lambda a, b, s: (at(a, b), 0, 0, 0)
            )

        out_specs = (
            half(lambda a, b: a * b),
            half(lambda a, b: jnp.where(a == 0, b, 1)),
            half(lambda a, b: a),
            half(lambda a, b: a),
        )
        outs = (shape(2, 2, rows // 2, columns, dtype=BF),) * 4
    else:
        out_specs = block
        outs = shape(4, 2, rows, columns, dtype=BF)
    return pl.pallas_call(
        kernel,
        out_shape=outs,
        grid_spec=pltpu.PrefetchScalarGridSpec(
            num_scalar_prefetch=1, grid=(2, 2), in_specs=in_specs, out_specs=out_specs
        ),
        compiler_params=pltpu.CompilerParams(vmem_limit_bytes=48 * 1024 * 1024),
        cost_estimate=pl.CostEstimate(
            flops=int(flops), bytes_accessed=int(4 * 2 * rows * columns * 2 * 2), transcendentals=0
        ),
    )(spot, *operands)


def wide_swap(v, bit):
    size = lax.axis_size("wide")
    return lax.ppermute(v, "wide", [(i, i ^ bit) for i in range(size)])


def narrow_swap(v, bit):
    size = lax.axis_size("narrow")
    return lax.ppermute(v, "narrow", [(i, i ^ bit) for i in range(size)])


def wide_add(v):
    return v.astype(F32)


def reduce_group(kind, spot, operands):
    sent = grad_call(kind, spot, operands, None)
    got = wide_swap(sent, 1)
    send0, keep0, send1, keep1 = grad_call(kind, spot, operands, got)
    got0 = wide_swap(send0, 2)
    got1 = wide_swap(send1, 4)
    next0 = wide_swap(low(wide_add(keep0[1]) + wide_add(got0[1])), 4)
    next1 = wide_swap(low(wide_add(keep1[1]) + wide_add(got1[1])), 2)
    sum0 = wide_add(keep0[0]) + wide_add(got0[0]) + wide_add(next0)
    sum1 = wide_add(keep1[0]) + wide_add(got1[0]) + wide_add(next1)
    full = jnp.concatenate([sum0, sum1], axis=1)
    near = narrow_swap(low(full[1]), 1)
    total = full[0] + wide_add(near)
    if kind == "ffn":
        mine = (total[:96], total[192:, :384])
        other = jnp.concatenate([total[96:192, :384], total[96:192, 384:], total[192:, 384:]], axis=0)
        far = wide_add(narrow_swap(low(other), 2))
        grad_in = mine[0] + jnp.concatenate([far[:96], far[96:192]], axis=1)
        grad_out = (mine[1] + far[192:]).T
        return grad_in, grad_out
    quarter = D // 4
    mine = jnp.concatenate([total[:, :quarter], total[:, 2 * quarter : 5 * quarter]], axis=1)
    other = jnp.concatenate([total[:, quarter : 2 * quarter], total[:, 5 * quarter :]], axis=1)
    both = mine + wide_add(narrow_swap(low(other), 2))
    return both[:, quarter:], both[:, :quarter]


def reduce_plain(left, right):
    term = low(tn(left, right))
    part = lax.psum_scatter(term, "narrow", scatter_dimension=1, tiled=True)
    return lax.psum_scatter(part.astype(F32), "wide", scatter_dimension=0, tiled=True)


def travel(state, step):
    size = lax.axis_size("narrow")
    got = []
    for shift in range(1, size):
        pairs = [(i, i + step * shift) for i in range(size) if 0 <= i + step * shift < size]
        got.append(lax.ppermute(state, "narrow", pairs))
    return got


def shards(
    tokens,
    cotangent,
    horizons,
    qkv_weight,
    out_weight,
    ffn_in_weight,
    ffn_out_weight,
    qkv_bias,
    ffn_in_bias,
    model_biases,
    norm_gains,
):
    rows = tokens.shape[0]
    wide = lax.axis_size("wide")
    narrow = lax.axis_size("narrow")
    wide_at = lax.axis_index("wide")
    narrow_at = lax.axis_index("narrow")
    spot = jnp.stack(
        [wide_at % 2, (wide_at // 4) % 2, (wide_at // 2) % 2, narrow_at % 2, (narrow_at // 2) % 2]
    ).astype(jnp.int32)
    step = 0.5 * math.pi / horizons[0].astype(F32)
    places = (narrow_at * rows + jnp.arange(rows)).astype(F32) * step
    cs = jnp.concatenate(
        [
            jnp.broadcast_to(jnp.cos(places)[:, None], (rows, HEAD_DIM)),
            jnp.broadcast_to(jnp.sin(places)[:, None], (rows, HEAD_DIM)),
        ],
        axis=1,
    )
    apart = jnp.arange(rows)[:, None] - jnp.arange(rows)[None, :]
    cm = jnp.where(apart >= 0, jnp.cos(apart.astype(F32) * step), 0.0)

    x = tokens
    saved = []
    for layer in range(LAYERS):
        packed, xt, state = project(layer, x, qkv_weight, qkv_bias, cs)
        recv = travel(state, 1)
        num, den, sq = inside(packed, cm)
        out_type = BF if layer == LAYERS - 1 else F32
        before, mixed, mixt, inv, n1, r1, midt, hid, slope, n2, r2, x_next = layer_forward(
            layer,
            recv,
            x,
            num,
            den,
            sq,
            cs,
            out_weight,
            ffn_in_weight,
            ffn_out_weight,
            ffn_in_bias,
            model_biases,
            norm_gains,
            out_type,
        )
        saved.append((packed, xt, sq, before, mixed, mixt, inv, n1, r1, midt, hid, slope, n2, r2))
        x = x_next
    output = x
    gs = cotangent
    layer_grads = [None] * LAYERS
    layer_sums = [None] * LAYERS
    for layer in reversed(range(LAYERS)):
        packed, xt, sq, before, mixed, mixt, inv, n1, r1, midt, hid, slope, n2, r2 = saved[layer]
        gb2t, gpre, gb1, gz1, u, dd, state, sums = layer_back(
            layer,
            gs,
            n2,
            r2,
            slope,
            n1,
            r1,
            mixed,
            inv,
            sq,
            cs,
            out_weight,
            ffn_in_weight,
            ffn_out_weight,
            norm_gains,
        )
        recv = travel(state, -1)
        if wide == 8 and narrow == 4:
            grad_in, grad_out = reduce_group("ffn", spot, (midt, gpre, gb2t, hid))
        else:
            grad_in = reduce_plain(midt.T, gpre)
            grad_out = reduce_plain(hid, gb2t.T)
        gpk, gcol, gs, gpk_sums = mix_back(
            layer, recv, spot, packed, u, dd, before, cs, cm, gb1, gz1, qkv_weight
        )
        if wide == 8 and narrow == 4:
            grad_qkv, grad_o = reduce_group("mix", spot, (xt, mixt, gcol))
        else:
            grad_qkv = reduce_plain(xt.T, gpk)
            grad_o = reduce_plain(mixt.T, gb1)
        layer_grads[layer] = (grad_qkv, grad_o, grad_in, grad_out)
        layer_sums[layer] = jnp.concatenate([sums[:10], gpk_sums], axis=0)
    sums = jnp.stack(layer_sums)
    if wide == 8 and narrow == 4:
        for bit in (1, 2, 4):
            sums = sums + wide_swap(sums, bit)
        for bit in (1, 2):
            sums = sums + narrow_swap(sums, bit)
    else:
        sums = lax.psum(sums, ("wide", "narrow"))

    def columns(v):
        width = v.shape[-1] // narrow
        return lax.dynamic_slice_in_dim(v, narrow_at * width, width, axis=v.ndim - 1)

    grads = [jnp.stack([layer_grads[l][k] for l in range(LAYERS)]) for k in range(4)]
    return (
        output,
        gs,
        grads[0],
        grads[1],
        grads[2],
        grads[3],
        columns(sums[:, 10:13].reshape(LAYERS, 3 * D)),
        columns(sums[:, 0:4].reshape(LAYERS, FF)),
        columns(sums[:, 4:8]),
        columns(sums[:, 8:10]),
    )


def solution(mesh):
    rows = P(("wide", "narrow"), None)
    placed = (rows, rows, P("wide")) + (P(),) * 8
    return jax.shard_map(
        shards,
        mesh=mesh,
        in_specs=placed,
        out_specs=(rows, rows)
        + (P(None, "wide", "narrow"),) * 4
        + (P(None, "narrow"),) * 2
        + (P(None, None, "narrow"),) * 2,
        check_vma=False,
    )
```

```python
import math

import jax
import jax.numpy as jnp
from jax import lax
from jax.experimental import pallas as pl
from jax.experimental.pallas import tpu as pltpu
from jax.sharding import PartitionSpec as P

D = 768
HEADS = 12
HEAD_DIM = 64
FF = 3072
LAYERS = 2
PAIRS = HEADS // 2
NORM_EPS = 1e-05
LANES = 128
STATE_ROWS = PAIRS * LANES + 16

BF = jnp.bfloat16
F32 = jnp.float32


def nn(a, b):
    return lax.dot_general(a, b, (((1,), (0,)), ((), ())), preferred_element_type=F32)


def nt(a, b):
    return lax.dot_general(a, b, (((1,), (1,)), ((), ())), preferred_element_type=F32)


def tn(a, b):
    return lax.dot_general(a, b, (((0,), (0,)), ((), ())), preferred_element_type=F32)


def low(v):
    return v.astype(BF)


def up(v):
    return v.astype(F32)


def beside(a, b):
    return jnp.concatenate([a, b], axis=1)


def above(a, b):
    return jnp.concatenate([a, b], axis=0)


def softplus(u):
    return jnp.maximum(u, 0.0) + jnp.log1p(jnp.exp(-jnp.abs(u)))


def sigmoid(u):
    return 1.0 / (1.0 + jnp.exp(-u))


def swap(v):
    return pltpu.roll(v, HEAD_DIM, 1)


def lane_of(rows):
    return lax.broadcasted_iota(jnp.int32, (rows, LANES), 1)


def row_mean(v):
    return jnp.mean(v, axis=-1, keepdims=True)


def norm_apply(total, gain, shift):
    centred = total - row_mean(total)
    scale = lax.rsqrt(row_mean(centred * centred) + NORM_EPS)
    normal = centred * scale
    return normal * gain + shift, normal, scale


def norm_back(upstream, normal, scale, gain):
    grad = upstream * gain
    return scale * (grad - row_mean(grad) - normal * row_mean(grad * normal))


def column_sum(v):
    return jnp.sum(v, axis=0, keepdims=True)


def shape(*dims, dtype=F32):
    return jax.ShapeDtypeStruct(dims, dtype)


class Box(dict):
    __getattr__ = dict.__getitem__
    __setattr__ = dict.__setitem__


class Refs:
    def __init__(self):
        self.refs = Box()
        self.copies = Box()
        self.flushes = Box()

    def __getitem__(self, name):
        for copy in self.copies.pop(name, []):
            if copy is not None:
                copy.wait()
        return self.refs[name]

    def __getattr__(self, name):
        return self[name]

    def part(self, name, at):
        copies = self.copies.get(name)
        if copies and copies[at] is not None:
            copies[at].wait()
            copies[at] = None
        return self.refs[name].at[at]

    def done(self, name):
        if name in self.flushes:
            self.flushes[name].start()


def in_hbm(array):
    return pltpu.with_memory_space_constraint(array, pltpu.HBM)


def in_vmem(array):
    return pltpu.with_memory_space_constraint(array, pltpu.VMEM)


def whole_cut(ref):
    return ref


def run(body, ins, outs, deps=(), scratch=None, limit=20, flops=0, nbytes=0):
    scratch = scratch or Box()
    in_names = list(ins)
    out_names = list(outs)
    operands, in_specs, out_shapes, out_specs, scratch_shapes = [], [], [], [], []
    vmem = pl.BlockSpec(memory_space=pltpu.VMEM)
    hbm = pl.BlockSpec(memory_space=pltpu.HBM)
    smem = pl.BlockSpec(memory_space=pltpu.SMEM)
    for name in in_names:
        mode, array = ins[name][:2]
        operands.append(Box(d=in_hbm, v=in_vmem).get(mode, whole_cut)(array))
        in_specs.append(Box(v=vmem, s=smem, d=hbm)[mode])
    fetch_names = [name for name in out_names if outs[name][0] == "f"]
    for name in fetch_names:
        operands.append(in_hbm(outs[name][1]))
        in_specs.append(hbm)
    for dep in deps:
        operands.append(in_vmem(dep))
        in_specs.append(vmem)
    copy_count = 0
    plan = []
    for name in in_names:
        if ins[name][0] == "d":
            array = ins[name][1]
            cuts, block = ins[name][2] if len(ins[name]) > 2 else (None, array.shape)
            scratch_shapes.append(
                pltpu.VMEM(block if cuts is None else (len(cuts),) + block, array.dtype)
            )
            plan.append((name, cuts))
            copy_count += 1 if cuts is None else len(cuts)
    for name in out_names:
        mode = outs[name][0]
        if mode == "f":
            array, cuts, block = outs[name][1:]
            out_shapes.append(pltpu.VMEM((len(cuts),) + block, array.dtype))
            copy_count += len(cuts)
        else:
            given = outs[name][1]
            space = pltpu.HBM if mode == "h" else pltpu.VMEM
            out_shapes.append(space(given.shape, given.dtype))
            if mode == "h":
                scratch_shapes.append(pltpu.VMEM(outs[name][1].shape, outs[name][1].dtype))
                copy_count += 1
        out_specs.append(hbm if mode == "h" else vmem)
    out_shapes.append(pltpu.VMEM((8, LANES), F32))
    out_specs.append(vmem)
    for spec in scratch.values():
        scratch_shapes.append(spec)
    scratch_shapes.append(pltpu.SemaphoreType.DMA((max(copy_count, 1),)))

    def kernel(*refs):
        refs = list(refs)
        sems = refs.pop()
        used = [0]

        def make(source, target):
            copy = pltpu.make_async_copy(source, target, sems.at[used[0]])
            used[0] += 1
            return copy

        n_in, n_fetch, n_out = len(in_names), len(fetch_names), len(out_names)
        in_refs = dict(zip(in_names, refs[:n_in]))
        fetch_refs = dict(zip(fetch_names, refs[n_in : n_in + n_fetch]))
        rest = refs[n_in + n_fetch + len(deps) :]
        out_refs = dict(zip(out_names, rest[:n_out]))
        token = rest[n_out]
        spare = rest[n_out + 1 :]
        io = Refs()
        for name in in_names:
            io.refs[name] = in_refs[name]
        for name, cuts in plan:
            buffer = spare.pop(0)
            io.refs[name] = buffer
            if cuts is None:
                io.copies[name] = [make(in_refs[name], buffer)]
            else:
                io.copies[name] = [
                    make(cut(in_refs[name]), buffer.at[at]) for at, cut in enumerate(cuts)
                ]
            for copy in io.copies[name]:
                copy.start()
        fetches = []
        for name in out_names:
            mode = outs[name][0]
            if mode == "f":
                for at, cut in enumerate(outs[name][2]):
                    fetches.append(make(cut(fetch_refs[name]), out_refs[name].at[at]))
                io.refs[name] = out_refs[name]
            elif mode == "h":
                buffer = spare.pop(0)
                io.refs[name] = buffer
                io.flushes[name] = make(buffer, out_refs[name])
            else:
                io.refs[name] = out_refs[name]
        for name in scratch:
            io.refs[name] = spare.pop(0)
        for copy in fetches:
            copy.start()
        token[...] = jnp.zeros(token.shape, F32)
        body(io)
        for name in list(io.copies):
            io[name]
        for copy in fetches:
            copy.wait()
        for copy in io.flushes.values():
            copy.wait()

    cost = COSTS[min(Counter.at, len(COSTS) - 1)]
    Counter.at += 1
    results = pl.pallas_call(
        kernel,
        out_shape=tuple(out_shapes),
        in_specs=in_specs,
        out_specs=tuple(out_specs),
        scratch_shapes=scratch_shapes,
        compiler_params=pltpu.CompilerParams(vmem_limit_bytes=limit * 1024 * 1024),
        cost_estimate=pl.CostEstimate(
            flops=int(cost * 10**9), bytes_accessed=10**8, transcendentals=0
        ),
    )(*operands)
    return Box(zip(out_names, results)), results[-1]


def columns_of(layer, parts):
    return [lambda ref, j=j: ref.at[layer, :, pl.ds(D * j, D)] for j in range(parts)], (D, D)


def rows_of(layer, parts):
    return [lambda ref, j=j: ref.at[layer, pl.ds(D * j, D), :] for j in range(parts)], (D, D)


def layer_of(layer, block):
    return [lambda ref: ref.at[layer]], block


COSTS = [120, 10, 15, 60, 0.3, 30, 30, 120, 0.3, 0.3, 1, 30, 120, 3, 10, 6, 15, 6, 1, 6, 3, 0.3, 22, 30, 22, 22, 3, 6, 22, 10, 120, 3, 10, 0.3, 3, 10, 120, 3, 10, 60, 0.3, 30, 0.3]


class Counter:
    at = 0


def project(layer, x, x_mode, wq, vecs, cs, long, deps):
    rows = x.shape[0]

    def body(io):
        x_in = up(io.x[...])
        xb = low(x_in)
        io.xt[...] = low(x_in.T)
        io.done("xt")
        lane = lane_of(rows)
        lo = lane < HEAD_DIM
        lane_state = lane_of(LANES)
        lo_state = lane_state < HEAD_DIM
        totals = jnp.zeros((LANES, LANES), F32)
        for j in range(3):
            w = io.part("wq", j)
            bias = vector(io, "qkv_bias", layer)[:, D * j : D * (j + 1)]
            pk = low(nn(xb, w[...]) + bias)
            io.packed[:, D * j : D * (j + 1)] = pk
            if long:
                io.kept[:, D * j : D * (j + 1)] = pk
            pf = up(pk)
            cs_now = io.cs[...]
            for p in range(2):
                t0, t1, t2 = (
                    pf[:, (3 * p + i) * LANES : (3 * p + i + 1) * LANES] for i in range(3)
                )
                sp0 = softplus(t0)
                sp2 = softplus(t2)
                kf0 = low(jnp.where(lo, swap(sp0), sp0) * cs_now)
                kf1 = low(jnp.where(lo, sp2, swap(sp2)) * cs_now)
                s0 = tn(kf0, low(jnp.where(lo, t1, 1.0)))
                s1 = tn(kf1, low(jnp.where(lo, 1.0, t2)))
                pair = 2 * j + p
                io.state[pair * LANES : (pair + 1) * LANES, :] = low(
                    jnp.where(lo_state, s0, s1)
                )
                totals = jnp.where(lane_state == 2 * pair, swap(s0), totals)
                totals = jnp.where(lane_state == 2 * pair + 1, s1, totals)
        io.state[PAIRS * LANES :, :] = low(totals.T[:16])
        if long:
            io.done("kept")

    outs = Box(
        packed=("v", shape(rows, 3 * D, dtype=BF)),
        xt=("h", shape(D, rows, dtype=BF)),
        state=("v", shape(STATE_ROWS, LANES, dtype=BF)),
    )
    if long:
        outs.kept = ("h", shape(rows, 3 * D, dtype=BF))
    return run(
        body,
        Box(x=(x_mode, x), wq=wq, cs=("d", cs), **vecs),
        outs,
        deps,
        flops=2 * rows * D * 3 * D,
        nbytes=2 * D * 3 * D,
    )


def inside(packed, cm, long, fetches, deps):
    rows = packed.shape[0]

    def body(io):
        lo = lane_of(rows) < HEAD_DIM
        for pair in range(PAIRS):
            at = pair * 3 * LANES
            t0, t1, t2 = (
                up(io.packed[:, at + i * LANES : at + (i + 1) * LANES]) for i in range(3)
            )
            sp0, sp1, sp2 = softplus(t0), softplus(t1), softplus(t2)
            a0 = nt(low(jnp.where(lo, sp0, 0.0)), low(swap(sp0)))
            a1 = nt(low(jnp.where(lo, 0.0, sp1)), low(swap(sp2)))
            mask = io.cm[...]
            n0 = nn(low(a0 * mask), low(jnp.where(lo, t1, 1.0)))
            n1 = nn(low(a1 * mask), low(jnp.where(lo, 1.0, t2)))
            here = slice(pair * LANES, (pair + 1) * LANES)
            io.num[:, here] = jnp.where(lo, n0, n1)
            io.den[:, here] = swap(jnp.where(lo, n1, n0))
            sq = low(jnp.where(lo, sp0, sp1))
            io.sq[:, here] = sq
            if long:
                io.sq_kept[:, here] = sq

    outs = Box(
        num=("v", shape(rows, D)),
        den=("v", shape(rows, D)),
        sq=("v", shape(rows, D, dtype=BF)),
    )
    if long:
        outs.sq_kept = ("h", shape(rows, D, dtype=BF))

    def body_all(io):
        body(io)
        if long:
            io.done("sq_kept")

    outs.update(fetches)
    return run(
        body_all,
        Box(packed=("v", packed), cm=("d", cm)),
        outs,
        deps,
        flops=4 * HEADS * rows * rows * LANES,
        nbytes=rows * D * 16,
    )


def sum_states(io, count):
    total = up(io.recv0[...])
    for at in range(1, count):
        total = total + up(io["recv%d" % at][...])
    return total


def vector(io, name, layer):
    return up(io[name][...])[layer : layer + 1]


def state_totals(total):
    return jnp.concatenate(
        [total[PAIRS * LANES :], jnp.zeros((LANES - 16, LANES), F32)], axis=0
    ).T


def totals_column(totals, head):
    return jnp.broadcast_to(totals[:, head : head + 1], (LANES, LANES))


def diagonal(a, b):
    zero = jnp.zeros((LANES, LANES), BF)
    return above(beside(a, zero), beside(zero, b))


def second_norm_back(io, gs, n2, r2, gain):
    gz2 = norm_back(gs, n2, r2, gain)
    gb2 = low(gz2)
    io.gz2[...] = gz2
    io.gb2[...] = gb2
    io.gb2t[...] = low(gz2.T)
    io.sums_a[...] = jnp.zeros((8, D), F32)
    io.sums_a[0:1, :] = column_sum(up(gb2))
    io.sums_a[1:2, :] = column_sum(gs)
    io.sums_a[2:3, :] = column_sum(gs * n2)
    io.done("sums_a")


def second_norm_outs(rows):
    return Box(
        gz2=("v", shape(rows, D)),
        gb2=("v", shape(rows, D, dtype=BF)),
        gb2t=("v", shape(D, rows, dtype=BF)),
        sums_a=("h", shape(8, D)),
    )


def layer_forward(layer, recv, x, x_mode, inner, weights, vecs, cs, cotangent, deps):
    rows = x.shape[0]
    last = cotangent is not None

    def body(io):
        lane = lane_of(rows)
        lo = lane < HEAD_DIM
        lo_state = lane_of(LANES) < HEAD_DIM
        before = sum_states(io, len(recv))
        io.before[...] = low(before)
        io.done("before")
        totals = state_totals(before)
        for pair in range(PAIRS):
            here = slice(pair * LANES, (pair + 1) * LANES)
            sq = up(io.sq[:, here])
            other = swap(sq)
            state = before[here]
            cs_now = io.cs[...]
            feats = beside(
                low(jnp.where(lo, sq, other) * cs_now), low(jnp.where(lo, other, sq) * cs_now)
            )
            both = nn(
                feats,
                diagonal(
                    low(jnp.where(lo_state, state, totals_column(totals, 2 * pair))),
                    low(jnp.where(lo_state, totals_column(totals, 2 * pair + 1), state)),
                ),
            )
            n0 = both[:, :LANES]
            n1 = both[:, LANES:]
            num = io.num[:, here] + jnp.where(lo, n0, n1)
            inv = 1.0 / (io.den[:, here] + swap(jnp.where(lo, n1, n0)))
            mixed = num * inv
            io.inv[:, here] = inv
            io.mixed[:, here] = low(mixed)
            io.mixt[here, :] = low(mixed.T)
        io.done("inv")
        io.done("mixed")
        io.done("mixt")
        shifts = up(io.shifts[layer])
        gains = up(io.gains[layer])
        bias = vector(io, "ffn_bias", layer)
        branch = nn(io.mixed[...], io.part("wo", 0)[...]) + shifts[0:1]
        middle, n1, r1 = norm_apply(up(io.x[...]) + branch, gains[0:1], shifts[2:3])
        io.n1[...] = n1
        io.done("n1")
        io.r1[...] = jnp.broadcast_to(r1, (rows, LANES))
        io.done("r1")
        io.midt[...] = low(middle.T)
        io.done("midt")
        mid = low(middle)
        total = middle + shifts[1:2]
        for j in range(FF // D):
            here = slice(D * j, D * (j + 1))
            pre = nn(mid, io.part("w1", j)[...]) + bias[:, here]
            cdf = 0.5 * (1.0 + lax.erf(pre * (1.0 / math.sqrt(2.0))))
            hid = low(pre * cdf)
            io.hid[:, here] = hid
            io.slope[:, here] = low(
                cdf + pre * jnp.exp(-0.5 * pre * pre) * (1.0 / math.sqrt(2.0 * math.pi))
            )
            total = total + nn(hid, io.part("w2", j)[...])
        io.done("hid")
        io.done("slope")
        s_next, n2, r2 = norm_apply(total, gains[1:2], shifts[3:4])
        if last:
            io.output[...] = low(s_next)
            io.done("output")
            second_norm_back(io, up(io.cot[...]), n2, r2, gains[1:2])
        else:
            io.s_next[...] = s_next
            io.n2[...] = n2
            io.done("n2")
            io.r2[...] = jnp.broadcast_to(r2, (rows, LANES))
            io.done("r2")

    ins = Box({"recv%d" % i: ("v", recv[i]) for i in range(len(recv))})
    ins.update(
        Box(
            x=(x_mode, x),
            num=("v", inner.num),
            den=("v", inner.den),
            sq=("v", inner.sq),
            wo=("v", weights.wo),
            w1=("v", weights.w1),
            w2=("v", weights.w2),
            cs=("d", cs),
            **vecs,
        )
    )
    if last:
        ins.cot = ("d", cotangent)
    mode = "v" if last else "h"
    outs = Box(
        before=("h", shape(STATE_ROWS, LANES, dtype=BF)),
        mixed=(mode, shape(rows, D, dtype=BF)),
        mixt=("h", shape(D, rows, dtype=BF)),
        inv=(mode, shape(rows, D)),
        n1=(mode, shape(rows, D)),
        r1=(mode, shape(rows, LANES)),
        midt=(mode, shape(D, rows, dtype=BF)),
        hid=(mode, shape(rows, FF, dtype=BF)),
        slope=(mode, shape(rows, FF, dtype=BF)),
    )
    if last:
        outs.output = ("h", shape(rows, D, dtype=BF))
        outs.update(second_norm_outs(rows))
    else:
        outs.s_next = ("v", shape(rows, D))
        outs.n2 = ("h", shape(rows, D))
        outs.r2 = ("h", shape(rows, LANES))
    return run(
        body,
        ins,
        outs,
        deps,
        limit=20,
        flops=2 * rows * D * (D + 2 * FF),
        nbytes=2 * D * (D + 2 * FF),
    )


def layer_back(layer, top, kept, mode, weights, vecs, cs, fetches, deps):
    rows = top.gz2.shape[0]

    def body(io):
        lane = lane_of(rows)
        lo = lane < HEAD_DIM
        lane_state = lane_of(LANES)
        lo_state = lane_state < HEAD_DIM
        left_rows = lax.broadcasted_iota(jnp.int32, (LANES, LANES), 0) < HEAD_DIM
        same = low(jnp.where(lo_state == left_rows, 1.0, 0.0))
        gb2 = io.gb2[...]
        gmid = io.gz2[...]
        sums = io.sums_b
        sums[...] = jnp.zeros((8, D), F32)
        for j in range(FF // D):
            here = slice(D * j, D * (j + 1))
            gpre = low(nt(gb2, io.part("w2", j)[...]) * up(io.slope[:, here]))
            io.gpre[:, here] = gpre
            sums[j : j + 1, :] = column_sum(up(gpre))
            gmid = gmid + nt(gpre, io.part("w1", j)[...])
        n1 = io.n1[...]
        gz1 = norm_back(gmid, n1, io.r1[:, :1], up(io.gains[layer])[0:1])
        gb1 = low(gz1)
        io.gz1[...] = gz1
        io.gb1[...] = gb1
        sums[4:5, :] = column_sum(up(gb1))
        sums[5:6, :] = column_sum(gmid)
        sums[6:7, :] = column_sum(gmid * n1)
        io.done("sums_b")
        gmixed = up(low(nt(gb1, io.part("wo", 0)[...])))
        totals = jnp.zeros((LANES, LANES), F32)
        for pair in range(PAIRS):
            here = slice(pair * LANES, (pair + 1) * LANES)
            u = gmixed[:, here] * io.inv[:, here]
            dd = -nn(low(u * up(io.mixed[:, here])), same)
            io.u[:, here] = low(u)
            io.dd[:, here] = low(dd)
            ds = swap(dd)
            sq = up(io.sq[:, here])
            other = swap(sq)
            cs_now = io.cs[...]
            s0 = tn(low(jnp.where(lo, sq, other) * cs_now), low(jnp.where(lo, u, ds)))
            s1 = tn(low(jnp.where(lo, other, sq) * cs_now), low(jnp.where(lo, ds, u)))
            io.state[here, :] = low(jnp.where(lo_state, s0, s1))
            totals = jnp.where(lane_state == 2 * pair, swap(s0), totals)
            totals = jnp.where(lane_state == 2 * pair + 1, s1, totals)
        io.state[PAIRS * LANES :, :] = low(totals.T[:16])

    ins = Box(
        gz2=("v", top.gz2),
        gb2=("v", top.gb2),
        wo=("v", weights.wo),
        w1=("v", weights.w1),
        w2=("v", weights.w2),
    )
    for name in ("slope", "n1", "r1", "inv", "mixed", "sq"):
        ins[name] = (mode, kept[name])
    ins.gains = vecs.gains
    ins.cs = ("d", cs)
    outs = Box(
        gpre=("v", shape(rows, FF, dtype=BF)),
        gb1=("v", shape(rows, D, dtype=BF)),
        gz1=("v", shape(rows, D)),
        u=("v", shape(rows, D, dtype=BF)),
        dd=("v", shape(rows, D, dtype=BF)),
        state=("v", shape(STATE_ROWS, LANES, dtype=BF)),
        sums_b=("h", shape(8, D)),
    )
    outs.update(fetches)
    return run(
        body,
        ins,
        outs,
        deps,
        limit=20,
        flops=2 * rows * D * (D + 2 * FF),
        nbytes=2 * D * (D + 2 * FF),
    )


def mix_back(layer, recv, spot, low_part, kept, cs, cm, wq, below, fetches, deps):
    rows = low_part.u.shape[0]

    def body(io):
        lane = lane_of(rows)
        lo = lane < HEAD_DIM
        lane_state = lane_of(LANES)
        lo_state = lane_state < HEAD_DIM
        one_left = jnp.where(lane == 0, 1.0, 0.0)
        one_right = jnp.where(lane == HEAD_DIM, 1.0, 0.0)
        later = sum_states(io, len(recv))
        later_totals = state_totals(later)
        before = up(io.before[...])
        before_totals = state_totals(before)

        def halves(state, totals, pair):
            first = jnp.where(
                lo_state,
                state,
                jnp.where(lane_state == HEAD_DIM, totals_column(totals, 2 * pair), 0.0),
            )
            second = jnp.where(
                lo_state,
                jnp.where(lane_state == 0, totals_column(totals, 2 * pair + 1), 0.0),
                state,
            )
            return diagonal(low(first), low(second))

        def fold(v, cs_now):
            first = v[:, :LANES] * cs_now
            second = v[:, LANES:] * cs_now
            return jnp.where(lo, first + swap(first), second + swap(second))

        for pair in range(PAIRS):
            here = slice(pair * LANES, (pair + 1) * LANES)
            at = pair * 3 * LANES
            t0, t1, t2 = (
                up(io.packed[:, at + i * LANES : at + (i + 1) * LANES]) for i in range(3)
            )
            cs_now = io.cs[...]
            mask = io.cm[...]
            sp0, sp1, sp2 = softplus(t0), softplus(t1), softplus(t2)
            sw0 = swap(sp0)
            sw2 = swap(sp2)
            q0 = low(jnp.where(lo, sp0, 0.0))
            k0 = low(jnp.where(lo, sw0, 0.0))
            q1 = low(jnp.where(lo, 0.0, sp1))
            k1 = low(jnp.where(lo, 0.0, sw2))
            kf = beside(
                low(jnp.where(lo, sw0, sp0) * cs_now), low(jnp.where(lo, sp2, sw2) * cs_now)
            )
            v0 = low(jnp.where(lo, t1, one_right))
            v1 = low(jnp.where(lo, one_left, t2))
            uf = up(io.u[:, here])
            ds = swap(up(io.dd[:, here]))
            u0 = low(jnp.where(lo, uf, ds))
            u1 = low(jnp.where(lo, ds, uf))
            ua = low(jnp.where(lo, uf, 0.0))
            ub = low(jnp.where(lo, 0.0, uf))
            p0 = low(nt(q0, k0) * mask)
            p1 = low(nt(q1, k1) * mask)
            d0 = low(nt(u0, v0) * mask)
            d1 = low(nt(u1, v1) * mask)
            after = later[here]
            eq = nt(beside(u0, u1), halves(before[here], before_totals, pair))
            ek = nt(beside(v0, v1), halves(after, later_totals, pair))
            after_split = above(
                low(jnp.where(lo_state, after, 0.0)), low(jnp.where(lo_state, 0.0, after))
            )
            dq = fold(eq, cs_now) + nn(d0, k0) + nn(d1, k1)
            dk = fold(ek, cs_now) + tn(d0, q0) + tn(d1, q1)
            dv = nn(kf, after_split) + tn(p0, ua) + tn(p1, ub)
            dks = swap(dk)
            gpk = io.gpk
            gpk[:, at : at + LANES] = low(jnp.where(lo, dq, dks) * sigmoid(t0))
            gpk[:, at + LANES : at + 2 * LANES] = low(jnp.where(lo, dv, dq * sigmoid(t1)))
            gpk[:, at + 2 * LANES : at + 3 * LANES] = low(jnp.where(lo, dks * sigmoid(t2), dv))
        grad = io.gz1[...]
        io.sums_c[...] = jnp.zeros((8, D), F32)
        for j in range(3):
            gpk = io.gpk[:, D * j : D * (j + 1)]
            io.sums_c[j : j + 1, :] = column_sum(up(gpk))
            grad = grad + nt(gpk, io.part("wq", j)[...])
        io.done("sums_c")
        if below is None:
            io.grad[...] = grad
            io.done("grad")
        else:
            gain = up(io.gains[layer - 1])[1:2]
            second_norm_back(io, grad, io.n2[...], io.r2[:, :1], gain)
        near = io.spot[3]
        far = io.spot[4]
        gpk = up(io.gpk[...])
        gb1 = up(io.gb1[...])
        for low_bit in range(2):
            slot = low_bit ^ near
            for source, start in ((gb1, 0), (gpk, D // 2)):
                width = source.shape[1] // 4
                first = source[:, low_bit * width : (low_bit + 1) * width]
                second = source[:, (low_bit + 2) * width : (low_bit + 3) * width]
                both = beside(
                    jnp.where(far == 0, first, second), jnp.where(far == 0, second, first)
                )
                io.gcol[slot, :, start : start + 2 * width] = low(both)

    ins = Box({"recv%d" % i: ("v", recv[i]) for i in range(len(recv))})
    ins.update(
        Box(
            spot=("s", spot),
            u=("v", low_part.u),
            dd=("v", low_part.dd),
            gb1=("v", low_part.gb1),
            gz1=("v", low_part.gz1),
            packed=("d", kept.packed),
            cs=("d", cs),
            cm=("d", cm),
            before=("d", kept.before),
            wq=wq,
        )
    )
    outs = Box(
        gcol=("v", shape(2, rows, 2 * D, dtype=BF)),
        sums_c=("h", shape(8, D)),
    )
    if below is None:
        outs.grad = ("h", shape(rows, D))
    else:
        ins.n2 = ("d", below.n2)
        ins.r2 = ("d", below.r2)
        ins.gains = below.vecs.gains
        outs.update(second_norm_outs(rows))
    outs.update(fetches)
    return run(
        body,
        ins,
        outs,
        deps,
        scratch=Box(gpk=pltpu.VMEM((rows, 3 * D), BF)),
        limit=20,
        flops=2 * rows * D * 3 * D + 12 * HEADS * rows * rows * LANES,
        nbytes=2 * D * 3 * D,
    )


def owners(spot, core):
    return [
        ((spot[1] ^ along) * 2 + (spot[2] ^ across)) * 2 + core
        for across in range(2)
        for along in range(2)
    ]


def out_terms(io, core, put):
    near, far = io.spot[3], io.spot[4]
    for at, block in enumerate(owners(io.spot, core)):
        lanes = pl.ds(pl.multiple_of(block * (FF // 8), LANES), FF // 8)
        io.rhs[:, at * (FF // 8) : (at + 1) * (FF // 8)] = io.hid[:, lanes]
    lhs = io.gb2t[...]
    for half in range(2):
        grad = nn(lhs, io.rhs[:, half * D : (half + 1) * D])
        for sub in range(2):
            at = 2 * half + sub
            for n in range(4):
                lanes = pl.ds(pl.multiple_of(((n // 2) ^ far) * (D // 2), LANES), D // 2)
                put(
                    at,
                    (n % 2) ^ near,
                    None,
                    lanes,
                    grad[n * 192 : (n + 1) * 192, sub * (D // 2) : (sub + 1) * (D // 2)],
                )


def gather_rows(io, name, target, core):
    for at, block in enumerate(owners(io.spot, core)):
        io[target][at * 96 : (at + 1) * 96, :] = io[name][
            pl.ds(pl.multiple_of(block * 96, 16), 96), :
        ]


def in_terms(io, core, put):
    near, far = io.spot[3], io.spot[4]
    gather_rows(io, "midt", "lhs", core)
    for n in range(4):
        grad = nn(io.lhs[...], io.gpre[:, n * D : (n + 1) * D])
        for at in range(4):
            put(at, (n % 2) ^ near, (n // 2) ^ far, slice(None), grad[at * 96 : (at + 1) * 96])


def mix_terms(io, core, put):
    gather_rows(io, "mixt", "lhs", core)
    gather_rows(io, "xt", "lhs_two", core)
    for slot in range(2):
        for lhs, start, stop in (("lhs", 0, D // 2), ("lhs_two", D // 2, 2 * D)):
            grad = nn(io[lhs][...], io.gcol[slot, :, start:stop])
            for at in range(4):
                put(
                    at,
                    slot,
                    None,
                    slice(start, stop),
                    grad[at * 96 : (at + 1) * 96],
                )


def part_rows(part, count):
    if part is None:
        return slice(None)
    return pl.ds(pl.multiple_of(part * count, 16), count)


TERMS = Box(out=out_terms, inner=in_terms, mix=mix_terms)


def grad_setup(kind, spot, operands):
    ins = Box(spot=("s", spot))
    if kind == "out":
        gb2t, hid = operands
        tokens = gb2t.shape[1]
        ins.gb2t = ("v", gb2t)
        ins.hid = ("v", hid)
        return ins, Box(rhs=pltpu.VMEM((tokens, FF // 2), BF)), (192, D), tokens
    lhs = pltpu.VMEM((D // 2, operands[0].shape[1]), BF)
    if kind == "inner":
        midt, gpre = operands
        ins.midt = ("v", midt)
        ins.gpre = ("v", gpre)
        return ins, Box(lhs=lhs), (192, D), midt.shape[1]
    mixt, xt, gcol = operands
    ins.mixt = ("d", mixt)
    ins.xt = ("d", xt)
    ins.gcol = ("v", gcol)
    return ins, Box(lhs=lhs, lhs_two=lhs), (96, 2 * D), xt.shape[1]


def grad_send(kind, spot, operands, deps):
    ins, scratch, block, tokens = grad_setup(kind, spot, operands)

    def body(io):
        def put(at, slot, part, lanes, value):
            io.send[at, slot, part_rows(part, value.shape[0]), lanes] = low(value)

        TERMS[kind](io, 1 - io.spot[0], put)

    outs, token = run(
        body,
        ins,
        Box(send=("v", shape(4, 2, *block, dtype=BF))),
        deps,
        scratch=scratch,
        flops=2 * tokens * 8 * block[0] * block[1],
        nbytes=4 * 2 * 2 * block[0] * block[1],
    )
    return outs.send, token


def grad_keep(kind, spot, operands, got, order, deps):
    ins, scratch, block, tokens = grad_setup(kind, spot, operands)
    ins.got = ("v", got)
    rows_all = block[0]
    if order == "both":
        half = (rows_all // 2, block[1])
    else:
        half = block

    def body(io):
        def put(at, slot, part, lanes, value):
            count = value.shape[0]
            rows = part_rows(part, count)
            value = low(value + up(io.got[at, slot, rows, lanes]))
            across, along = at // 2, at % 2
            if order == "x":
                io["send0" if across else "keep0"][along, slot, rows, lanes] = value
            elif order == "y":
                io["send0" if along else "keep0"][across, slot, rows, lanes] = value
            else:
                rows = part_rows(part, count // 2)
                first, second = value[: count // 2], value[count // 2 :]
                io["send0" if across else "keep0"][along, slot, rows, lanes] = first
                io["send1" if along else "keep1"][across, slot, rows, lanes] = second

        TERMS[kind](io, io.spot[0], put)

    names = ["send0", "keep0"] + (["send1", "keep1"] if order == "both" else [])
    return run(
        body,
        ins,
        {name: ("v", shape(2, 2, *half, dtype=BF)) for name in names},
        deps,
        scratch=scratch,
        flops=2 * tokens * 8 * block[0] * block[1],
        nbytes=4 * 2 * 4 * block[0] * block[1],
    )


def grad_pass(groups, deps):
    pairs = [
        (group["keep%d" % at], group["got%d" % at]) for group in groups for at in halves_of(group)
    ]
    ins, outs = Box(), Box()
    for at, (keep, got) in enumerate(pairs):
        ins["keep%d" % at] = ("v", keep)
        ins["got%d" % at] = ("v", got)
        outs["next%d" % at] = ("v", shape(*keep.shape[1:], dtype=BF))

    def body(io):
        for at in range(len(pairs)):
            io["next%d" % at][...] = low(
                up(io["keep%d" % at][1]) + up(io["got%d" % at][1])
            )

    outs, token = run(body, ins, outs, deps)
    return [outs["next%d" % at] for at in range(len(pairs))], token


def halves_of(group):
    return [at for at in range(2) if "keep%d" % at in group]


def group_ins(groups):
    ins = Box()
    for which, group in enumerate(groups):
        for at in halves_of(group):
            for name in ("keep", "got", "come"):
                ins["%s%d_%d" % (name, which, at)] = ("v", group["%s%d" % (name, at)])
    return ins


def group_sum(io, which, at, slot):
    return (
        up(io["keep%d_%d" % (which, at)][0, slot])
        + up(io["got%d_%d" % (which, at)][0, slot])
        + up(io["come%d_%d" % (which, at)][slot])
    )


def grad_near(groups, deps):
    ins = group_ins(groups)
    places = [(which, at) for which, group in enumerate(groups) for at in halves_of(group)]
    total = sum(group["keep%d" % at].shape[2] for group in groups for at in halves_of(group))
    lanes = groups[0].keep0.shape[3]

    def body(io):
        start = 0
        for which, at in places:
            rows = groups[which]["keep%d" % at].shape[2]
            here = slice(start, start + rows)
            io.near[here, :] = low(group_sum(io, which, at, 1))
            io.stay[here, :] = low(group_sum(io, which, at, 0))
            start += rows

    return run(
        body,
        ins,
        Box(
            near=("v", shape(total, lanes, dtype=BF)),
            stay=("v", shape(total, lanes, dtype=BF)),
        ),
        deps,
    )


def grad_collect(kinds, groups, deps):
    ins = group_ins(groups)
    ins.spot = ("s", groups[0].spot)

    def body(io):
        near, far = io.spot[3], io.spot[4]
        for which, kind in enumerate(kinds):
            for slot in range(2):
                full = [group_sum(io, which, at, slot) for at in halves_of(groups[which])]
                if kind == "mix":
                    both = above(full[0], full[1])
                    quarter = D // 4
                    parts = [
                        beside(both[:, :quarter], both[:, 2 * quarter : 5 * quarter]),
                        beside(both[:, quarter : 2 * quarter], both[:, 5 * quarter :]),
                    ]
                elif kind == "inner":
                    parts = [full[0][:96], full[0][96:]]
                else:
                    parts = [
                        beside(full[0][:96, : D // 2], full[0][96:, : D // 2]),
                        beside(full[0][:96, D // 2 :], full[0][96:, D // 2 :]),
                    ]
                for half in range(2):
                    owner = (slot ^ near) + 2 * (half ^ far)
                    io.blocks[owner, which * 96 : (which + 1) * 96, :] = low(parts[half])

    outs, token = run(
        body, ins, Box(blocks=("v", shape(4, 96 * len(kinds), D, dtype=BF))), deps
    )
    return outs.blocks, token


def grad_far(kinds, stay, near, deps):
    count = len(kinds)

    def body(io):
        full = up(io.stay[...]) + up(io.near[...])
        if kinds[0] == "mix":
            quarter = D // 4
            io.own[...] = beside(full[:, :quarter], full[:, 2 * quarter : 5 * quarter])
            io.far[...] = low(
                beside(full[:, quarter : 2 * quarter], full[:, 5 * quarter : 8 * quarter])
            )
            return
        for at, kind in enumerate(kinds):
            part = full[192 * at : 192 * (at + 1)]
            here = slice(96 * at, 96 * (at + 1))
            if kind == "out":
                io.own[here, :] = beside(part[:96, : D // 2], part[96:, : D // 2])
                io.far[here, :] = low(beside(part[:96, D // 2 :], part[96:, D // 2 :]))
            else:
                io.own[here, :] = part[:96]
                io.far[here, :] = low(part[96:])

    return run(
        body,
        Box(stay=("v", stay), near=("v", near)),
        Box(
            own=("v", shape(count * 96, D)),
            far=("v", shape(count * 96, D, dtype=BF)),
        ),
        deps,
    )


def grad_last(kind, terms, deps):
    ins = Box()
    for layer in range(LAYERS):
        for at, term in enumerate(terms[layer]):
            ins["term%d_%d" % (layer, at)] = ("v", term)
    if kind == "mix":
        outs = Box(
            first=("h", shape(LAYERS, 96, 3 * D // 4)),
            second=("h", shape(LAYERS, 96, D // 4)),
        )
    else:
        outs = Box(
            first=("h", shape(LAYERS, 96, D)),
            second=("h", shape(LAYERS, FF // 8, D // 4)),
        )

    def body(io):
        for layer in range(LAYERS):
            full = up(io["term%d_0" % layer][...])
            for at in range(1, len(terms[layer])):
                full = full + up(io["term%d_%d" % (layer, at)][...])
            if kind == "mix":
                io.first[layer] = full[:, D // 4 :]
                io.second[layer] = full[:, : D // 4]
            else:
                io.first[layer] = full[96:]
                io.second[layer, :, :96] = full[:96, : D // 2].T
                io.second[layer, :, 96:] = full[:96, D // 2 :].T
        io.done("first")
        io.done("second")

    return run(body, ins, outs, deps)


def wide_swap(v, bit):
    size = lax.axis_size("wide")
    return lax.ppermute(v, "wide", [(i, i ^ bit) for i in range(size)])


def narrow_swap(v, bit):
    size = lax.axis_size("narrow")
    return lax.ppermute(v, "narrow", [(i, i ^ bit) for i in range(size)])


CORE, ACROSS, ALONG = 1, 2, 4
NEAR, FAR = 1, 2


def reduce_plain(left, right):
    term = low(tn(left, right))
    part = lax.psum_scatter(term, "narrow", scatter_dimension=1, tiled=True)
    return lax.psum_scatter(up(part), "wide", scatter_dimension=0, tiled=True)


def move(v, shift):
    size = lax.axis_size("narrow")
    pairs = [(i, i + shift) for i in range(size) if 0 <= i + shift < size]
    return lax.ppermute(v, "narrow", pairs)


def travel(state, step):
    return [move(state, step * shift) for shift in range(1, lax.axis_size("narrow"))]


def add_up(a, b, deps):
    def body(io):
        io.sum[...] = (up(io.a[...]) + up(io.b[...])).astype(a.dtype)

    outs, token = run(
        body,
        Box(a=("v", a), b=("v", b)),
        Box(sum=("v", shape(*a.shape, dtype=a.dtype))),
        deps,
    )
    return outs.sum, token


def shards(
    tokens,
    cotangent,
    horizons,
    qkv_weight,
    out_weight,
    ffn_in_weight,
    ffn_out_weight,
    qkv_bias,
    ffn_in_bias,
    model_biases,
    norm_gains,
):
    Counter.at = 0
    rows = tokens.shape[0]
    wide = lax.axis_size("wide")
    narrow = lax.axis_size("narrow")
    wide_at = lax.axis_index("wide")
    narrow_at = lax.axis_index("narrow")
    fast = wide == 8 and narrow == 4
    place = [wide_at % 2, (wide_at // 4) % 2, (wide_at // 2) % 2, narrow_at % 2, narrow_at // 2]
    if not fast:
        place = [wide_at * 0] * 5
    place.append(narrow_at)
    spot = jnp.stack(place).astype(jnp.int32)
    step = 0.5 * math.pi / up(horizons[0])
    places = up(narrow_at * rows + jnp.arange(rows)) * step
    cs = beside(
        jnp.broadcast_to(jnp.cos(places)[:, None], (rows, HEAD_DIM)),
        jnp.broadcast_to(jnp.sin(places)[:, None], (rows, HEAD_DIM)),
    )

    def mask(step):
        apart = jnp.arange(rows)[:, None] - jnp.arange(rows)[None, :]
        return jnp.where(apart >= 0, jnp.cos(up(apart) * step), 0.0)

    vecs = Box(
        ffn_bias=("d", ffn_in_bias),
        shifts=("d", model_biases),
        gains=("d", norm_gains),
    )
    wq_cuts = [("d", qkv_weight, columns_of(layer, 3)) for layer in range(LAYERS)]

    def weight_fetch(layer):
        return Box(
            wo=("f", out_weight) + layer_of(layer, (D, D)),
            w1=("f", ffn_in_weight) + columns_of(layer, 4),
            w2=("f", ffn_out_weight) + rows_of(layer, 4),
        )

    x = tokens
    wq = wq_cuts[0]
    saved = []
    deps = ()
    for layer in range(LAYERS):
        last = layer == LAYERS - 1
        first, token = project(
            layer, x, "v" if layer else "d", wq, Box(qkv_bias=("d", qkv_bias)), cs, True, deps
        )
        if not layer:
            cm = mask(step + token[0, 0])
        recv = travel(first.state, 1)
        fetches = weight_fetch(layer)
        if not last:
            fetches.wq = ("f", qkv_weight) + columns_of(layer + 1, 3)
        inner, token = inside(first.packed, cm, not last, fetches, (token,))
        weights = inner
        kept, token = layer_forward(
            layer,
            recv,
            x,
            "v" if layer else "d",
            inner,
            weights,
            vecs,
            cs,
            cotangent if last else None,
            (token,),
        )
        kept.packed = first.kept
        kept.xt = first.xt
        kept.sq = inner.sq if last else inner.sq_kept
        kept.vecs = vecs
        saved.append(kept)
        deps = (token,)
        if not last:
            x = kept.s_next
            wq = ("v", inner.wq)

    output = saved[1].output
    one, zero = saved[1], saved[0]
    if not fast:
        grads = [None] * LAYERS
        sums = [None] * LAYERS
        top = one
        for layer in (1, 0):
            kept = saved[layer]
            fetch = Box() if layer == 1 else Box()
            back, token = layer_back(
                layer, top, kept, "v" if layer else "d", weights, vecs, cs, fetch, (token,)
            )
            recv = travel(back.state, -1)
            below = saved[0] if layer == 1 else None
            fetch = weight_fetch(0) if layer == 1 else Box()
            mix, token = mix_back(
                layer, recv, spot, back, kept, cs, cm, wq_cuts[layer], below, fetch, (token,)
            )
            gcol = mix.gcol
            gpk = jnp.concatenate(
                [gcol[n % 2, :, 384 + 576 * (n // 2) : 960 + 576 * (n // 2)] for n in range(4)],
                axis=1,
            )
            grads[layer] = (
                reduce_plain(kept.xt.T, gpk),
                reduce_plain(kept.mixt.T, back.gb1),
                reduce_plain(kept.midt.T, back.gpre),
                reduce_plain(kept.hid, top.gb2),
            )
            sums[layer] = jnp.concatenate(
                [top.sums_a[:3], back.sums_b[:7], mix.sums_c[:3]], axis=0
            )
            top = mix
            weights = mix
        sums = lax.psum(jnp.stack(sums), ("wide", "narrow"))
        grad_qkv, grad_o, grad_in, grad_out = (
            jnp.stack([grads[l][k] for l in range(LAYERS)]) for k in range(4)
        )
        input_grad = mix.grad
    else:
        group = Box()
        ops = Box()

        def send(name, kind, operands, token):
            ops[name] = (kind, operands)
            sent, token = grad_send(kind, spot, operands, (token,))
            ops[name] += (wide_swap(sent, CORE),)
            return token

        def keep(name, order, token):
            kind, operands, got = ops[name]
            found, token = grad_keep(kind, spot, operands, got, order, (token,))
            axes = Box(x=(ACROSS,), y=(ALONG,), both=(ACROSS, ALONG))[order]
            for at, axis in enumerate(axes):
                found["got%d" % at] = wide_swap(found["send%d" % at], axis)
            found.axes = axes
            group[name] = found
            return token

        def forward(names, token):
            sent, token = grad_pass([group[name] for name in names], (token,))
            for name in names:
                for at in halves_of(group[name]):
                    axis = ACROSS + ALONG - group[name].axes[at]
                    group[name]["come%d" % at] = wide_swap(sent.pop(0), axis)
            return token

        def near(names, token):
            found, token = grad_near([group[name] for name in names], (token,))
            return (found.stay, narrow_swap(found.near, NEAR)), token

        def far(kinds, pair, token):
            found, token = grad_far(kinds, *pair, (token,))
            return (found.own, narrow_swap(found.far, FAR)), token

        def gather(kinds, names, token):
            for name in names:
                group[name].spot = spot
            blocks, token = grad_collect(kinds, [group[name] for name in names], (token,))
            mine = lax.psum_scatter(blocks, "narrow", scatter_dimension=0, tiled=True)
            return (mine.reshape(mine.shape[1:]),), token

        token = send("o1", "out", (one.gb2t, one.hid), token)
        back1, token = layer_back(1, one, one, "v", weights, vecs, cs, Box(), (token,))
        later1 = [move(back1.state, -1)]
        token = send("i1", "inner", (one.midt, back1.gpre), token)
        token = keep("o1", "y", token)
        both, token = add_up(back1.state, later1[0], (token,))
        later1.append(move(both, -2))
        token = keep("i1", "x", token)
        mix1, token = mix_back(
            1, later1, spot, back1, one, cs, cm, wq_cuts[1], zero, weight_fetch(0), (token,)
        )
        token = send("m1", "mix", (one.mixt, one.xt, mix1.gcol), token)
        token = forward(["o1"], token)
        token = forward(["i1"], token)
        fetch = Box(
            hid=("f", zero.hid, [whole_cut], (rows, FF)),
            midt=("f", zero.midt, [whole_cut], (D, rows)),
        )
        weights = mix1
        back0, token = layer_back(0, mix1, zero, "d", weights, vecs, cs, fetch, (token,))
        later0 = [move(back0.state, -1)]
        token = keep("m1", "both", token)
        f1, token = gather(["out", "inner"], ["o1", "i1"], token)
        both, token = add_up(back0.state, later0[0], (token,))
        later0.append(move(both, -2))
        token = send("o0", "out", (mix1.gb2t, back0.hid.reshape(rows, FF)), token)
        token = send("i0", "inner", (back0.midt.reshape(D, rows), back0.gpre), token)
        token = forward(["m1"], token)
        token = keep("o0", "y", token)
        token = keep("i0", "x", token)
        mix0, token = mix_back(
            0, later0, spot, back0, zero, cs, cm, wq_cuts[0], None, Box(), (token,)
        )
        input_grad = mix0.grad
        sums = jnp.concatenate(
            [
                mix1.sums_a[:3],
                back0.sums_b[:7],
                mix0.sums_c[:3],
                one.sums_a[:3],
                back1.sums_b[:7],
                mix1.sums_c[:3],
                jnp.zeros((6, D), F32),
            ],
            axis=0,
        )
        token = send("m0", "mix", (zero.mixt, zero.xt, mix0.gcol), token)
        come = wide_swap(sums, CORE)
        sums, token = add_up(sums, come, (token,))
        come = wide_swap(sums, ACROSS)
        mg1, token = gather(["mix"], ["m1"], token)
        sums, token = add_up(sums, come, (token,))
        come = wide_swap(sums, ALONG)
        token = forward(["o0"], token)
        token = forward(["i0"], token)
        sums, token = add_up(sums, come, (token,))
        come = narrow_swap(sums, NEAR)
        token = keep("m0", "both", token)
        sums, token = add_up(sums, come, (token,))
        come = narrow_swap(sums, FAR)
        near_f0, token = near(["o0", "i0"], token)
        sums, token = add_up(sums, come, (token,))
        token = forward(["m0"], token)
        far_f0, token = far(["out", "inner"], near_f0, token)
        near_m0, token = near(["m0"], token)
        far_m0, token = far(["mix"], near_m0, token)
        ffn_grads, token = grad_last("ffn", [far_f0, f1], (token,))
        mix_grads, token = grad_last("mix", [far_m0, mg1], (token,))
        sums = sums[:26].reshape(LAYERS, 13, D)
        grad_qkv, grad_o = mix_grads.first, mix_grads.second
        grad_in, grad_out = ffn_grads.first, ffn_grads.second

    def columns(v):
        width = v.shape[-1] // narrow
        return lax.dynamic_slice_in_dim(v, narrow_at * width, width, axis=v.ndim - 1)

    return (
        output,
        input_grad,
        grad_qkv,
        grad_o,
        grad_in,
        grad_out,
        columns(sums[:, 10:13].reshape(LAYERS, 3 * D)),
        columns(sums[:, 3:7].reshape(LAYERS, FF)),
        columns(jnp.stack([sums[:, 7], sums[:, 0], sums[:, 8], sums[:, 1]], axis=1)),
        columns(jnp.stack([sums[:, 9], sums[:, 2]], axis=1)),
    )


def solution(mesh):
    rows = P(("wide", "narrow"), None)
    placed = (rows, rows, P("wide")) + (P(),) * 8
    return jax.shard_map(
        shards,
        mesh=mesh,
        in_specs=placed,
        out_specs=(rows, rows)
        + (P(None, "wide", "narrow"),) * 4
        + (P(None, "narrow"),) * 2
        + (P(None, None, "narrow"),) * 2,
        check_vma=False,
    )
```

```python
import math

import jax
import jax.numpy as jnp
from jax import lax
from jax.experimental import pallas as pl
from jax.experimental.pallas import tpu as pltpu
from jax.sharding import PartitionSpec as P

D = 768
HEADS = 12
HEAD_DIM = 64
FF = 3072
LAYERS = 2
PAIRS = HEADS // 2
NORM_EPS = 1e-05
LANES = 128
STATE_ROWS = PAIRS * LANES + 16

BF = jnp.bfloat16
F32 = jnp.float32


def nn(a, b):
    return lax.dot_general(a, b, (((1,), (0,)), ((), ())), preferred_element_type=F32)


def nt(a, b):
    return lax.dot_general(a, b, (((1,), (1,)), ((), ())), preferred_element_type=F32)


def tn(a, b):
    return lax.dot_general(a, b, (((0,), (0,)), ((), ())), preferred_element_type=F32)


def low(v):
    return v.astype(BF)


def up(v):
    return v.astype(F32)


def beside(a, b):
    return jnp.concatenate([a, b], axis=1)


def above(a, b):
    return jnp.concatenate([a, b], axis=0)


def softplus(u):
    return jnp.maximum(u, 0.0) + jnp.log1p(jnp.exp(-jnp.abs(u)))


def sigmoid(u):
    return 1.0 / (1.0 + jnp.exp(-u))


def swap(v):
    return pltpu.roll(v, HEAD_DIM, 1)


def lane_of(rows):
    return lax.broadcasted_iota(jnp.int32, (rows, LANES), 1)


def row_mean(v):
    return jnp.mean(v, axis=-1, keepdims=True)


def norm_apply(total, gain, shift):
    centred = total - row_mean(total)
    scale = lax.rsqrt(row_mean(centred * centred) + NORM_EPS)
    normal = centred * scale
    return normal * gain + shift, normal, scale


def norm_back(upstream, normal, scale, gain):
    grad = upstream * gain
    return scale * (grad - row_mean(grad) - normal * row_mean(grad * normal))


def column_sum(v):
    return jnp.sum(v, axis=0, keepdims=True)


def shape(*dims, dtype=F32):
    return jax.ShapeDtypeStruct(dims, dtype)


class Box(dict):
    __getattr__ = dict.__getitem__
    __setattr__ = dict.__setitem__


class Refs:
    def __init__(self):
        self.refs = Box()
        self.copies = Box()
        self.flushes = Box()

    def __getitem__(self, name):
        for copy in self.copies.pop(name, []):
            if copy is not None:
                copy.wait()
        return self.refs[name]

    def __getattr__(self, name):
        return self[name]

    def part(self, name, at):
        copies = self.copies.get(name)
        if copies and copies[at] is not None:
            copies[at].wait()
            copies[at] = None
        return self.refs[name].at[at]

    def done(self, name):
        if name in self.flushes:
            self.flushes[name].start()


def in_hbm(array):
    return pltpu.with_memory_space_constraint(array, pltpu.HBM)


def in_vmem(array):
    return pltpu.with_memory_space_constraint(array, pltpu.VMEM)


def whole_cut(ref):
    return ref


def run(body, ins, outs, deps=(), scratch=None, limit=20, flops=0, nbytes=0):
    scratch = scratch or Box()
    in_names = list(ins)
    out_names = list(outs)
    operands, in_specs, out_shapes, out_specs, scratch_shapes = [], [], [], [], []
    vmem = pl.BlockSpec(memory_space=pltpu.VMEM)
    hbm = pl.BlockSpec(memory_space=pltpu.HBM)
    smem = pl.BlockSpec(memory_space=pltpu.SMEM)
    for name in in_names:
        mode, array = ins[name][:2]
        operands.append(Box(d=in_hbm, r=in_hbm, v=in_vmem).get(mode, whole_cut)(array))
        in_specs.append(Box(v=vmem, s=smem, d=hbm, r=hbm)[mode])
    fetch_names = [name for name in out_names if outs[name][0] == "f"]
    for name in fetch_names:
        operands.append(in_hbm(outs[name][1]))
        in_specs.append(hbm)
    for dep in deps:
        operands.append(in_vmem(dep))
        in_specs.append(vmem)
    copy_count = 0
    plan = []
    for name in in_names:
        if ins[name][0] == "d":
            array = ins[name][1]
            cuts, block = ins[name][2] if len(ins[name]) > 2 else (None, array.shape)
            scratch_shapes.append(
                pltpu.VMEM(block if cuts is None else (len(cuts),) + block, array.dtype)
            )
            plan.append((name, cuts))
            copy_count += 1 if cuts is None else len(cuts)
    for name in out_names:
        mode = outs[name][0]
        if mode == "f":
            array, cuts, block = outs[name][1:4]
            out_shapes.append(pltpu.VMEM((len(cuts),) + block, array.dtype))
            copy_count += len(cuts)
        else:
            given = outs[name][1]
            space = pltpu.HBM if mode == "h" else pltpu.VMEM
            out_shapes.append(space(given.shape, given.dtype))
            if mode == "h":
                scratch_shapes.append(pltpu.VMEM(outs[name][1].shape, outs[name][1].dtype))
                copy_count += 1
        out_specs.append(hbm if mode == "h" else vmem)
    out_shapes.append(pltpu.VMEM((8, LANES), F32))
    out_specs.append(vmem)
    for spec in scratch.values():
        scratch_shapes.append(spec)
    scratch_shapes.append(pltpu.SemaphoreType.DMA((max(copy_count, 1),)))

    def kernel(*refs):
        refs = list(refs)
        sems = refs.pop()
        used = [0]

        def make(source, target):
            copy = pltpu.make_async_copy(source, target, sems.at[used[0]])
            used[0] += 1
            return copy

        n_in, n_fetch, n_out = len(in_names), len(fetch_names), len(out_names)
        in_refs = dict(zip(in_names, refs[:n_in]))
        fetch_refs = dict(zip(fetch_names, refs[n_in : n_in + n_fetch]))
        rest = refs[n_in + n_fetch + len(deps) :]
        out_refs = dict(zip(out_names, rest[:n_out]))
        token = rest[n_out]
        spare = rest[n_out + 1 :]
        io = Refs()
        for name in in_names:
            io.refs[name] = in_refs[name]
        for name, cuts in plan:
            buffer = spare.pop(0)
            io.refs[name] = buffer
            if cuts is None:
                io.copies[name] = [make(in_refs[name], buffer)]
            else:
                io.copies[name] = [
                    make(cut(in_refs[name]), buffer.at[at]) for at, cut in enumerate(cuts)
                ]
            for copy in io.copies[name]:
                copy.start()
        fetches = []
        for name in out_names:
            mode = outs[name][0]
            if mode == "f":
                for at, cut in enumerate(outs[name][2]):
                    source = fetch_refs[name]
                    source = cut(source, io) if len(outs[name]) > 4 else cut(source)
                    fetches.append(make(source, out_refs[name].at[at]))
                io.refs[name] = out_refs[name]
            elif mode == "h":
                buffer = spare.pop(0)
                io.refs[name] = buffer
                io.flushes[name] = make(buffer, out_refs[name])
            else:
                io.refs[name] = out_refs[name]
        for name in scratch:
            io.refs[name] = spare.pop(0)
        for copy in fetches:
            copy.start()
        token[...] = jnp.zeros(token.shape, F32)
        body(io)
        for name in list(io.copies):
            io[name]
        for copy in fetches:
            copy.wait()
        for copy in io.flushes.values():
            copy.wait()

    cost = COSTS[min(Counter.at, len(COSTS) - 1)]
    Counter.at += 1
    results = pl.pallas_call(
        kernel,
        out_shape=tuple(out_shapes),
        in_specs=in_specs,
        out_specs=tuple(out_specs),
        scratch_shapes=scratch_shapes,
        compiler_params=pltpu.CompilerParams(vmem_limit_bytes=limit * 1024 * 1024),
        cost_estimate=pl.CostEstimate(
            flops=int(cost * 10**9), bytes_accessed=10**8, transcendentals=0
        ),
    )(*operands)
    return Box(zip(out_names, results)), results[-1]


def columns_of(layer, parts):
    return [lambda ref, j=j: ref.at[layer, :, pl.ds(D * j, D)] for j in range(parts)], (D, D)


def rows_of(layer, parts):
    return [lambda ref, j=j: ref.at[layer, pl.ds(D * j, D), :] for j in range(parts)], (D, D)


def half_of(rows, own):
    def cut(ref, io):
        along = io.spot[1] if own else 1 - io.spot[1]
        return ref.at[:, pl.ds(pl.multiple_of(along * (FF // 2), LANES), FF // 2)]

    return [cut], (rows, FF // 2), True


def layer_of(layer, block):
    return [lambda ref: ref.at[layer]], block


COSTS = [10, 10, 10, 10, 10, 10, 10, 3, 120, 30, 10, 3, 30, 120, 60, 10, 60, 1, 3, 0.3, 60, 30, 6, 120, 0.3, 3, 120, 3, 1, 10, 6, 10, 6, 3, 22, 30, 30, 15, 60, 3, 10, 3]


class Counter:
    at = 0


def project(layer, spot, x, x_mode, wq, vecs, cs, fetches, deps):
    rows = x.shape[0]

    def body(io):
        x_in = up(io.x[...])
        xb = low(x_in)
        io.xt[...] = low(x_in.T)
        io.done("xt")
        lane = lane_of(rows)
        lo = lane < HEAD_DIM
        lane_state = lane_of(LANES)
        lo_state = lane_state < HEAD_DIM
        totals = jnp.zeros((LANES, LANES), F32)
        for j in range(3):
            w = io.part("wq", j)
            bias = vector(io, "qkv_bias", layer)[:, D * j : D * (j + 1)]
            pk = low(nn(xb, w[...]) + bias)
            io.packed[:, D * j : D * (j + 1)] = pk
            io.kept[:, D * j : D * (j + 1)] = pk
            pf = up(pk)
            cs_now = io.cs[...]
            for p in range(2):
                t0, t1, t2 = (
                    pf[:, (3 * p + i) * LANES : (3 * p + i + 1) * LANES] for i in range(3)
                )
                sp0 = softplus(t0)
                sp2 = softplus(t2)
                kf0 = low(jnp.where(lo, swap(sp0), sp0) * cs_now)
                kf1 = low(jnp.where(lo, sp2, swap(sp2)) * cs_now)
                s0 = tn(kf0, low(jnp.where(lo, t1, 1.0)))
                s1 = tn(kf1, low(jnp.where(lo, 1.0, t2)))
                pair = 2 * j + p
                io.state[pair * LANES : (pair + 1) * LANES, :] = low(
                    jnp.where(lo_state, s0, s1)
                )
                totals = jnp.where(lane_state == 2 * pair, swap(s0), totals)
                totals = jnp.where(lane_state == 2 * pair + 1, s1, totals)
        io.state[PAIRS * LANES :, :] = low(totals.T[:16])
        io.done("kept")

    outs = Box(
        packed=("v", shape(rows, 3 * D, dtype=BF)),
        xt=("h", shape(D, rows, dtype=BF)),
        state=("v", shape(STATE_ROWS, LANES, dtype=BF)),
    )
    outs.kept = ("h", shape(rows, 3 * D, dtype=BF))
    outs.update(fetches)
    return run(
        body,
        Box(spot=("s", spot), x=(x_mode, x), wq=wq, cs=("d", cs), **vecs),
        outs,
        deps,
        flops=2 * rows * D * 3 * D,
        nbytes=2 * D * 3 * D,
    )


def inside(spot, packed, cm, long, fetches, deps):
    rows = packed.shape[0]

    def body(io):
        lo = lane_of(rows) < HEAD_DIM
        for pair in range(PAIRS):
            at = pair * 3 * LANES
            t0, t1, t2 = (
                up(io.packed[:, at + i * LANES : at + (i + 1) * LANES]) for i in range(3)
            )
            sp0, sp1, sp2 = softplus(t0), softplus(t1), softplus(t2)
            a0 = nt(low(jnp.where(lo, sp0, 0.0)), low(swap(sp0)))
            a1 = nt(low(jnp.where(lo, 0.0, sp1)), low(swap(sp2)))
            mask = io.cm[...]
            n0 = nn(low(a0 * mask), low(jnp.where(lo, t1, 1.0)))
            n1 = nn(low(a1 * mask), low(jnp.where(lo, 1.0, t2)))
            here = slice(pair * LANES, (pair + 1) * LANES)
            io.num[:, here] = jnp.where(lo, n0, n1)
            io.den[:, here] = swap(jnp.where(lo, n1, n0))
            sq = low(jnp.where(lo, sp0, sp1))
            io.sq[:, here] = sq
            if long:
                io.sq_kept[:, here] = sq

    outs = Box(
        num=("v", shape(rows, D)),
        den=("v", shape(rows, D)),
        sq=("v", shape(rows, D, dtype=BF)),
    )
    if long:
        outs.sq_kept = ("h", shape(rows, D, dtype=BF))

    def body_all(io):
        body(io)
        if long:
            io.done("sq_kept")

    outs.update(fetches)
    return run(
        body_all,
        Box(spot=("s", spot), packed=("v", packed), cm=("d", cm)),
        outs,
        deps,
        flops=4 * HEADS * rows * rows * LANES,
        nbytes=rows * D * 16,
    )


def sum_states(io, count):
    total = up(io.recv0[...])
    for at in range(1, count):
        total = total + up(io["recv%d" % at][...])
    return total


def vector(io, name, layer):
    return up(io[name][...])[layer : layer + 1]


def state_totals(total):
    return jnp.concatenate(
        [total[PAIRS * LANES :], jnp.zeros((LANES - 16, LANES), F32)], axis=0
    ).T


def totals_column(totals, head):
    return jnp.broadcast_to(totals[:, head : head + 1], (LANES, LANES))


def diagonal(a, b):
    zero = jnp.zeros((LANES, LANES), BF)
    return above(beside(a, zero), beside(zero, b))


def second_norm_back(io, gs, n2, r2, gain):
    gz2 = norm_back(gs, n2, r2, gain)
    gb2 = low(gz2)
    io.gz2[...] = gz2
    io.gb2[...] = gb2
    io.gb2t[...] = low(gz2.T)
    io.sums_a[...] = jnp.zeros((8, D), F32)
    io.sums_a[0:1, :] = column_sum(up(gb2))
    io.sums_a[1:2, :] = column_sum(gs)
    io.sums_a[2:3, :] = column_sum(gs * n2)
    io.done("sums_a")


def second_norm_outs(rows):
    return Box(
        gz2=("v", shape(rows, D)),
        gb2=("v", shape(rows, D, dtype=BF)),
        gb2t=("v", shape(D, rows, dtype=BF)),
        sums_a=("h", shape(8, D)),
    )


def layer_forward(layer, recv, x, x_mode, inner, weights, vecs, cs, cotangent, deps):
    rows = x.shape[0]
    last = cotangent is not None

    def body(io):
        lane = lane_of(rows)
        lo = lane < HEAD_DIM
        lo_state = lane_of(LANES) < HEAD_DIM
        before = sum_states(io, len(recv))
        io.before[...] = low(before)
        io.done("before")
        totals = state_totals(before)
        for pair in range(PAIRS):
            here = slice(pair * LANES, (pair + 1) * LANES)
            sq = up(io.sq[:, here])
            other = swap(sq)
            state = before[here]
            cs_now = io.cs[...]
            feats = beside(
                low(jnp.where(lo, sq, other) * cs_now), low(jnp.where(lo, other, sq) * cs_now)
            )
            both = nn(
                feats,
                diagonal(
                    low(jnp.where(lo_state, state, totals_column(totals, 2 * pair))),
                    low(jnp.where(lo_state, totals_column(totals, 2 * pair + 1), state)),
                ),
            )
            n0 = both[:, :LANES]
            n1 = both[:, LANES:]
            num = io.num[:, here] + jnp.where(lo, n0, n1)
            inv = 1.0 / (io.den[:, here] + swap(jnp.where(lo, n1, n0)))
            mixed = num * inv
            io.inv[:, here] = inv
            io.mixed[:, here] = low(mixed)
            io.mixt[here, :] = low(mixed.T)
        io.done("inv")
        io.done("mixed")
        io.done("mixt")
        shifts = up(io.shifts[layer])
        gains = up(io.gains[layer])
        bias = vector(io, "ffn_bias", layer)
        branch = nn(io.mixed[...], io.part("wo", 0)[...]) + shifts[0:1]
        middle, n1, r1 = norm_apply(up(io.x[...]) + branch, gains[0:1], shifts[2:3])
        io.n1[...] = n1
        io.done("n1")
        io.r1[...] = jnp.broadcast_to(r1, (rows, LANES))
        io.done("r1")
        io.midt[...] = low(middle.T)
        io.done("midt")
        mid = low(middle)
        total = middle + shifts[1:2]
        for j in range(FF // D):
            here = slice(D * j, D * (j + 1))
            pre = nn(mid, io.part("w1", j)[...]) + bias[:, here]
            cdf = 0.5 * (1.0 + lax.erf(pre * (1.0 / math.sqrt(2.0))))
            hid = low(pre * cdf)
            io.hid[:, here] = hid
            io.slope[:, here] = low(
                cdf + pre * jnp.exp(-0.5 * pre * pre) * (1.0 / math.sqrt(2.0 * math.pi))
            )
            total = total + nn(hid, io.part("w2", j)[...])
        io.done("hid")
        io.done("slope")
        s_next, n2, r2 = norm_apply(total, gains[1:2], shifts[3:4])
        if last:
            io.output[...] = low(s_next)
            io.done("output")
            second_norm_back(io, up(io.cot[...]), n2, r2, gains[1:2])
        else:
            io.s_next[...] = s_next
            io.n2[...] = n2
            io.done("n2")
            io.r2[...] = jnp.broadcast_to(r2, (rows, LANES))
            io.done("r2")

    ins = Box({"recv%d" % i: ("v", recv[i]) for i in range(len(recv))})
    ins.update(
        Box(
            x=(x_mode, x),
            num=("v", inner.num),
            den=("v", inner.den),
            sq=("v", inner.sq),
            wo=("v", weights.wo),
            w1=("v", weights.w1),
            w2=("v", weights.w2),
            cs=("d", cs),
            **vecs,
        )
    )
    if last:
        ins.cot = ("d", cotangent)
    mode = "v" if last else "h"
    outs = Box(
        before=("h", shape(STATE_ROWS, LANES, dtype=BF)),
        mixed=(mode, shape(rows, D, dtype=BF)),
        mixt=("h", shape(D, rows, dtype=BF)),
        inv=(mode, shape(rows, D)),
        n1=(mode, shape(rows, D)),
        r1=(mode, shape(rows, LANES)),
        midt=(mode, shape(D, rows, dtype=BF)),
        hid=(mode, shape(rows, FF, dtype=BF)),
        slope=(mode, shape(rows, FF, dtype=BF)),
    )
    if last:
        outs.output = ("h", shape(rows, D, dtype=BF))
        outs.update(second_norm_outs(rows))
    else:
        outs.s_next = ("v", shape(rows, D))
        outs.n2 = ("h", shape(rows, D))
        outs.r2 = ("h", shape(rows, LANES))
    return run(
        body,
        ins,
        outs,
        deps,
        limit=20,
        flops=2 * rows * D * (D + 2 * FF),
        nbytes=2 * D * (D + 2 * FF),
    )


def layer_back(layer, spot, top, kept, mode, weights, vecs, cs, fetches, deps, after=None):
    rows = top.gz2.shape[0]

    def body(io):
        lane = lane_of(rows)
        lo = lane < HEAD_DIM
        lane_state = lane_of(LANES)
        lo_state = lane_state < HEAD_DIM
        left_rows = lax.broadcasted_iota(jnp.int32, (LANES, LANES), 0) < HEAD_DIM
        same = low(jnp.where(lo_state == left_rows, 1.0, 0.0))
        gb2 = io.gb2[...]
        gmid = io.gz2[...]
        sums = io.sums_b
        sums[...] = jnp.zeros((8, D), F32)
        for j in range(FF // D):
            here = slice(D * j, D * (j + 1))
            gpre = low(nt(gb2, io.part("w2", j)[...]) * up(io.slope[:, here]))
            io.gpre[:, here] = gpre
            sums[j : j + 1, :] = column_sum(up(gpre))
            gmid = gmid + nt(gpre, io.part("w1", j)[...])
        n1 = io.n1[...]
        gz1 = norm_back(gmid, n1, io.r1[:, :1], up(io.gains[layer])[0:1])
        gb1 = low(gz1)
        io.gz1[...] = gz1
        io.gb1[...] = gb1
        sums[4:5, :] = column_sum(up(gb1))
        sums[5:6, :] = column_sum(gmid)
        sums[6:7, :] = column_sum(gmid * n1)
        io.done("sums_b")
        gmixed = up(low(nt(gb1, io.part("wo", 0)[...])))
        totals = jnp.zeros((LANES, LANES), F32)
        for pair in range(PAIRS):
            here = slice(pair * LANES, (pair + 1) * LANES)
            u = gmixed[:, here] * io.inv[:, here]
            dd = -nn(low(u * up(io.mixed[:, here])), same)
            io.u[:, here] = low(u)
            io.dd[:, here] = low(dd)
            ds = swap(dd)
            sq = up(io.sq[:, here])
            other = swap(sq)
            cs_now = io.cs[...]
            s0 = tn(low(jnp.where(lo, sq, other) * cs_now), low(jnp.where(lo, u, ds)))
            s1 = tn(low(jnp.where(lo, other, sq) * cs_now), low(jnp.where(lo, ds, u)))
            io.state[here, :] = low(jnp.where(lo_state, s0, s1))
            totals = jnp.where(lane_state == 2 * pair, swap(s0), totals)
            totals = jnp.where(lane_state == 2 * pair + 1, s1, totals)
        io.state[PAIRS * LANES :, :] = low(totals.T[:16])

    ins = Box(
        gz2=("v", top.gz2),
        gb2=("v", top.gb2),
        wo=("v", weights.wo),
        w1=("v", weights.w1),
        w2=("v", weights.w2),
    )
    for name in ("slope", "n1", "r1", "inv", "mixed", "sq"):
        ins[name] = (mode, kept[name])
    if after is not None:
        ins.after = ("r", after)
    ins.spot = ("s", spot)
    ins.gains = vecs.gains
    ins.cs = ("d", cs)
    outs = Box(
        gpre=("v", shape(rows, FF, dtype=BF)),
        gb1=("v", shape(rows, D, dtype=BF)),
        gz1=("v", shape(rows, D)),
        u=("v", shape(rows, D, dtype=BF)),
        dd=("v", shape(rows, D, dtype=BF)),
        state=("v", shape(STATE_ROWS, LANES, dtype=BF)),
        sums_b=("h", shape(8, D)),
    )
    outs.update(fetches)
    return run(
        body,
        ins,
        outs,
        deps,
        limit=20,
        flops=2 * rows * D * (D + 2 * FF),
        nbytes=2 * D * (D + 2 * FF),
    )


def mix_back(layer, recv, spot, low_part, kept, cs, cm, wq, below, fetches, deps):
    rows = low_part.u.shape[0]

    def body(io):
        lane = lane_of(rows)
        lo = lane < HEAD_DIM
        lane_state = lane_of(LANES)
        lo_state = lane_state < HEAD_DIM
        one_left = jnp.where(lane == 0, 1.0, 0.0)
        one_right = jnp.where(lane == HEAD_DIM, 1.0, 0.0)
        later = sum_states(io, len(recv))
        later_totals = state_totals(later)
        before = up(io.before[...])
        before_totals = state_totals(before)

        def halves(state, totals, pair):
            first = jnp.where(
                lo_state,
                state,
                jnp.where(lane_state == HEAD_DIM, totals_column(totals, 2 * pair), 0.0),
            )
            second = jnp.where(
                lo_state,
                jnp.where(lane_state == 0, totals_column(totals, 2 * pair + 1), 0.0),
                state,
            )
            return diagonal(low(first), low(second))

        def fold(v, cs_now):
            first = v[:, :LANES] * cs_now
            second = v[:, LANES:] * cs_now
            return jnp.where(lo, first + swap(first), second + swap(second))

        for pair in range(PAIRS):
            here = slice(pair * LANES, (pair + 1) * LANES)
            at = pair * 3 * LANES
            t0, t1, t2 = (
                up(io.packed[:, at + i * LANES : at + (i + 1) * LANES]) for i in range(3)
            )
            cs_now = io.cs[...]
            mask = io.cm[...]
            sp0, sp1, sp2 = softplus(t0), softplus(t1), softplus(t2)
            sw0 = swap(sp0)
            sw2 = swap(sp2)
            q0 = low(jnp.where(lo, sp0, 0.0))
            k0 = low(jnp.where(lo, sw0, 0.0))
            q1 = low(jnp.where(lo, 0.0, sp1))
            k1 = low(jnp.where(lo, 0.0, sw2))
            kf = beside(
                low(jnp.where(lo, sw0, sp0) * cs_now), low(jnp.where(lo, sp2, sw2) * cs_now)
            )
            v0 = low(jnp.where(lo, t1, one_right))
            v1 = low(jnp.where(lo, one_left, t2))
            uf = up(io.u[:, here])
            ds = swap(up(io.dd[:, here]))
            u0 = low(jnp.where(lo, uf, ds))
            u1 = low(jnp.where(lo, ds, uf))
            ua = low(jnp.where(lo, uf, 0.0))
            ub = low(jnp.where(lo, 0.0, uf))
            p0 = low(nt(q0, k0) * mask)
            p1 = low(nt(q1, k1) * mask)
            d0 = low(nt(u0, v0) * mask)
            d1 = low(nt(u1, v1) * mask)
            after = later[here]
            eq = nt(beside(u0, u1), halves(before[here], before_totals, pair))
            ek = nt(beside(v0, v1), halves(after, later_totals, pair))
            after_split = above(
                low(jnp.where(lo_state, after, 0.0)), low(jnp.where(lo_state, 0.0, after))
            )
            dq = fold(eq, cs_now) + nn(d0, k0) + nn(d1, k1)
            dk = fold(ek, cs_now) + tn(d0, q0) + tn(d1, q1)
            dv = nn(kf, after_split) + tn(p0, ua) + tn(p1, ub)
            dks = swap(dk)
            gpk = io.gpk
            gpk[:, at : at + LANES] = low(jnp.where(lo, dq, dks) * sigmoid(t0))
            gpk[:, at + LANES : at + 2 * LANES] = low(jnp.where(lo, dv, dq * sigmoid(t1)))
            gpk[:, at + 2 * LANES : at + 3 * LANES] = low(jnp.where(lo, dks * sigmoid(t2), dv))
        grad = io.gz1[...]
        io.sums_c[...] = jnp.zeros((8, D), F32)
        for j in range(3):
            gpk = io.gpk[:, D * j : D * (j + 1)]
            io.sums_c[j : j + 1, :] = column_sum(up(gpk))
            grad = grad + nt(gpk, io.part("wq", j)[...])
        io.done("sums_c")
        if below is None:
            io.grad[...] = grad
            io.done("grad")
        else:
            gain = up(io.gains[layer - 1])[1:2]
            second_norm_back(io, grad, io.n2[...], io.r2[:, :1], gain)
        near = io.spot[3]
        far = io.spot[4]
        gpk = up(io.gpk[...])
        gb1 = up(io.gb1[...])
        for low_bit in range(2):
            slot = low_bit ^ near
            for source, start in ((gb1, 0), (gpk, D // 2)):
                width = source.shape[1] // 4
                first = source[:, low_bit * width : (low_bit + 1) * width]
                second = source[:, (low_bit + 2) * width : (low_bit + 3) * width]
                both = beside(
                    jnp.where(far == 0, first, second), jnp.where(far == 0, second, first)
                )
                io.gcol[slot, :, start : start + 2 * width] = low(both)

    ins = Box({"recv%d" % i: ("v", recv[i]) for i in range(len(recv))})
    ins.update(
        Box(
            spot=("s", spot),
            u=("v", low_part.u),
            dd=("v", low_part.dd),
            gb1=("v", low_part.gb1),
            gz1=("v", low_part.gz1),
            packed=("d", kept.packed),
            cs=("d", cs),
            cm=("d", cm),
            before=("d", kept.before),
            wq=wq,
        )
    )
    outs = Box(
        gcol=("v", shape(2, rows, 2 * D, dtype=BF)),
        sums_c=("h", shape(8, D)),
    )
    if below is None:
        outs.grad = ("h", shape(rows, D))
    else:
        ins.n2 = ("d", below.n2)
        ins.r2 = ("d", below.r2)
        ins.gains = below.vecs.gains
        outs.update(second_norm_outs(rows))
    outs.update(fetches)
    return run(
        body,
        ins,
        outs,
        deps,
        scratch=Box(gpk=pltpu.VMEM((rows, 3 * D), BF)),
        limit=20,
        flops=2 * rows * D * 3 * D + 12 * HEADS * rows * rows * LANES,
        nbytes=2 * D * 3 * D,
    )


def owners(spot, core):
    return [
        ((spot[1] ^ along) * 2 + (spot[2] ^ across)) * 2 + core
        for across in range(2)
        for along in range(2)
    ]


def out_terms(io, core, put):
    near, far = io.spot[3], io.spot[4]
    for at, block in enumerate(owners(io.spot, core)):
        lanes = pl.ds(pl.multiple_of(block * (FF // 8), LANES), FF // 8)
        io.rhs[:, at * (FF // 8) : (at + 1) * (FF // 8)] = io.hid[:, lanes]
    lhs = io.gb2t[...]
    for half in range(2):
        grad = nn(lhs, io.rhs[:, half * D : (half + 1) * D])
        for sub in range(2):
            at = 2 * half + sub
            for n in range(4):
                lanes = pl.ds(pl.multiple_of(((n // 2) ^ far) * (D // 2), LANES), D // 2)
                put(
                    at,
                    (n % 2) ^ near,
                    None,
                    lanes,
                    grad[n * 192 : (n + 1) * 192, sub * (D // 2) : (sub + 1) * (D // 2)],
                )


def pair_terms(io, core, put):
    near, far = io.spot[3], io.spot[4]
    tokens = io.hid.shape[1]
    width = FF // 8
    io.lhs[:, :tokens] = io.gb2t[...]
    io.lhs[:, tokens:] = io.gb2t_got[...]
    for across in range(2):
        block = (io.spot[2] ^ across) * 2 + core
        lanes = pl.ds(pl.multiple_of(block * width, LANES), width)
        io.rhs[:tokens, across * width : (across + 1) * width] = io.hid[0, :, lanes]
        io.rhs[tokens:, across * width : (across + 1) * width] = io.hid_got[0, :, lanes]
    grad = nn(io.lhs[...], io.rhs[...])
    for across in range(2):
        for n in range(4):
            lanes = pl.ds(pl.multiple_of(((n // 2) ^ far) * width, LANES), width)
            put(
                across,
                (n % 2) ^ near,
                None,
                lanes,
                grad[n * 192 : (n + 1) * 192, across * width : (across + 1) * width],
            )


def gather_rows(io, name, target, core):
    for at, block in enumerate(owners(io.spot, core)):
        io[target][at * 96 : (at + 1) * 96, :] = io[name][
            pl.ds(pl.multiple_of(block * 96, 16), 96), :
        ]


def in_terms(io, core, put):
    near, far = io.spot[3], io.spot[4]
    gather_rows(io, "midt", "lhs", core)
    for n in range(4):
        grad = nn(io.lhs[...], io.gpre[:, n * D : (n + 1) * D])
        for at in range(4):
            put(at, (n % 2) ^ near, (n // 2) ^ far, slice(None), grad[at * 96 : (at + 1) * 96])


def mix_terms(io, core, put):
    gather_rows(io, "mixt", "lhs", core)
    gather_rows(io, "xt", "lhs_two", core)
    for slot in range(2):
        for lhs, start, stop in (("lhs", 0, D // 2), ("lhs_two", D // 2, 2 * D)):
            grad = nn(io[lhs][...], io.gcol[slot, :, start:stop])
            for at in range(4):
                put(
                    at,
                    slot,
                    None,
                    slice(start, stop),
                    grad[at * 96 : (at + 1) * 96],
                )


def part_rows(part, count):
    if part is None:
        return slice(None)
    return pl.ds(pl.multiple_of(part * count, 16), count)


TERMS = Box(pair=pair_terms, out=out_terms, inner=in_terms, mix=mix_terms)


def grad_setup(kind, spot, operands):
    ins = Box(spot=("s", spot))
    if kind == "out":
        gb2t, hid = operands
        tokens = gb2t.shape[1]
        ins.gb2t = ("v", gb2t)
        ins.hid = ("v", hid)
        return ins, Box(rhs=pltpu.VMEM((tokens, FF // 2), BF)), (192, D), tokens
    if kind == "pair":
        for name, array in zip(("gb2t", "gb2t_got", "hid", "hid_got"), operands):
            ins[name] = ("v", array)
        tokens = 2 * operands[0].shape[1]
        both = Box(lhs=pltpu.VMEM((D, tokens), BF), rhs=pltpu.VMEM((tokens, D), BF))
        return ins, both, (192, D), tokens
    lhs = pltpu.VMEM((D // 2, operands[0].shape[1]), BF)
    if kind == "inner":
        midt, gpre = operands
        ins.midt = ("v", midt)
        ins.gpre = ("v", gpre)
        return ins, Box(lhs=lhs), (192, D), midt.shape[1]
    mixt, xt, gcol = operands
    ins.mixt = ("d", mixt)
    ins.xt = ("d", xt)
    ins.gcol = ("v", gcol)
    return ins, Box(lhs=lhs, lhs_two=lhs), (96, 2 * D), xt.shape[1]


def grad_send(kind, spot, operands, deps):
    ins, scratch, block, tokens = grad_setup(kind, spot, operands)

    def body(io):
        def put(at, slot, part, lanes, value):
            io.send[at, slot, part_rows(part, value.shape[0]), lanes] = low(value)

        TERMS[kind](io, 1 - io.spot[0], put)

    outs, token = run(
        body,
        ins,
        Box(send=("v", shape(2 if kind == "pair" else 4, 2, *block, dtype=BF))),
        deps,
        scratch=scratch,
        flops=2 * tokens * 8 * block[0] * block[1],
        nbytes=4 * 2 * 2 * block[0] * block[1],
    )
    return outs.send, token


def grad_keep(kind, spot, operands, got, order, deps):
    ins, scratch, block, tokens = grad_setup(kind, spot, operands)
    ins.got = ("v", got)
    rows_all = block[0]
    if order == "both":
        half = (rows_all // 2, block[1])
    else:
        half = block

    def body(io):
        def put(at, slot, part, lanes, value):
            count = value.shape[0]
            rows = part_rows(part, count)
            value = low(value + up(io.got[at, slot, rows, lanes]))
            across, along = at // 2, at % 2
            if kind == "pair":
                io["send0" if at else "keep0"][slot, rows, lanes] = value
            elif order == "x":
                io["send0" if across else "keep0"][along, slot, rows, lanes] = value
            elif order == "y":
                io["send0" if along else "keep0"][across, slot, rows, lanes] = value
            else:
                rows = part_rows(part, count // 2)
                first, second = value[: count // 2], value[count // 2 :]
                io["send0" if across else "keep0"][along, slot, rows, lanes] = first
                io["send1" if along else "keep1"][across, slot, rows, lanes] = second

        TERMS[kind](io, io.spot[0], put)

    names = ["send0", "keep0"] + (["send1", "keep1"] if order == "both" else [])
    return run(
        body,
        ins,
        {
            name: ("v", shape(*((2,) if kind == "pair" else (2, 2)), *half, dtype=BF))
            for name in names
        },
        deps,
        scratch=scratch,
        flops=2 * tokens * 8 * block[0] * block[1],
        nbytes=4 * 2 * 4 * block[0] * block[1],
    )


def grad_pass(groups, deps):
    pairs = [
        (group["keep%d" % at], group["got%d" % at]) for group in groups for at in halves_of(group)
    ]
    ins, outs = Box(), Box()
    for at, (keep, got) in enumerate(pairs):
        ins["keep%d" % at] = ("v", keep)
        ins["got%d" % at] = ("v", got)
        outs["next%d" % at] = ("v", shape(*keep.shape[1:], dtype=BF))

    def body(io):
        for at in range(len(pairs)):
            io["next%d" % at][...] = low(
                up(io["keep%d" % at][1]) + up(io["got%d" % at][1])
            )

    outs, token = run(body, ins, outs, deps)
    return [outs["next%d" % at] for at in range(len(pairs))], token


def halves_of(group):
    return [at for at in range(2) if "keep%d" % at in group]


def group_ins(groups):
    ins = Box()
    for which, group in enumerate(groups):
        for at in halves_of(group):
            for name in ("keep", "got", "come"):
                if "%s%d" % (name, at) in group:
                    ins["%s%d_%d" % (name, which, at)] = ("v", group["%s%d" % (name, at)])
    return ins


def group_sum(io, which, at, slot):
    if "come%d_%d" % (which, at) not in io.refs:
        return up(io["keep%d_%d" % (which, at)][slot]) + up(io["got%d_%d" % (which, at)][slot])
    return (
        up(io["keep%d_%d" % (which, at)][0, slot])
        + up(io["got%d_%d" % (which, at)][0, slot])
        + up(io["come%d_%d" % (which, at)][slot])
    )


def grad_near(groups, deps):
    ins = group_ins(groups)
    places = [(which, at) for which, group in enumerate(groups) for at in halves_of(group)]
    total = sum(group["keep%d" % at].shape[-2] for group in groups for at in halves_of(group))
    lanes = groups[0].keep0.shape[-1]

    def body(io):
        start = 0
        for which, at in places:
            rows = groups[which]["keep%d" % at].shape[-2]
            here = slice(start, start + rows)
            io.near[here, :] = low(group_sum(io, which, at, 1))
            io.stay[here, :] = low(group_sum(io, which, at, 0))
            start += rows

    return run(
        body,
        ins,
        Box(
            near=("v", shape(total, lanes, dtype=BF)),
            stay=("v", shape(total, lanes, dtype=BF)),
        ),
        deps,
    )


def grad_collect(kinds, groups, deps):
    ins = group_ins(groups)
    ins.spot = ("s", groups[0].spot)

    def body(io):
        near, far = io.spot[3], io.spot[4]
        for which, kind in enumerate(kinds):
            for slot in range(2):
                full = [group_sum(io, which, at, slot) for at in halves_of(groups[which])]
                if kind == "mix":
                    both = above(full[0], full[1])
                    quarter = D // 4
                    parts = [
                        beside(both[:, :quarter], both[:, 2 * quarter : 5 * quarter]),
                        beside(both[:, quarter : 2 * quarter], both[:, 5 * quarter :]),
                    ]
                elif kind == "inner":
                    parts = [full[0][:96], full[0][96:]]
                else:
                    parts = [
                        beside(full[0][:96, : D // 2], full[0][96:, : D // 2]),
                        beside(full[0][:96, D // 2 :], full[0][96:, D // 2 :]),
                    ]
                for half in range(2):
                    owner = (slot ^ near) + 2 * (half ^ far)
                    io.blocks[owner, which * 96 : (which + 1) * 96, :] = low(parts[half])

    outs, token = run(
        body, ins, Box(blocks=("v", shape(4, 96 * len(kinds), D, dtype=BF))), deps
    )
    return outs.blocks, token


def grad_far(kinds, stay, near, deps):
    count = len(kinds)

    def body(io):
        full = up(io.stay[...]) + up(io.near[...])
        if kinds[0] == "mix":
            quarter = D // 4
            io.own[...] = beside(full[:, :quarter], full[:, 2 * quarter : 5 * quarter])
            io.far[...] = low(
                beside(full[:, quarter : 2 * quarter], full[:, 5 * quarter : 8 * quarter])
            )
            return
        for at, kind in enumerate(kinds):
            part = full[192 * at : 192 * (at + 1)]
            here = slice(96 * at, 96 * (at + 1))
            if kind == "out":
                io.own[here, :] = beside(part[:96, : D // 2], part[96:, : D // 2])
                io.far[here, :] = low(beside(part[:96, D // 2 :], part[96:, D // 2 :]))
            elif kind == "inner":
                io.own[here, :] = part[:96]
                io.far[here, :] = low(part[96:])
            else:
                io.own[here, :] = above(part[:48], part[96:144])
                io.far[here, :] = low(above(part[48:96], part[144:]))

    return run(
        body,
        Box(stay=("v", stay), near=("v", near)),
        Box(
            own=("v", shape(count * 96, D)),
            far=("v", shape(count * 96, D, dtype=BF)),
        ),
        deps,
    )


def grad_last(kind, terms, deps):
    ins = Box()
    for layer in range(LAYERS):
        for at, term in enumerate(terms[layer]):
            ins["term%d_%d" % (layer, at)] = ("v", term)
    if kind == "mix":
        outs = Box(
            first=("h", shape(LAYERS, 96, 3 * D // 4)),
            second=("h", shape(LAYERS, 96, D // 4)),
        )
    else:
        outs = Box(
            first=("h", shape(LAYERS, 96, D)),
            second=("h", shape(LAYERS, FF // 8, D // 4)),
        )

    def body(io):
        for layer in range(LAYERS):
            full = up(io["term%d_0" % layer][...])
            for at in range(1, len(terms[layer])):
                full = full + up(io["term%d_%d" % (layer, at)][...])
            if kind == "mix":
                io.first[layer] = full[:, D // 4 :]
                io.second[layer] = full[:, : D // 4]
            else:
                io.first[layer] = full[96:]
                io.second[layer, :, :96] = full[:96, : D // 2].T
                io.second[layer, :, 96:] = full[:96, D // 2 :].T
        io.done("first")
        io.done("second")

    return run(body, ins, outs, deps)


def wide_swap(v, bit):
    size = lax.axis_size("wide")
    return lax.ppermute(v, "wide", [(i, i ^ bit) for i in range(size)])


def narrow_swap(v, bit):
    size = lax.axis_size("narrow")
    return lax.ppermute(v, "narrow", [(i, i ^ bit) for i in range(size)])


CORE, ACROSS, ALONG = 1, 2, 4
NEAR, FAR = 1, 2


def reduce_plain(left, right):
    term = low(tn(left, right))
    part = lax.psum_scatter(term, "narrow", scatter_dimension=1, tiled=True)
    return lax.psum_scatter(up(part), "wide", scatter_dimension=0, tiled=True)


def move(v, shift):
    size = lax.axis_size("narrow")
    pairs = [(i, i + shift) for i in range(size) if 0 <= i + shift < size]
    return lax.ppermute(v, "narrow", pairs)


def travel(state, step):
    return [move(state, step * shift) for shift in range(1, lax.axis_size("narrow"))]


SUM_ROWS = (3, 7, 3)


def collect_sums(parts, deps):
    def body(io):
        io.sums[...] = jnp.zeros((32, D), F32)
        start = 0
        for at in range(len(parts)):
            rows = SUM_ROWS[at % 3]
            io.sums[start : start + rows, :] = io["part%d" % at][:rows, :]
            start += rows

    outs, token = run(
        body,
        Box({"part%d" % at: ("d", part) for at, part in enumerate(parts)}),
        Box(sums=("v", shape(32, D))),
        deps,
    )
    return outs.sums, token


def add_up(a, b, deps):
    def body(io):
        io.sum[...] = (up(io.a[...]) + up(io.b[...])).astype(a.dtype)

    outs, token = run(
        body,
        Box(a=("v", a), b=("v", b)),
        Box(sum=("v", shape(*a.shape, dtype=a.dtype))),
        deps,
    )
    return outs.sum, token


def shards(
    tokens,
    cotangent,
    horizons,
    qkv_weight,
    out_weight,
    ffn_in_weight,
    ffn_out_weight,
    qkv_bias,
    ffn_in_bias,
    model_biases,
    norm_gains,
):
    Counter.at = 0
    rows = tokens.shape[0]
    wide = lax.axis_size("wide")
    narrow = lax.axis_size("narrow")
    wide_at = lax.axis_index("wide")
    narrow_at = lax.axis_index("narrow")
    fast = wide == 8 and narrow == 4
    place = [wide_at % 2, (wide_at // 4) % 2, (wide_at // 2) % 2, narrow_at % 2, narrow_at // 2]
    if not fast:
        place = [wide_at * 0] * 5
    place.append(narrow_at)
    spot = jnp.stack(place).astype(jnp.int32)
    step = 0.5 * math.pi / up(horizons[0])
    places = up(narrow_at * rows + jnp.arange(rows)) * step
    cs = beside(
        jnp.broadcast_to(jnp.cos(places)[:, None], (rows, HEAD_DIM)),
        jnp.broadcast_to(jnp.sin(places)[:, None], (rows, HEAD_DIM)),
    )

    def mask(step):
        apart = jnp.arange(rows)[:, None] - jnp.arange(rows)[None, :]
        return jnp.where(apart >= 0, jnp.cos(up(apart) * step), 0.0)

    vecs = Box(
        ffn_bias=("d", ffn_in_bias),
        shifts=("d", model_biases),
        gains=("d", norm_gains),
    )
    wq_cuts = [("d", qkv_weight, columns_of(layer, 3)) for layer in range(LAYERS)]

    def weight_fetch(layer):
        return Box(
            wo=("f", out_weight) + layer_of(layer, (D, D)),
            w1=("f", ffn_in_weight) + columns_of(layer, 4),
            w2=("f", ffn_out_weight) + rows_of(layer, 4),
        )

    x = tokens
    wq = wq_cuts[0]
    saved = []
    deps = ()
    for layer in range(LAYERS):
        last = layer == LAYERS - 1
        hidden = last and fast
        fetches = Box(hid_send=("f", saved[0].hid) + half_of(rows, False)) if hidden else Box()
        x_mode = "v" if layer else "d"
        bias = Box(qkv_bias=("d", qkv_bias))
        first, token = project(layer, spot, x, x_mode, wq, bias, cs, fetches, deps)
        hid_got = wide_swap(first.hid_send, ALONG) if hidden else None
        if not layer:
            cm = mask(step + token[0, 0])
        recv = travel(first.state, 1)
        fetches = weight_fetch(layer)
        if not last:
            fetches.wq = ("f", qkv_weight) + columns_of(layer + 1, 3)
        inner, token = inside(spot, first.packed, cm, not last, fetches, (token,))
        weights = inner
        kept, token = layer_forward(
            layer,
            recv,
            x,
            "v" if layer else "d",
            inner,
            weights,
            vecs,
            cs,
            cotangent if last else None,
            (token,),
        )
        kept.packed = first.kept
        kept.xt = first.xt
        kept.sq = inner.sq if last else inner.sq_kept
        kept.vecs = vecs
        saved.append(kept)
        deps = (token,)
        if not last:
            x = kept.s_next
            wq = ("v", inner.wq)

    output = saved[1].output
    one, zero = saved[1], saved[0]
    if not fast:
        grads = [None] * LAYERS
        sums = [None] * LAYERS
        top = one
        for layer in (1, 0):
            kept = saved[layer]
            fetch = Box() if layer == 1 else Box()
            back, token = layer_back(
                layer, spot, top, kept, "v" if layer else "d", weights, vecs, cs, fetch, (token,)
            )
            recv = travel(back.state, -1)
            below = saved[0] if layer == 1 else None
            fetch = weight_fetch(0) if layer == 1 else Box()
            mix, token = mix_back(
                layer, recv, spot, back, kept, cs, cm, wq_cuts[layer], below, fetch, (token,)
            )
            gcol = mix.gcol
            gpk = jnp.concatenate(
                [gcol[n % 2, :, 384 + 576 * (n // 2) : 960 + 576 * (n // 2)] for n in range(4)],
                axis=1,
            )
            grads[layer] = (
                reduce_plain(kept.xt.T, gpk),
                reduce_plain(kept.mixt.T, back.gb1),
                reduce_plain(kept.midt.T, back.gpre),
                reduce_plain(kept.hid, top.gb2),
            )
            sums[layer] = jnp.concatenate(
                [top.sums_a[:3], back.sums_b[:7], mix.sums_c[:3]], axis=0
            )
            top = mix
            weights = mix
        sums = lax.psum(jnp.stack(sums), ("wide", "narrow"))
        grad_qkv, grad_o, grad_in, grad_out = (
            jnp.stack([grads[l][k] for l in range(LAYERS)]) for k in range(4)
        )
        input_grad = mix.grad
    else:
        group = Box()
        ops = Box()

        def send(name, kind, operands, token):
            ops[name] = (kind, operands)
            sent, token = grad_send(kind, spot, operands, (token,))
            ops[name] += (wide_swap(sent, CORE),)
            return token

        def keep(name, order, token):
            kind, operands, got = ops[name]
            found, token = grad_keep(kind, spot, operands, got, order, (token,))
            axes = Box(x=(ACROSS,), y=(ALONG,), both=(ACROSS, ALONG))[order]
            for at, axis in enumerate(axes):
                found["got%d" % at] = wide_swap(found["send%d" % at], axis)
            found.axes = axes
            group[name] = found
            return token

        def forward(names, token):
            sent, token = grad_pass([group[name] for name in names], (token,))
            for name in names:
                for at in halves_of(group[name]):
                    axis = ACROSS + ALONG - group[name].axes[at]
                    group[name]["come%d" % at] = wide_swap(sent.pop(0), axis)
            return token

        def near(names, token):
            found, token = grad_near([group[name] for name in names], (token,))
            return (found.stay, narrow_swap(found.near, NEAR)), token

        def far(kinds, pair, token):
            found, token = grad_far(kinds, *pair, (token,))
            return (found.own, narrow_swap(found.far, FAR)), token

        def gather(kinds, names, token, *after):
            for name in names:
                group[name].spot = spot
            groups = [group[name] for name in names]
            blocks, token = grad_collect(kinds, groups, (token, *after))
            mine = lax.psum_scatter(blocks, "narrow", scatter_dimension=0, tiled=True)
            return (mine.reshape(mine.shape[1:]),), token

        token = send("o1", "out", (one.gb2t, one.hid), token)
        back1, token = layer_back(
            1, spot, one, one, "v", weights, vecs, cs, Box(), (token,), hid_got
        )
        later1 = travel(back1.state, -1)
        token = send("i1", "inner", (one.midt, back1.gpre), token)
        token = keep("o1", "y", token)
        token = keep("i1", "x", token)
        mix1, token = mix_back(
            1, later1, spot, back1, one, cs, cm, wq_cuts[1], zero, weight_fetch(0), (token,)
        )
        token = send("m1", "mix", (one.mixt, one.xt, mix1.gcol), token)
        token = forward(["o1"], token)
        token = forward(["i1"], token)
        gb2t_got = wide_swap(mix1.gb2t, ALONG)
        fetch = Box(
            hid=("f", zero.hid) + half_of(rows, True),
            hid_got=("f", hid_got, [lambda ref: ref.at[0]], (rows, FF // 2)),
            midt=("f", zero.midt, [whole_cut], (D, rows)),
        )
        weights = mix1
        back0, token = layer_back(0, spot, mix1, zero, "d", weights, vecs, cs, fetch, (token,))
        later0 = [move(back0.state, -1)]
        token = keep("m1", "both", token)
        pair = (mix1.gb2t, gb2t_got, back0.hid, back0.hid_got)
        token = send("o0", "pair", pair, token)
        both, token = add_up(back0.state, later0[0], (token,))
        later0.append(move(both, -2))
        token = send("i0", "inner", (back0.midt.reshape(D, rows), back0.gpre), token)
        token = forward(["m1"], token)
        token = keep("o0", "x", token)
        token = keep("i0", "both", token)
        f1, token = gather(["out", "inner"], ["o1", "i1"], token, later0[1])
        mix0, token = mix_back(
            0, later0, spot, back0, zero, cs, cm, wq_cuts[0], None, Box(), (token,)
        )
        input_grad = mix0.grad
        parts = (mix1.sums_a, back0.sums_b, mix0.sums_c, one.sums_a, back1.sums_b, mix1.sums_c)
        token = send("m0", "mix", (zero.mixt, zero.xt, mix0.gcol), token)
        token = forward(["i0"], token)
        token = keep("m0", "both", token)
        near_f0, token = near(["o0", "i0"], token)
        sums, token = collect_sums(parts, (token,))
        come = wide_swap(sums, CORE)
        mg1, token = gather(["mix"], ["m1"], token)
        sums, token = add_up(sums, come, (token,))
        come = wide_swap(sums, ACROSS)
        token = forward(["m0"], token)
        sums, token = add_up(sums, come, (token,))
        come = wide_swap(sums, ALONG)
        far_f0, token = far(["out", "inner both"], near_f0, token)
        sums, token = add_up(sums, come, (token,))
        come = narrow_swap(sums, NEAR)
        near_m0, token = near(["m0"], token)
        sums, token = add_up(sums, come, (token,))
        come = narrow_swap(sums, FAR)
        far_m0, token = far(["mix"], near_m0, token)
        ffn_grads, token = grad_last("ffn", [far_f0, f1], (token,))
        sums, token = add_up(sums, come, (token,))
        mix_grads, token = grad_last("mix", [far_m0, mg1], (token,))
        sums = sums[:26].reshape(LAYERS, 13, D)
        grad_qkv, grad_o = mix_grads.first, mix_grads.second
        grad_in, grad_out = ffn_grads.first, ffn_grads.second

    def columns(v):
        width = v.shape[-1] // narrow
        return lax.dynamic_slice_in_dim(v, narrow_at * width, width, axis=v.ndim - 1)

    return (
        output,
        input_grad,
        grad_qkv,
        grad_o,
        grad_in,
        grad_out,
        columns(sums[:, 10:13].reshape(LAYERS, 3 * D)),
        columns(sums[:, 3:7].reshape(LAYERS, FF)),
        columns(jnp.stack([sums[:, 7], sums[:, 0], sums[:, 8], sums[:, 1]], axis=1)),
        columns(jnp.stack([sums[:, 9], sums[:, 2]], axis=1)),
    )


def solution(mesh):
    rows = P(("wide", "narrow"), None)
    placed = (rows, rows, P("wide")) + (P(),) * 8
    return jax.shard_map(
        shards,
        mesh=mesh,
        in_specs=placed,
        out_specs=(rows, rows)
        + (P(None, "wide", "narrow"),) * 4
        + (P(None, "narrow"),) * 2
        + (P(None, None, "narrow"),) * 2,
        check_vma=False,
    )
```

```python
import math

import jax
import jax.numpy as jnp
from jax import lax
from jax.experimental import pallas as pl
from jax.experimental.pallas import tpu as pltpu
from jax.sharding import PartitionSpec as P

D = 768
HEADS = 12
HEAD_DIM = 64
FF = 3072
LAYERS = 2
PAIRS = HEADS // 2
NORM_EPS = 1e-05
LANES = 128
STATE_ROWS = PAIRS * LANES + 16

BF = jnp.bfloat16
F32 = jnp.float32


def nn(a, b):
    return lax.dot_general(a, b, (((1,), (0,)), ((), ())), preferred_element_type=F32)


def nt(a, b):
    return lax.dot_general(a, b, (((1,), (1,)), ((), ())), preferred_element_type=F32)


def tn(a, b):
    return lax.dot_general(a, b, (((0,), (0,)), ((), ())), preferred_element_type=F32)


def low(v):
    return v.astype(BF)


def up(v):
    return v.astype(F32)


def beside(a, b):
    return jnp.concatenate([a, b], axis=1)


def above(a, b):
    return jnp.concatenate([a, b], axis=0)


def softplus(u):
    return jnp.maximum(u, 0.0) + jnp.log1p(jnp.exp(-jnp.abs(u)))


def sigmoid(u):
    return 1.0 / (1.0 + jnp.exp(-u))


def swap(v):
    return pltpu.roll(v, HEAD_DIM, 1)


def lane_of(rows):
    return lax.broadcasted_iota(jnp.int32, (rows, LANES), 1)


def row_mean(v):
    return jnp.mean(v, axis=-1, keepdims=True)


def norm_apply(total, gain, shift):
    centred = total - row_mean(total)
    scale = lax.rsqrt(row_mean(centred * centred) + NORM_EPS)
    normal = centred * scale
    return normal * gain + shift, normal, scale


def norm_back(upstream, normal, scale, gain):
    grad = upstream * gain
    return scale * (grad - row_mean(grad) - normal * row_mean(grad * normal))


def column_sum(v):
    return jnp.sum(v, axis=0, keepdims=True)


def shape(*dims, dtype=F32):
    return jax.ShapeDtypeStruct(dims, dtype)


class Box(dict):
    __getattr__ = dict.__getitem__
    __setattr__ = dict.__setitem__


class Refs:
    def __init__(self):
        self.refs = Box()
        self.copies = Box()
        self.flushes = Box()

    def __getitem__(self, name):
        for copy in self.copies.pop(name, []):
            if copy is not None:
                copy.wait()
        return self.refs[name]

    def __getattr__(self, name):
        return self[name]

    def part(self, name, at):
        copies = self.copies.get(name)
        if copies and copies[at] is not None:
            copies[at].wait()
            copies[at] = None
        return self.refs[name].at[at]

    def done(self, name):
        if name in self.flushes:
            self.flushes[name].start()


def in_hbm(array):
    return pltpu.with_memory_space_constraint(array, pltpu.HBM)


def in_vmem(array):
    return pltpu.with_memory_space_constraint(array, pltpu.VMEM)


def whole_cut(ref):
    return ref


def run(body, ins, outs, deps=(), scratch=None, limit=20, flops=0, nbytes=0):
    scratch = scratch or Box()
    in_names = list(ins)
    out_names = list(outs)
    operands, in_specs, out_shapes, out_specs, scratch_shapes = [], [], [], [], []
    vmem = pl.BlockSpec(memory_space=pltpu.VMEM)
    hbm = pl.BlockSpec(memory_space=pltpu.HBM)
    smem = pl.BlockSpec(memory_space=pltpu.SMEM)
    for name in in_names:
        mode, array = ins[name][:2]
        operands.append(Box(d=in_hbm, r=in_hbm, v=in_vmem).get(mode, whole_cut)(array))
        in_specs.append(Box(v=vmem, s=smem, d=hbm, r=hbm)[mode])
    fetch_names = [name for name in out_names if outs[name][0] == "f"]
    for name in fetch_names:
        operands.append(in_hbm(outs[name][1]))
        in_specs.append(hbm)
    for dep in deps:
        operands.append(in_vmem(dep))
        in_specs.append(vmem)
    copy_count = 0
    plan = []
    for name in in_names:
        if ins[name][0] == "d":
            array = ins[name][1]
            cuts, block = ins[name][2] if len(ins[name]) > 2 else (None, array.shape)
            scratch_shapes.append(
                pltpu.VMEM(block if cuts is None else (len(cuts),) + block, array.dtype)
            )
            plan.append((name, cuts))
            copy_count += 1 if cuts is None else len(cuts)
    for name in out_names:
        mode = outs[name][0]
        if mode == "f":
            array, cuts, block = outs[name][1:4]
            out_shapes.append(pltpu.VMEM((len(cuts),) + block, array.dtype))
            copy_count += len(cuts)
        else:
            given = outs[name][1]
            space = pltpu.HBM if mode == "h" else pltpu.VMEM
            out_shapes.append(space(given.shape, given.dtype))
            if mode == "h":
                scratch_shapes.append(pltpu.VMEM(outs[name][1].shape, outs[name][1].dtype))
                copy_count += 1
        out_specs.append(hbm if mode == "h" else vmem)
    out_shapes.append(pltpu.VMEM((8, LANES), F32))
    out_specs.append(vmem)
    for spec in scratch.values():
        scratch_shapes.append(spec)
    scratch_shapes.append(pltpu.SemaphoreType.DMA((max(copy_count, 1),)))

    def kernel(*refs):
        refs = list(refs)
        sems = refs.pop()
        used = [0]

        def make(source, target):
            copy = pltpu.make_async_copy(source, target, sems.at[used[0]])
            used[0] += 1
            return copy

        n_in, n_fetch, n_out = len(in_names), len(fetch_names), len(out_names)
        in_refs = dict(zip(in_names, refs[:n_in]))
        fetch_refs = dict(zip(fetch_names, refs[n_in : n_in + n_fetch]))
        rest = refs[n_in + n_fetch + len(deps) :]
        out_refs = dict(zip(out_names, rest[:n_out]))
        token = rest[n_out]
        spare = rest[n_out + 1 :]
        io = Refs()
        for name in in_names:
            io.refs[name] = in_refs[name]
        for name, cuts in plan:
            buffer = spare.pop(0)
            io.refs[name] = buffer
            if cuts is None:
                io.copies[name] = [make(in_refs[name], buffer)]
            else:
                io.copies[name] = [
                    make(cut(in_refs[name]), buffer.at[at]) for at, cut in enumerate(cuts)
                ]
            for copy in io.copies[name]:
                copy.start()
        fetches = []
        for name in out_names:
            mode = outs[name][0]
            if mode == "f":
                for at, cut in enumerate(outs[name][2]):
                    source = fetch_refs[name]
                    source = cut(source, io) if len(outs[name]) > 4 else cut(source)
                    fetches.append(make(source, out_refs[name].at[at]))
                io.refs[name] = out_refs[name]
            elif mode == "h":
                buffer = spare.pop(0)
                io.refs[name] = buffer
                io.flushes[name] = make(buffer, out_refs[name])
            else:
                io.refs[name] = out_refs[name]
        for name in scratch:
            io.refs[name] = spare.pop(0)
        for copy in fetches:
            copy.start()
        token[...] = jnp.zeros(token.shape, F32)
        body(io)
        for name in list(io.copies):
            io[name]
        for copy in fetches:
            copy.wait()
        for copy in io.flushes.values():
            copy.wait()

    cost = COSTS[min(Counter.at, len(COSTS) - 1)]
    Counter.at += 1
    results = pl.pallas_call(
        kernel,
        out_shape=tuple(out_shapes),
        in_specs=in_specs,
        out_specs=tuple(out_specs),
        scratch_shapes=scratch_shapes,
        compiler_params=pltpu.CompilerParams(vmem_limit_bytes=limit * 1024 * 1024),
        cost_estimate=pl.CostEstimate(
            flops=int(cost * 10**9), bytes_accessed=10**8, transcendentals=0
        ),
    )(*operands)
    return Box(zip(out_names, results)), results[-1]


def columns_of(layer, parts):
    return [lambda ref, j=j: ref.at[layer, :, pl.ds(D * j, D)] for j in range(parts)], (D, D)


def rows_of(layer, parts):
    return [lambda ref, j=j: ref.at[layer, pl.ds(D * j, D), :] for j in range(parts)], (D, D)


def half_of(rows, own):
    def cut(ref, io):
        along = io.spot[1] if own else 1 - io.spot[1]
        return ref.at[:, pl.ds(pl.multiple_of(along * (FF // 2), LANES), FF // 2)]

    return [cut], (rows, FF // 2), True


def layer_of(layer, block):
    return [lambda ref: ref.at[layer]], block


COSTS = [10, 10, 10, 10, 10, 10, 0.3, 0.3, 0.3, 1, 0.3, 0.3, 0.3, 0.3, 0.3, 15, 1, 0.3, 1, 3, 0.3, 10, 15, 1, 6, 0.3, 0.3, 22, 10, 3, 1, 3, 1, 0.3, 0.3, 6, 3, 0.3, 0.3, 0.3, 0.3, 1]


class Counter:
    at = 0


def project(layer, spot, x, x_mode, wq, vecs, cs, fetches, deps):
    rows = x.shape[0]

    def body(io):
        x_in = up(io.x[...])
        xb = low(x_in)
        io.xt[...] = low(x_in.T)
        io.done("xt")
        lane = lane_of(rows)
        lo = lane < HEAD_DIM
        lane_state = lane_of(LANES)
        lo_state = lane_state < HEAD_DIM
        totals = jnp.zeros((LANES, LANES), F32)
        for j in range(3):
            w = io.part("wq", j)
            bias = vector(io, "qkv_bias", layer)[:, D * j : D * (j + 1)]
            pk = low(nn(xb, w[...]) + bias)
            io.packed[:, D * j : D * (j + 1)] = pk
            io.kept[:, D * j : D * (j + 1)] = pk
            pf = up(pk)
            cs_now = io.cs[...]
            for p in range(2):
                t0, t1, t2 = (
                    pf[:, (3 * p + i) * LANES : (3 * p + i + 1) * LANES] for i in range(3)
                )
                sp0 = softplus(t0)
                sp2 = softplus(t2)
                kf0 = low(jnp.where(lo, swap(sp0), sp0) * cs_now)
                kf1 = low(jnp.where(lo, sp2, swap(sp2)) * cs_now)
                s0 = tn(kf0, low(jnp.where(lo, t1, 1.0)))
                s1 = tn(kf1, low(jnp.where(lo, 1.0, t2)))
                pair = 2 * j + p
                io.state[pair * LANES : (pair + 1) * LANES, :] = low(
                    jnp.where(lo_state, s0, s1)
                )
                totals = jnp.where(lane_state == 2 * pair, swap(s0), totals)
                totals = jnp.where(lane_state == 2 * pair + 1, s1, totals)
        io.state[PAIRS * LANES :, :] = low(totals.T[:16])
        io.done("kept")

    outs = Box(
        packed=("v", shape(rows, 3 * D, dtype=BF)),
        xt=("h", shape(D, rows, dtype=BF)),
        state=("v", shape(STATE_ROWS, LANES, dtype=BF)),
    )
    outs.kept = ("h", shape(rows, 3 * D, dtype=BF))
    outs.update(fetches)
    return run(
        body,
        Box(spot=("s", spot), x=(x_mode, x), wq=wq, cs=("d", cs), **vecs),
        outs,
        deps,
        flops=2 * rows * D * 3 * D,
        nbytes=2 * D * 3 * D,
    )


def inside(spot, packed, cm, long, fetches, deps):
    rows = packed.shape[0]

    def body(io):
        lo = lane_of(rows) < HEAD_DIM
        for pair in range(PAIRS):
            at = pair * 3 * LANES
            t0, t1, t2 = (
                up(io.packed[:, at + i * LANES : at + (i + 1) * LANES]) for i in range(3)
            )
            sp0, sp1, sp2 = softplus(t0), softplus(t1), softplus(t2)
            a0 = nt(low(jnp.where(lo, sp0, 0.0)), low(swap(sp0)))
            a1 = nt(low(jnp.where(lo, 0.0, sp1)), low(swap(sp2)))
            mask = io.cm[...]
            n0 = nn(low(a0 * mask), low(jnp.where(lo, t1, 1.0)))
            n1 = nn(low(a1 * mask), low(jnp.where(lo, 1.0, t2)))
            here = slice(pair * LANES, (pair + 1) * LANES)
            io.num[:, here] = jnp.where(lo, n0, n1)
            io.den[:, here] = swap(jnp.where(lo, n1, n0))
            sq = low(jnp.where(lo, sp0, sp1))
            io.sq[:, here] = sq
            if long:
                io.sq_kept[:, here] = sq

    outs = Box(
        num=("v", shape(rows, D)),
        den=("v", shape(rows, D)),
        sq=("v", shape(rows, D, dtype=BF)),
    )
    if long:
        outs.sq_kept = ("h", shape(rows, D, dtype=BF))

    def body_all(io):
        body(io)
        if long:
            io.done("sq_kept")

    outs.update(fetches)
    return run(
        body_all,
        Box(spot=("s", spot), packed=("v", packed), cm=("d", cm)),
        outs,
        deps,
        flops=4 * HEADS * rows * rows * LANES,
        nbytes=rows * D * 16,
    )


def sum_states(io, count):
    total = up(io.recv0[...])
    for at in range(1, count):
        total = total + up(io["recv%d" % at][...])
    return total


def vector(io, name, layer):
    return up(io[name][...])[layer : layer + 1]


def state_totals(total):
    return jnp.concatenate(
        [total[PAIRS * LANES :], jnp.zeros((LANES - 16, LANES), F32)], axis=0
    ).T


def totals_column(totals, head):
    return jnp.broadcast_to(totals[:, head : head + 1], (LANES, LANES))


def diagonal(a, b):
    zero = jnp.zeros((LANES, LANES), BF)
    return above(beside(a, zero), beside(zero, b))


def second_norm_back(io, gs, n2, r2, gain):
    gz2 = norm_back(gs, n2, r2, gain)
    gb2 = low(gz2)
    io.gz2[...] = gz2
    io.gb2[...] = gb2
    io.gb2t[...] = low(gz2.T)
    io.sums_a[...] = jnp.zeros((8, D), F32)
    io.sums_a[0:1, :] = column_sum(up(gb2))
    io.sums_a[1:2, :] = column_sum(gs)
    io.sums_a[2:3, :] = column_sum(gs * n2)
    io.done("sums_a")


def second_norm_outs(rows):
    return Box(
        gz2=("v", shape(rows, D)),
        gb2=("v", shape(rows, D, dtype=BF)),
        gb2t=("v", shape(D, rows, dtype=BF)),
        sums_a=("h", shape(8, D)),
    )


def layer_forward(layer, recv, x, x_mode, inner, weights, vecs, cs, cotangent, deps):
    rows = x.shape[0]
    last = cotangent is not None

    def body(io):
        lane = lane_of(rows)
        lo = lane < HEAD_DIM
        lo_state = lane_of(LANES) < HEAD_DIM
        before = sum_states(io, len(recv))
        io.before[...] = low(before)
        io.done("before")
        totals = state_totals(before)
        for pair in range(PAIRS):
            here = slice(pair * LANES, (pair + 1) * LANES)
            sq = up(io.sq[:, here])
            other = swap(sq)
            state = before[here]
            cs_now = io.cs[...]
            feats = beside(
                low(jnp.where(lo, sq, other) * cs_now), low(jnp.where(lo, other, sq) * cs_now)
            )
            both = nn(
                feats,
                diagonal(
                    low(jnp.where(lo_state, state, totals_column(totals, 2 * pair))),
                    low(jnp.where(lo_state, totals_column(totals, 2 * pair + 1), state)),
                ),
            )
            n0 = both[:, :LANES]
            n1 = both[:, LANES:]
            num = io.num[:, here] + jnp.where(lo, n0, n1)
            inv = 1.0 / (io.den[:, here] + swap(jnp.where(lo, n1, n0)))
            mixed = num * inv
            io.inv[:, here] = inv
            io.mixed[:, here] = low(mixed)
            io.mixt[here, :] = low(mixed.T)
        io.done("inv")
        io.done("mixed")
        io.done("mixt")
        shifts = up(io.shifts[layer])
        gains = up(io.gains[layer])
        bias = vector(io, "ffn_bias", layer)
        branch = nn(io.mixed[...], io.part("wo", 0)[...]) + shifts[0:1]
        middle, n1, r1 = norm_apply(up(io.x[...]) + branch, gains[0:1], shifts[2:3])
        io.n1[...] = n1
        io.done("n1")
        io.r1[...] = jnp.broadcast_to(r1, (rows, LANES))
        io.done("r1")
        io.midt[...] = low(middle.T)
        io.done("midt")
        mid = low(middle)
        total = middle + shifts[1:2]
        for j in range(FF // D):
            here = slice(D * j, D * (j + 1))
            pre = nn(mid, io.part("w1", j)[...]) + bias[:, here]
            cdf = 0.5 * (1.0 + lax.erf(pre * (1.0 / math.sqrt(2.0))))
            hid = low(pre * cdf)
            io.hid[:, here] = hid
            io.slope[:, here] = low(
                cdf + pre * jnp.exp(-0.5 * pre * pre) * (1.0 / math.sqrt(2.0 * math.pi))
            )
            total = total + nn(hid, io.part("w2", j)[...])
        io.done("hid")
        io.done("slope")
        s_next, n2, r2 = norm_apply(total, gains[1:2], shifts[3:4])
        if last:
            io.output[...] = low(s_next)
            io.done("output")
            second_norm_back(io, up(io.cot[...]), n2, r2, gains[1:2])
        else:
            io.s_next[...] = s_next
            io.n2[...] = n2
            io.done("n2")
            io.r2[...] = jnp.broadcast_to(r2, (rows, LANES))
            io.done("r2")

    ins = Box({"recv%d" % i: ("v", recv[i]) for i in range(len(recv))})
    ins.update(
        Box(
            x=(x_mode, x),
            num=("v", inner.num),
            den=("v", inner.den),
            sq=("v", inner.sq),
            wo=("v", weights.wo),
            w1=("v", weights.w1),
            w2=("v", weights.w2),
            cs=("d", cs),
            **vecs,
        )
    )
    if last:
        ins.cot = ("d", cotangent)
    mode = "v" if last else "h"
    outs = Box(
        before=("h", shape(STATE_ROWS, LANES, dtype=BF)),
        mixed=(mode, shape(rows, D, dtype=BF)),
        mixt=("h", shape(D, rows, dtype=BF)),
        inv=(mode, shape(rows, D)),
        n1=(mode, shape(rows, D)),
        r1=(mode, shape(rows, LANES)),
        midt=(mode, shape(D, rows, dtype=BF)),
        hid=(mode, shape(rows, FF, dtype=BF)),
        slope=(mode, shape(rows, FF, dtype=BF)),
    )
    if last:
        outs.output = ("h", shape(rows, D, dtype=BF))
        outs.update(second_norm_outs(rows))
    else:
        outs.s_next = ("v", shape(rows, D))
        outs.n2 = ("h", shape(rows, D))
        outs.r2 = ("h", shape(rows, LANES))
    return run(
        body,
        ins,
        outs,
        deps,
        limit=20,
        flops=2 * rows * D * (D + 2 * FF),
        nbytes=2 * D * (D + 2 * FF),
    )


def layer_back(layer, spot, top, kept, mode, weights, vecs, cs, fetches, deps, after=None):
    rows = top.gz2.shape[0]

    def body(io):
        lane = lane_of(rows)
        lo = lane < HEAD_DIM
        lane_state = lane_of(LANES)
        lo_state = lane_state < HEAD_DIM
        left_rows = lax.broadcasted_iota(jnp.int32, (LANES, LANES), 0) < HEAD_DIM
        same = low(jnp.where(lo_state == left_rows, 1.0, 0.0))
        gb2 = io.gb2[...]
        gmid = io.gz2[...]
        sums = io.sums_b
        sums[...] = jnp.zeros((8, D), F32)
        for j in range(FF // D):
            here = slice(D * j, D * (j + 1))
            gpre = low(nt(gb2, io.part("w2", j)[...]) * up(io.slope[:, here]))
            io.gpre[:, here] = gpre
            sums[j : j + 1, :] = column_sum(up(gpre))
            gmid = gmid + nt(gpre, io.part("w1", j)[...])
        n1 = io.n1[...]
        gz1 = norm_back(gmid, n1, io.r1[:, :1], up(io.gains[layer])[0:1])
        gb1 = low(gz1)
        io.gz1[...] = gz1
        io.gb1[...] = gb1
        sums[4:5, :] = column_sum(up(gb1))
        sums[5:6, :] = column_sum(gmid)
        sums[6:7, :] = column_sum(gmid * n1)
        io.done("sums_b")
        gmixed = up(low(nt(gb1, io.part("wo", 0)[...])))
        totals = jnp.zeros((LANES, LANES), F32)
        for pair in range(PAIRS):
            here = slice(pair * LANES, (pair + 1) * LANES)
            u = gmixed[:, here] * io.inv[:, here]
            dd = -nn(low(u * up(io.mixed[:, here])), same)
            io.u[:, here] = low(u)
            io.dd[:, here] = low(dd)
            ds = swap(dd)
            sq = up(io.sq[:, here])
            other = swap(sq)
            cs_now = io.cs[...]
            s0 = tn(low(jnp.where(lo, sq, other) * cs_now), low(jnp.where(lo, u, ds)))
            s1 = tn(low(jnp.where(lo, other, sq) * cs_now), low(jnp.where(lo, ds, u)))
            io.state[here, :] = low(jnp.where(lo_state, s0, s1))
            totals = jnp.where(lane_state == 2 * pair, swap(s0), totals)
            totals = jnp.where(lane_state == 2 * pair + 1, s1, totals)
        io.state[PAIRS * LANES :, :] = low(totals.T[:16])

    ins = Box(
        gz2=("v", top.gz2),
        gb2=("v", top.gb2),
        wo=("v", weights.wo),
        w1=("v", weights.w1),
        w2=("v", weights.w2),
    )
    for name in ("slope", "n1", "r1", "inv", "mixed", "sq"):
        ins[name] = (mode, kept[name])
    if after is not None:
        ins.after = ("r", after)
    ins.spot = ("s", spot)
    ins.gains = vecs.gains
    ins.cs = ("d", cs)
    outs = Box(
        gpre=("v", shape(rows, FF, dtype=BF)),
        gb1=("v", shape(rows, D, dtype=BF)),
        gz1=("v", shape(rows, D)),
        u=("v", shape(rows, D, dtype=BF)),
        dd=("v", shape(rows, D, dtype=BF)),
        state=("v", shape(STATE_ROWS, LANES, dtype=BF)),
        sums_b=("h", shape(8, D)),
    )
    outs.update(fetches)
    return run(
        body,
        ins,
        outs,
        deps,
        limit=20,
        flops=2 * rows * D * (D + 2 * FF),
        nbytes=2 * D * (D + 2 * FF),
    )


def mix_back(layer, recv, spot, low_part, kept, cs, cm, wq, below, fetches, deps):
    rows = low_part.u.shape[0]

    def body(io):
        lane = lane_of(rows)
        lo = lane < HEAD_DIM
        lane_state = lane_of(LANES)
        lo_state = lane_state < HEAD_DIM
        one_left = jnp.where(lane == 0, 1.0, 0.0)
        one_right = jnp.where(lane == HEAD_DIM, 1.0, 0.0)
        later = sum_states(io, len(recv))
        later_totals = state_totals(later)
        before = up(io.before[...])
        before_totals = state_totals(before)

        def halves(state, totals, pair):
            first = jnp.where(
                lo_state,
                state,
                jnp.where(lane_state == HEAD_DIM, totals_column(totals, 2 * pair), 0.0),
            )
            second = jnp.where(
                lo_state,
                jnp.where(lane_state == 0, totals_column(totals, 2 * pair + 1), 0.0),
                state,
            )
            return diagonal(low(first), low(second))

        def fold(v, cs_now):
            first = v[:, :LANES] * cs_now
            second = v[:, LANES:] * cs_now
            return jnp.where(lo, first + swap(first), second + swap(second))

        io.cmt[...] = io.cm[...].T
        for pair in range(PAIRS):
            here = slice(pair * LANES, (pair + 1) * LANES)
            at = pair * 3 * LANES
            t0, t1, t2 = (
                up(io.packed[:, at + i * LANES : at + (i + 1) * LANES]) for i in range(3)
            )
            cs_now = io.cs[...]
            mask = io.cm[...]
            sp0, sp1, sp2 = softplus(t0), softplus(t1), softplus(t2)
            sw0 = swap(sp0)
            sw2 = swap(sp2)
            q0 = low(jnp.where(lo, sp0, 0.0))
            k0 = low(jnp.where(lo, sw0, 0.0))
            q1 = low(jnp.where(lo, 0.0, sp1))
            k1 = low(jnp.where(lo, 0.0, sw2))
            kf = beside(
                low(jnp.where(lo, sw0, sp0) * cs_now), low(jnp.where(lo, sp2, sw2) * cs_now)
            )
            v0 = low(jnp.where(lo, t1, one_right))
            v1 = low(jnp.where(lo, one_left, t2))
            uf = up(io.u[:, here])
            ds = swap(up(io.dd[:, here]))
            u0 = low(jnp.where(lo, uf, ds))
            u1 = low(jnp.where(lo, ds, uf))
            ua = low(jnp.where(lo, uf, 0.0))
            ub = low(jnp.where(lo, 0.0, uf))
            mask_t = io.cmt[...]
            pt = beside(low(nt(k0, q0) * mask_t), low(nt(k1, q1) * mask_t))
            d = beside(low(nt(u0, v0) * mask), low(nt(u1, v1) * mask))
            dt = beside(low(nt(v0, u0) * mask_t), low(nt(v1, u1) * mask_t))
            after = later[here]
            eq = nt(beside(u0, u1), halves(before[here], before_totals, pair))
            ek = nt(beside(v0, v1), halves(after, later_totals, pair))
            after_split = above(
                low(jnp.where(lo_state, after, 0.0)), low(jnp.where(lo_state, 0.0, after))
            )
            dq = fold(eq, cs_now) + nn(d, above(k0, k1))
            dk = fold(ek, cs_now) + nn(dt, above(q0, q1))
            dv = nn(beside(kf, pt), jnp.concatenate([after_split, ua, ub], axis=0))
            dks = swap(dk)
            gpk = io.gpk
            gpk[:, at : at + LANES] = low(jnp.where(lo, dq, dks) * sigmoid(t0))
            gpk[:, at + LANES : at + 2 * LANES] = low(jnp.where(lo, dv, dq * sigmoid(t1)))
            gpk[:, at + 2 * LANES : at + 3 * LANES] = low(jnp.where(lo, dks * sigmoid(t2), dv))
        grad = io.gz1[...]
        io.sums_c[...] = jnp.zeros((8, D), F32)
        for j in range(3):
            gpk = io.gpk[:, D * j : D * (j + 1)]
            io.sums_c[j : j + 1, :] = column_sum(up(gpk))
            grad = grad + nt(gpk, io.part("wq", j)[...])
        io.done("sums_c")
        if below is None:
            io.grad[...] = grad
            io.done("grad")
        else:
            gain = up(io.gains[layer - 1])[1:2]
            second_norm_back(io, grad, io.n2[...], io.r2[:, :1], gain)
        near = io.spot[3]
        far = io.spot[4]
        gpk = up(io.gpk[...])
        gb1 = up(io.gb1[...])
        for low_bit in range(2):
            slot = low_bit ^ near
            for source, start in ((gb1, 0), (gpk, D // 2)):
                width = source.shape[1] // 4
                first = source[:, low_bit * width : (low_bit + 1) * width]
                second = source[:, (low_bit + 2) * width : (low_bit + 3) * width]
                both = beside(
                    jnp.where(far == 0, first, second), jnp.where(far == 0, second, first)
                )
                io.gcol[slot, :, start : start + 2 * width] = low(both)

    ins = Box({"recv%d" % i: ("v", recv[i]) for i in range(len(recv))})
    ins.update(
        Box(
            spot=("s", spot),
            u=("v", low_part.u),
            dd=("v", low_part.dd),
            gb1=("v", low_part.gb1),
            gz1=("v", low_part.gz1),
            packed=("d", kept.packed),
            cs=("d", cs),
            cm=("d", cm),
            before=("d", kept.before),
            wq=wq,
        )
    )
    outs = Box(
        gcol=("v", shape(2, rows, 2 * D, dtype=BF)),
        sums_c=("h", shape(8, D)),
    )
    if below is None:
        outs.grad = ("h", shape(rows, D))
    else:
        ins.n2 = ("d", below.n2)
        ins.r2 = ("d", below.r2)
        ins.gains = below.vecs.gains
        outs.update(second_norm_outs(rows))
    outs.update(fetches)
    return run(
        body,
        ins,
        outs,
        deps,
        scratch=Box(gpk=pltpu.VMEM((rows, 3 * D), BF), cmt=pltpu.VMEM((rows, rows), F32)),
        limit=20,
        flops=2 * rows * D * 3 * D + 12 * HEADS * rows * rows * LANES,
        nbytes=2 * D * 3 * D,
    )


def owners(spot, core):
    return [
        ((spot[1] ^ along) * 2 + (spot[2] ^ across)) * 2 + core
        for across in range(2)
        for along in range(2)
    ]


def out_terms(io, core, put):
    near, far = io.spot[3], io.spot[4]
    for at, block in enumerate(owners(io.spot, core)):
        lanes = pl.ds(pl.multiple_of(block * (FF // 8), LANES), FF // 8)
        io.rhs[:, at * (FF // 8) : (at + 1) * (FF // 8)] = io.hid[:, lanes]
    lhs = io.gb2t[...]
    for half in range(2):
        grad = nn(lhs, io.rhs[:, half * D : (half + 1) * D])
        for sub in range(2):
            at = 2 * half + sub
            for n in range(4):
                lanes = pl.ds(pl.multiple_of(((n // 2) ^ far) * (D // 2), LANES), D // 2)
                put(
                    at,
                    (n % 2) ^ near,
                    None,
                    lanes,
                    grad[n * 192 : (n + 1) * 192, sub * (D // 2) : (sub + 1) * (D // 2)],
                )


def pair_terms(io, core, put):
    near, far = io.spot[3], io.spot[4]
    tokens = io.hid.shape[1]
    width = FF // 8
    io.lhs[:, :tokens] = io.gb2t[...]
    io.lhs[:, tokens:] = io.gb2t_got[...]
    for across in range(2):
        block = (io.spot[2] ^ across) * 2 + core
        lanes = pl.ds(pl.multiple_of(block * width, LANES), width)
        io.rhs[:tokens, across * width : (across + 1) * width] = io.hid[0, :, lanes]
        io.rhs[tokens:, across * width : (across + 1) * width] = io.hid_got[0, :, lanes]
    grad = nn(io.lhs[...], io.rhs[...])
    for across in range(2):
        for n in range(4):
            lanes = pl.ds(pl.multiple_of(((n // 2) ^ far) * width, LANES), width)
            put(
                across,
                (n % 2) ^ near,
                None,
                lanes,
                grad[n * 192 : (n + 1) * 192, across * width : (across + 1) * width],
            )


def gather_rows(io, name, target, core):
    for at, block in enumerate(owners(io.spot, core)):
        io[target][at * 96 : (at + 1) * 96, :] = io[name][
            pl.ds(pl.multiple_of(block * 96, 16), 96), :
        ]


def in_terms(io, core, put):
    near, far = io.spot[3], io.spot[4]
    gather_rows(io, "midt", "lhs", core)
    for n in range(4):
        grad = nn(io.lhs[...], io.gpre[:, n * D : (n + 1) * D])
        for at in range(4):
            put(at, (n % 2) ^ near, (n // 2) ^ far, slice(None), grad[at * 96 : (at + 1) * 96])


def mix_terms(io, core, put):
    gather_rows(io, "mixt", "lhs", core)
    gather_rows(io, "xt", "lhs_two", core)
    for slot in range(2):
        for lhs, start, stop in (("lhs", 0, D // 2), ("lhs_two", D // 2, 2 * D)):
            grad = nn(io[lhs][...], io.gcol[slot, :, start:stop])
            for at in range(4):
                put(
                    at,
                    slot,
                    None,
                    slice(start, stop),
                    grad[at * 96 : (at + 1) * 96],
                )


def part_rows(part, count):
    if part is None:
        return slice(None)
    return pl.ds(pl.multiple_of(part * count, 16), count)


TERMS = Box(pair=pair_terms, out=out_terms, inner=in_terms, mix=mix_terms)


def grad_setup(kind, spot, operands):
    ins = Box(spot=("s", spot))
    if kind == "out":
        gb2t, hid = operands
        tokens = gb2t.shape[1]
        ins.gb2t = ("v", gb2t)
        ins.hid = ("v", hid)
        return ins, Box(rhs=pltpu.VMEM((tokens, FF // 2), BF)), (192, D), tokens
    if kind == "pair":
        for name, array in zip(("gb2t", "gb2t_got", "hid", "hid_got"), operands):
            ins[name] = ("v", array)
        tokens = 2 * operands[0].shape[1]
        both = Box(lhs=pltpu.VMEM((D, tokens), BF), rhs=pltpu.VMEM((tokens, D), BF))
        return ins, both, (192, D), tokens
    lhs = pltpu.VMEM((D // 2, operands[0].shape[1]), BF)
    if kind == "inner":
        midt, gpre = operands
        ins.midt = ("v", midt)
        ins.gpre = ("v", gpre)
        return ins, Box(lhs=lhs), (192, D), midt.shape[1]
    mixt, xt, gcol = operands
    ins.mixt = ("v", mixt)
    ins.xt = ("v", xt)
    ins.gcol = ("v", gcol)
    return ins, Box(lhs=lhs, lhs_two=lhs), (96, 2 * D), xt.shape[1]


def grad_send(kind, spot, operands, deps):
    ins, scratch, block, tokens = grad_setup(kind, spot, operands)

    def body(io):
        def put(at, slot, part, lanes, value):
            io.send[at, slot, part_rows(part, value.shape[0]), lanes] = low(value)

        TERMS[kind](io, 1 - io.spot[0], put)

    outs, token = run(
        body,
        ins,
        Box(send=("v", shape(2 if kind == "pair" else 4, 2, *block, dtype=BF))),
        deps,
        scratch=scratch,
        flops=2 * tokens * 8 * block[0] * block[1],
        nbytes=4 * 2 * 2 * block[0] * block[1],
    )
    return outs.send, token


def grad_keep(kind, spot, operands, got, order, deps):
    ins, scratch, block, tokens = grad_setup(kind, spot, operands)
    ins.got = ("v", got)
    rows_all = block[0]
    if order == "both":
        half = (rows_all // 2, block[1])
    else:
        half = block

    def body(io):
        def put(at, slot, part, lanes, value):
            count = value.shape[0]
            rows = part_rows(part, count)
            value = low(value + up(io.got[at, slot, rows, lanes]))
            across, along = at // 2, at % 2
            if kind == "pair":
                io["send0" if at else "keep0"][slot, rows, lanes] = value
            elif order == "x":
                io["send0" if across else "keep0"][along, slot, rows, lanes] = value
            elif order == "y":
                io["send0" if along else "keep0"][across, slot, rows, lanes] = value
            else:
                rows = part_rows(part, count // 2)
                first, second = value[: count // 2], value[count // 2 :]
                io["send0" if across else "keep0"][along, slot, rows, lanes] = first
                io["send1" if along else "keep1"][across, slot, rows, lanes] = second

        TERMS[kind](io, io.spot[0], put)

    names = ["send0", "keep0"] + (["send1", "keep1"] if order == "both" else [])
    return run(
        body,
        ins,
        {
            name: ("v", shape(*((2,) if kind == "pair" else (2, 2)), *half, dtype=BF))
            for name in names
        },
        deps,
        scratch=scratch,
        flops=2 * tokens * 8 * block[0] * block[1],
        nbytes=4 * 2 * 4 * block[0] * block[1],
    )


def grad_pass(groups, deps):
    pairs = [
        (group["keep%d" % at], group["got%d" % at]) for group in groups for at in halves_of(group)
    ]
    ins, outs = Box(), Box()
    for at, (keep, got) in enumerate(pairs):
        ins["keep%d" % at] = ("v", keep)
        ins["got%d" % at] = ("v", got)
        outs["next%d" % at] = ("v", shape(*keep.shape[1:], dtype=BF))

    def body(io):
        for at in range(len(pairs)):
            io["next%d" % at][...] = low(
                up(io["keep%d" % at][1]) + up(io["got%d" % at][1])
            )

    outs, token = run(body, ins, outs, deps)
    return [outs["next%d" % at] for at in range(len(pairs))], token


def halves_of(group):
    return [at for at in range(2) if "keep%d" % at in group]


def group_ins(groups):
    ins = Box()
    for which, group in enumerate(groups):
        for at in halves_of(group):
            for name in ("keep", "got", "come"):
                if "%s%d" % (name, at) in group:
                    ins["%s%d_%d" % (name, which, at)] = ("v", group["%s%d" % (name, at)])
    return ins


def group_sum(io, which, at, slot):
    if "come%d_%d" % (which, at) not in io.refs:
        return up(io["keep%d_%d" % (which, at)][slot]) + up(io["got%d_%d" % (which, at)][slot])
    return (
        up(io["keep%d_%d" % (which, at)][0, slot])
        + up(io["got%d_%d" % (which, at)][0, slot])
        + up(io["come%d_%d" % (which, at)][slot])
    )


def grad_near(groups, deps):
    ins = group_ins(groups)
    places = [(which, at) for which, group in enumerate(groups) for at in halves_of(group)]
    sizes = [groups[which]["keep%d" % at].shape[-2:] for which, at in places]
    total = sum(rows * lanes // D for rows, lanes in sizes)

    def body(io):
        start = 0
        for which, at in places:
            rows, lanes = groups[which]["keep%d" % at].shape[-2:]
            for slot, target in ((1, io.near), (0, io.stay)):
                value = low(group_sum(io, which, at, slot))
                for part in range(lanes // D):
                    here = slice(start + part * rows, start + (part + 1) * rows)
                    target[here, :] = value[:, part * D : (part + 1) * D]
            start += rows * lanes // D

    return run(
        body,
        ins,
        Box(
            near=("v", shape(total, D, dtype=BF)),
            stay=("v", shape(total, D, dtype=BF)),
        ),
        deps,
    )


def grad_collect(kinds, groups, deps):
    ins = group_ins(groups)
    ins.spot = ("s", groups[0].spot)

    def body(io):
        near, far = io.spot[3], io.spot[4]
        for which, kind in enumerate(kinds):
            for slot in range(2):
                full = [group_sum(io, which, at, slot) for at in halves_of(groups[which])]
                if kind == "mix":
                    both = full[0]
                    quarter = D // 4
                    parts = [
                        beside(both[:, :quarter], both[:, 2 * quarter : 5 * quarter]),
                        beside(both[:, quarter : 2 * quarter], both[:, 5 * quarter :]),
                    ]
                elif kind == "inner":
                    parts = [full[0][:96], full[0][96:]]
                else:
                    parts = [
                        beside(full[0][:96, : D // 2], full[0][96:, : D // 2]),
                        beside(full[0][:96, D // 2 :], full[0][96:, D // 2 :]),
                    ]
                for half in range(2):
                    owner = (slot ^ near) + 2 * (half ^ far)
                    io.blocks[owner, which * 96 : (which + 1) * 96, :] = low(parts[half])

    outs, token = run(
        body, ins, Box(blocks=("v", shape(4, 96 * len(kinds), D, dtype=BF))), deps
    )
    return outs.blocks, token


def grad_far(kinds, pairs, deps):
    count = len(kinds)
    ins = Box()
    for at, (stay, near) in enumerate(pairs):
        ins["stay%d" % at] = ("v", stay)
        ins["near%d" % at] = ("v", near)

    def body(io):
        sums = [
            up(io["stay%d" % at][...]) + up(io["near%d" % at][...]) for at in range(len(pairs))
        ]
        full = jnp.concatenate(sums, axis=0)
        for at, kind in enumerate(kinds):
            part = full[192 * at : 192 * (at + 1)]
            here = slice(96 * at, 96 * (at + 1))
            if kind in ("mix", "mix both"):
                if kind == "mix":
                    both = beside(part[:96], part[96:])
                else:
                    both = above(beside(part[:48], part[48:96]), beside(part[96:144], part[144:]))
                quarter = D // 4
                io.own[here, :] = beside(both[:, :quarter], both[:, 2 * quarter : 5 * quarter])
                io.far[here, :] = low(
                    beside(both[:, quarter : 2 * quarter], both[:, 5 * quarter : 8 * quarter])
                )
            elif kind == "out":
                io.own[here, :] = beside(part[:96, : D // 2], part[96:, : D // 2])
                io.far[here, :] = low(beside(part[:96, D // 2 :], part[96:, D // 2 :]))
            else:
                io.own[here, :] = above(part[:48], part[96:144])
                io.far[here, :] = low(above(part[48:96], part[144:]))

    return run(
        body,
        ins,
        Box(
            own=("v", shape(count * 96, D)),
            far=("v", shape(count * 96, D, dtype=BF)),
        ),
        deps,
    )


def grad_last(kind, terms, starts, deps):
    size = 96 if kind == "mix" else 192
    ins = Box()
    for layer in range(LAYERS):
        for at, term in enumerate(terms[layer]):
            ins["term%d_%d" % (layer, at)] = ("v", term)
    if kind == "mix":
        outs = Box(
            first=("h", shape(LAYERS, 96, 3 * D // 4)),
            second=("h", shape(LAYERS, 96, D // 4)),
        )
    else:
        outs = Box(
            first=("h", shape(LAYERS, 96, D)),
            second=("h", shape(LAYERS, FF // 8, D // 4)),
        )

    def body(io):
        for layer in range(LAYERS):
            here = slice(starts[layer], starts[layer] + size)
            full = up(io["term%d_0" % layer][here, :])
            for at in range(1, len(terms[layer])):
                full = full + up(io["term%d_%d" % (layer, at)][here, :])
            if kind == "mix":
                io.first[layer] = full[:, D // 4 :]
                io.second[layer] = full[:, : D // 4]
            else:
                io.first[layer] = full[:96]
                io.second[layer, :, :96] = full[96:, : D // 2].T
                io.second[layer, :, 96:] = full[96:, D // 2 :].T
        io.done("first")
        io.done("second")

    return run(body, ins, outs, deps)


def wide_swap(v, bit):
    size = lax.axis_size("wide")
    return lax.ppermute(v, "wide", [(i, i ^ bit) for i in range(size)])


def narrow_swap(v, bit):
    size = lax.axis_size("narrow")
    return lax.ppermute(v, "narrow", [(i, i ^ bit) for i in range(size)])


CORE, ACROSS, ALONG = 1, 2, 4
NEAR, FAR = 1, 2


def reduce_plain(left, right):
    term = low(tn(left, right))
    part = lax.psum_scatter(term, "narrow", scatter_dimension=1, tiled=True)
    return lax.psum_scatter(up(part), "wide", scatter_dimension=0, tiled=True)


def move(v, shift):
    size = lax.axis_size("narrow")
    pairs = [(i, i + shift) for i in range(size) if 0 <= i + shift < size]
    return lax.ppermute(v, "narrow", pairs)


def travel(state, step):
    return [move(state, step * shift) for shift in range(1, lax.axis_size("narrow"))]


SUM_ROWS = (3, 7, 3)


def collect_sums(parts, deps):
    def body(io):
        io.sums[...] = jnp.zeros((32, D), F32)
        start = 0
        for at in range(len(parts)):
            rows = SUM_ROWS[at % 3]
            io.sums[start : start + rows, :] = io["part%d" % at][:rows, :]
            start += rows

    outs, token = run(
        body,
        Box({"part%d" % at: ("d", part) for at, part in enumerate(parts)}),
        Box(sums=("v", shape(32, D))),
        deps,
    )
    return outs.sums, token


def add_up(a, b, deps):
    def body(io):
        io.sum[...] = (up(io.a[...]) + up(io.b[...])).astype(a.dtype)

    outs, token = run(
        body,
        Box(a=("v", a), b=("v", b)),
        Box(sum=("v", shape(*a.shape, dtype=a.dtype))),
        deps,
    )
    return outs.sum, token


def shards(
    tokens,
    cotangent,
    horizons,
    qkv_weight,
    out_weight,
    ffn_in_weight,
    ffn_out_weight,
    qkv_bias,
    ffn_in_bias,
    model_biases,
    norm_gains,
):
    Counter.at = 0
    rows = tokens.shape[0]
    wide = lax.axis_size("wide")
    narrow = lax.axis_size("narrow")
    wide_at = lax.axis_index("wide")
    narrow_at = lax.axis_index("narrow")
    fast = wide == 8 and narrow == 4
    place = [wide_at % 2, (wide_at // 4) % 2, (wide_at // 2) % 2, narrow_at % 2, narrow_at // 2]
    if not fast:
        place = [wide_at * 0] * 5
    place.append(narrow_at)
    spot = jnp.stack(place).astype(jnp.int32)
    step = 0.5 * math.pi / up(horizons[0])
    places = up(narrow_at * rows + jnp.arange(rows)) * step
    cs = beside(
        jnp.broadcast_to(jnp.cos(places)[:, None], (rows, HEAD_DIM)),
        jnp.broadcast_to(jnp.sin(places)[:, None], (rows, HEAD_DIM)),
    )

    def mask(step):
        apart = jnp.arange(rows)[:, None] - jnp.arange(rows)[None, :]
        return jnp.where(apart >= 0, jnp.cos(up(apart) * step), 0.0)

    vecs = Box(
        ffn_bias=("d", ffn_in_bias),
        shifts=("d", model_biases),
        gains=("d", norm_gains),
    )
    wq_cuts = [("d", qkv_weight, columns_of(layer, 3)) for layer in range(LAYERS)]

    def weight_fetch(layer):
        return Box(
            wo=("f", out_weight) + layer_of(layer, (D, D)),
            w1=("f", ffn_in_weight) + columns_of(layer, 4),
            w2=("f", ffn_out_weight) + rows_of(layer, 4),
        )

    x = tokens
    wq = wq_cuts[0]
    saved = []
    deps = ()
    for layer in range(LAYERS):
        last = layer == LAYERS - 1
        hidden = last and fast
        fetches = Box(hid_send=("f", saved[0].hid) + half_of(rows, False)) if hidden else Box()
        x_mode = "v" if layer else "d"
        bias = Box(qkv_bias=("d", qkv_bias))
        first, token = project(layer, spot, x, x_mode, wq, bias, cs, fetches, deps)
        hid_got = wide_swap(first.hid_send, ALONG) if hidden else None
        if not layer:
            cm = mask(step + token[0, 0])
        recv = travel(first.state, 1)
        fetches = weight_fetch(layer)
        if not last:
            fetches.wq = ("f", qkv_weight) + columns_of(layer + 1, 3)
        inner, token = inside(spot, first.packed, cm, not last, fetches, (token,))
        weights = inner
        kept, token = layer_forward(
            layer,
            recv,
            x,
            "v" if layer else "d",
            inner,
            weights,
            vecs,
            cs,
            cotangent if last else None,
            (token,),
        )
        kept.packed = first.kept
        kept.xt = first.xt
        kept.sq = inner.sq if last else inner.sq_kept
        kept.vecs = vecs
        saved.append(kept)
        deps = (token,)
        if not last:
            x = kept.s_next
            wq = ("v", inner.wq)

    output = saved[1].output
    one, zero = saved[1], saved[0]
    if not fast:
        grads = [None] * LAYERS
        sums = [None] * LAYERS
        top = one
        for layer in (1, 0):
            kept = saved[layer]
            fetch = Box() if layer == 1 else Box()
            back, token = layer_back(
                layer, spot, top, kept, "v" if layer else "d", weights, vecs, cs, fetch, (token,)
            )
            recv = travel(back.state, -1)
            below = saved[0] if layer == 1 else None
            fetch = weight_fetch(0) if layer == 1 else Box()
            mix, token = mix_back(
                layer, recv, spot, back, kept, cs, cm, wq_cuts[layer], below, fetch, (token,)
            )
            gcol = mix.gcol
            gpk = jnp.concatenate(
                [gcol[n % 2, :, 384 + 576 * (n // 2) : 960 + 576 * (n // 2)] for n in range(4)],
                axis=1,
            )
            grads[layer] = (
                reduce_plain(kept.xt.T, gpk),
                reduce_plain(kept.mixt.T, back.gb1),
                reduce_plain(kept.midt.T, back.gpre),
                reduce_plain(kept.hid, top.gb2),
            )
            sums[layer] = jnp.concatenate(
                [top.sums_a[:3], back.sums_b[:7], mix.sums_c[:3]], axis=0
            )
            top = mix
            weights = mix
        sums = lax.psum(jnp.stack(sums), ("wide", "narrow"))
        grad_qkv, grad_o, grad_in, grad_out = (
            jnp.stack([grads[l][k] for l in range(LAYERS)]) for k in range(4)
        )
        input_grad = mix.grad
    else:
        group = Box()
        ops = Box()

        def send(name, kind, operands, token):
            ops[name] = (kind, operands)
            sent, token = grad_send(kind, spot, operands, (token,))
            ops[name] += (wide_swap(sent, CORE),)
            return token

        def keep(name, order, token):
            kind, operands, got = ops[name]
            found, token = grad_keep(kind, spot, operands, got, order, (token,))
            axes = Box(x=(ACROSS,), y=(ALONG,), both=(ACROSS, ALONG))[order]
            for at, axis in enumerate(axes):
                found["got%d" % at] = wide_swap(found["send%d" % at], axis)
            found.axes = axes
            group[name] = found
            return token

        def forward(names, token):
            sent, token = grad_pass([group[name] for name in names], (token,))
            for name in names:
                for at in halves_of(group[name]):
                    axis = ACROSS + ALONG - group[name].axes[at]
                    group[name]["come%d" % at] = wide_swap(sent.pop(0), axis)
            return token

        def near(names, token):
            found, token = grad_near([group[name] for name in names], (token,))
            return (found.stay, narrow_swap(found.near, NEAR)), token

        def far(kinds, pairs, token):
            found, token = grad_far(kinds, pairs, (token,))
            return (found.own, narrow_swap(found.far, FAR)), token

        def gather(kinds, names, token, *after):
            for name in names:
                group[name].spot = spot
            groups = [group[name] for name in names]
            blocks, token = grad_collect(kinds, groups, (token, *after))
            mine = lax.psum_scatter(blocks, "narrow", scatter_dimension=0, tiled=True)
            return (mine.reshape(mine.shape[1:]),), token

        token = send("o1", "out", (one.gb2t, one.hid), token)
        back1, token = layer_back(
            1, spot, one, one, "v", weights, vecs, cs, Box(), (token,), hid_got
        )
        later1 = travel(back1.state, -1)
        token = send("i1", "inner", (one.midt, back1.gpre), token)
        token = keep("o1", "y", token)
        token = keep("i1", "x", token)
        def features(kept):
            return Box(
                mixt=("f", kept.mixt, [whole_cut], (D, rows)),
                xt=("f", kept.xt, [whole_cut], (D, rows)),
            )

        def mix_operands(mix):
            return mix.mixt.reshape(D, rows), mix.xt.reshape(D, rows), mix.gcol

        fetch = weight_fetch(0)
        fetch.update(features(one))
        mix1, token = mix_back(
            1, later1, spot, back1, one, cs, cm, wq_cuts[1], zero, fetch, (token,)
        )
        token = send("m1", "mix", mix_operands(mix1), token)
        token = forward(["o1"], token)
        token = forward(["i1"], token)
        gb2t_got = wide_swap(mix1.gb2t, ALONG)
        fetch = Box(
            hid=("f", zero.hid) + half_of(rows, True),
            hid_got=("f", hid_got, [lambda ref: ref.at[0]], (rows, FF // 2)),
            midt=("f", zero.midt, [whole_cut], (D, rows)),
        )
        weights = mix1
        back0, token = layer_back(0, spot, mix1, zero, "d", weights, vecs, cs, fetch, (token,))
        later0 = [move(back0.state, -1)]
        token = keep("m1", "both", token)
        pair = (mix1.gb2t, gb2t_got, back0.hid, back0.hid_got)
        token = send("o0", "pair", pair, token)
        both, token = add_up(back0.state, later0[0], (token,))
        later0.append(move(both, -2))
        f1, token = gather(["inner", "out"], ["i1", "o1"], token)
        token = send("i0", "inner", (back0.midt.reshape(D, rows), back0.gpre), token)
        token = forward(["m1"], token)
        token = keep("o0", "x", token)
        token = keep("i0", "both", token)
        mix0, token = mix_back(
            0, later0, spot, back0, zero, cs, cm, wq_cuts[0], None, features(zero), (token,)
        )
        input_grad = mix0.grad
        parts = (mix1.sums_a, back0.sums_b, mix0.sums_c, one.sums_a, back1.sums_b, mix1.sums_c)
        token = send("m0", "mix", mix_operands(mix0), token)
        near_a, token = near(["o0", "m1"], token)
        token = forward(["i0"], token)
        token = keep("m0", "both", token)
        near_b, token = near(["i0"], token)
        sums, token = collect_sums(parts, (token,))
        come = wide_swap(sums, CORE)
        sums, token = add_up(sums, come, (token,))
        come = wide_swap(sums, ACROSS)
        token = forward(["m0"], token)
        sums, token = add_up(sums, come, (token,))
        come = wide_swap(sums, ALONG)
        far_f0, token = far(["inner both", "out", "mix both"], [near_b, near_a], token)
        sums, token = add_up(sums, come, (token,))
        come = narrow_swap(sums, NEAR)
        near_m0, token = near(["m0"], token)
        sums, token = add_up(sums, come, (token,))
        come = narrow_swap(sums, FAR)
        far_m0, token = far(["mix both"], [near_m0], token)
        ffn_grads, token = grad_last("ffn", [far_f0, f1], (0, 0), (token,))
        sums, token = add_up(sums, come, (token,))
        mix_grads, token = grad_last("mix", [far_m0, far_f0], (0, 192), (token,))
        sums = sums[:26].reshape(LAYERS, 13, D)
        grad_qkv, grad_o = mix_grads.first, mix_grads.second
        grad_in, grad_out = ffn_grads.first, ffn_grads.second

    def columns(v):
        width = v.shape[-1] // narrow
        return lax.dynamic_slice_in_dim(v, narrow_at * width, width, axis=v.ndim - 1)

    return (
        output,
        input_grad,
        grad_qkv,
        grad_o,
        grad_in,
        grad_out,
        columns(sums[:, 10:13].reshape(LAYERS, 3 * D)),
        columns(sums[:, 3:7].reshape(LAYERS, FF)),
        columns(jnp.stack([sums[:, 7], sums[:, 0], sums[:, 8], sums[:, 1]], axis=1)),
        columns(jnp.stack([sums[:, 9], sums[:, 2]], axis=1)),
    )


def solution(mesh):
    rows = P(("wide", "narrow"), None)
    placed = (rows, rows, P("wide")) + (P(),) * 8
    return jax.shard_map(
        shards,
        mesh=mesh,
        in_specs=placed,
        out_specs=(rows, rows)
        + (P(None, "wide", "narrow"),) * 4
        + (P(None, "narrow"),) * 2
        + (P(None, None, "narrow"),) * 2,
        check_vma=False,
    )
```

```python
import math

import jax
import jax.numpy as jnp
from jax import lax
from jax.experimental import pallas as pl
from jax.experimental.pallas import tpu as pltpu
from jax.sharding import PartitionSpec as P

D = 768
HEADS = 12
HEAD_DIM = 64
FF = 3072
LAYERS = 2
PAIRS = HEADS // 2
NORM_EPS = 1e-05
LANES = 128
STATE_ROWS = PAIRS * LANES + 16

BF = jnp.bfloat16
F32 = jnp.float32


def nn(a, b):
    return lax.dot_general(a, b, (((1,), (0,)), ((), ())), preferred_element_type=F32)


def nt(a, b):
    return lax.dot_general(a, b, (((1,), (1,)), ((), ())), preferred_element_type=F32)


def tn(a, b):
    return lax.dot_general(a, b, (((0,), (0,)), ((), ())), preferred_element_type=F32)


def low(v):
    return v.astype(BF)


def up(v):
    return v.astype(F32)


def beside(a, b):
    return jnp.concatenate([a, b], axis=1)


def above(a, b):
    return jnp.concatenate([a, b], axis=0)


def softplus(u):
    return jnp.maximum(u, 0.0) + jnp.log1p(jnp.exp(-jnp.abs(u)))


def sigmoid(u):
    return 1.0 / (1.0 + jnp.exp(-u))


def swap(v):
    return pltpu.roll(v, HEAD_DIM, 1)


def lane_of(rows):
    return lax.broadcasted_iota(jnp.int32, (rows, LANES), 1)


def row_mean(v):
    return jnp.mean(v, axis=-1, keepdims=True)


def norm_apply(total, gain, shift):
    centred = total - row_mean(total)
    scale = lax.rsqrt(row_mean(centred * centred) + NORM_EPS)
    normal = centred * scale
    return normal * gain + shift, normal, scale


def norm_back(upstream, normal, scale, gain):
    grad = upstream * gain
    return scale * (grad - row_mean(grad) - normal * row_mean(grad * normal))


def column_sum(v):
    return jnp.sum(v, axis=0, keepdims=True)


def shape(*dims, dtype=F32):
    return jax.ShapeDtypeStruct(dims, dtype)


class Box(dict):
    __getattr__ = dict.__getitem__
    __setattr__ = dict.__setitem__


class Refs:
    def __init__(self):
        self.refs = Box()
        self.copies = Box()
        self.flushes = Box()

    def __getitem__(self, name):
        for copy in self.copies.pop(name, []):
            if copy is not None:
                copy.wait()
        return self.refs[name]

    def __getattr__(self, name):
        return self[name]

    def part(self, name, at):
        copies = self.copies.get(name)
        if copies and copies[at] is not None:
            copies[at].wait()
            copies[at] = None
        return self.refs[name].at[at]

    def done(self, name):
        if name in self.flushes:
            self.flushes[name].start()


def in_hbm(array):
    return pltpu.with_memory_space_constraint(array, pltpu.HBM)


def in_vmem(array):
    return pltpu.with_memory_space_constraint(array, pltpu.VMEM)


def whole_cut(ref):
    return ref


def run(body, ins, outs, deps=(), scratch=None, limit=20, flops=0, nbytes=0):
    scratch = scratch or Box()
    in_names = list(ins)
    out_names = list(outs)
    operands, in_specs, out_shapes, out_specs, scratch_shapes = [], [], [], [], []
    vmem = pl.BlockSpec(memory_space=pltpu.VMEM)
    hbm = pl.BlockSpec(memory_space=pltpu.HBM)
    smem = pl.BlockSpec(memory_space=pltpu.SMEM)
    for name in in_names:
        mode, array = ins[name][:2]
        operands.append(Box(d=in_hbm, r=in_hbm, v=in_vmem).get(mode, whole_cut)(array))
        in_specs.append(Box(v=vmem, s=smem, d=hbm, r=hbm)[mode])
    fetch_names = [name for name in out_names if outs[name][0] == "f"]
    for name in fetch_names:
        operands.append(in_hbm(outs[name][1]))
        in_specs.append(hbm)
    for dep in deps:
        operands.append(in_vmem(dep))
        in_specs.append(vmem)
    copy_count = 0
    plan = []
    for name in in_names:
        if ins[name][0] == "d":
            array = ins[name][1]
            cuts, block = ins[name][2] if len(ins[name]) > 2 else (None, array.shape)
            scratch_shapes.append(
                pltpu.VMEM(block if cuts is None else (len(cuts),) + block, array.dtype)
            )
            plan.append((name, cuts))
            copy_count += 1 if cuts is None else len(cuts)
    for name in out_names:
        mode = outs[name][0]
        if mode == "f":
            array, cuts, block = outs[name][1:4]
            out_shapes.append(pltpu.VMEM((len(cuts),) + block, array.dtype))
            copy_count += len(cuts)
        else:
            given = outs[name][1]
            space = pltpu.HBM if mode == "h" else pltpu.VMEM
            out_shapes.append(space(given.shape, given.dtype))
            if mode == "h":
                scratch_shapes.append(pltpu.VMEM(outs[name][1].shape, outs[name][1].dtype))
                copy_count += 1
        out_specs.append(hbm if mode == "h" else vmem)
    out_shapes.append(pltpu.VMEM((8, LANES), F32))
    out_specs.append(vmem)
    for spec in scratch.values():
        scratch_shapes.append(spec)
    scratch_shapes.append(pltpu.SemaphoreType.DMA((max(copy_count, 1),)))

    def kernel(*refs):
        refs = list(refs)
        sems = refs.pop()
        used = [0]

        def make(source, target):
            copy = pltpu.make_async_copy(source, target, sems.at[used[0]])
            used[0] += 1
            return copy

        n_in, n_fetch, n_out = len(in_names), len(fetch_names), len(out_names)
        in_refs = dict(zip(in_names, refs[:n_in]))
        fetch_refs = dict(zip(fetch_names, refs[n_in : n_in + n_fetch]))
        rest = refs[n_in + n_fetch + len(deps) :]
        out_refs = dict(zip(out_names, rest[:n_out]))
        token = rest[n_out]
        spare = rest[n_out + 1 :]
        io = Refs()
        for name in in_names:
            io.refs[name] = in_refs[name]
        for name, cuts in plan:
            buffer = spare.pop(0)
            io.refs[name] = buffer
            if cuts is None:
                io.copies[name] = [make(in_refs[name], buffer)]
            else:
                io.copies[name] = [
                    make(cut(in_refs[name]), buffer.at[at]) for at, cut in enumerate(cuts)
                ]
            for copy in io.copies[name]:
                copy.start()
        fetches = []
        for name in out_names:
            mode = outs[name][0]
            if mode == "f":
                for at, cut in enumerate(outs[name][2]):
                    source = fetch_refs[name]
                    source = cut(source, io) if len(outs[name]) > 4 else cut(source)
                    fetches.append(make(source, out_refs[name].at[at]))
                io.refs[name] = out_refs[name]
            elif mode == "h":
                buffer = spare.pop(0)
                io.refs[name] = buffer
                io.flushes[name] = make(buffer, out_refs[name])
            else:
                io.refs[name] = out_refs[name]
        for name in scratch:
            io.refs[name] = spare.pop(0)
        for copy in fetches:
            copy.start()
        token[...] = jnp.zeros(token.shape, F32)
        body(io)
        for name in list(io.copies):
            io[name]
        for copy in fetches:
            copy.wait()
        for copy in io.flushes.values():
            copy.wait()

    cost = COSTS[min(Counter.at, len(COSTS) - 1)]
    Counter.at += 1
    results = pl.pallas_call(
        kernel,
        out_shape=tuple(out_shapes),
        in_specs=in_specs,
        out_specs=tuple(out_specs),
        scratch_shapes=scratch_shapes,
        compiler_params=pltpu.CompilerParams(vmem_limit_bytes=limit * 1024 * 1024),
        cost_estimate=pl.CostEstimate(
            flops=int(cost * 10**9), bytes_accessed=10**8, transcendentals=0
        ),
    )(*operands)
    return Box(zip(out_names, results)), results[-1]


def columns_of(layer, parts):
    return [lambda ref, j=j: ref.at[layer, :, pl.ds(D * j, D)] for j in range(parts)], (D, D)


def rows_of(layer, parts):
    return [lambda ref, j=j: ref.at[layer, pl.ds(D * j, D), :] for j in range(parts)], (D, D)


def half_of(rows, own):
    def cut(ref, io):
        along = io.spot[1] if own else 1 - io.spot[1]
        return ref.at[:, pl.ds(pl.multiple_of(along * (FF // 2), LANES), FF // 2)]

    return [cut], (rows, FF // 2), True


def layer_of(layer, block):
    return [lambda ref: ref.at[layer]], block


COSTS = [10, 10, 10, 10, 10, 10, 0.3, 0.3, 0.3, 1, 0.3, 0.3, 0.3, 0.3, 0.3, 15, 1, 0.3, 1, 3, 0.3, 10, 15, 1, 6, 0.3, 0.3, 22, 10, 3, 1, 3, 1, 0.3, 0.3, 6, 3, 0.3, 0.3, 0.3, 0.3, 1]


class Counter:
    at = 0


def project(layer, spot, x, x_mode, wq, vecs, cs, fetches, deps):
    rows = x.shape[0]

    def body(io):
        x_in = up(io.x[...])
        xb = low(x_in)
        io.xt[...] = low(x_in.T)
        io.done("xt")
        lane = lane_of(rows)
        lo = lane < HEAD_DIM
        lane_state = lane_of(LANES)
        lo_state = lane_state < HEAD_DIM
        totals = jnp.zeros((LANES, LANES), F32)
        for j in range(3):
            w = io.part("wq", j)
            bias = vector(io, "qkv_bias", layer)[:, D * j : D * (j + 1)]
            pk = low(nn(xb, w[...]) + bias)
            io.packed[:, D * j : D * (j + 1)] = pk
            io.kept[:, D * j : D * (j + 1)] = pk
            pf = up(pk)
            cs_now = io.cs[...]
            for p in range(2):
                t0, t1, t2 = (
                    pf[:, (3 * p + i) * LANES : (3 * p + i + 1) * LANES] for i in range(3)
                )
                sp0 = softplus(t0)
                sp2 = softplus(t2)
                kf0 = low(jnp.where(lo, swap(sp0), sp0) * cs_now)
                kf1 = low(jnp.where(lo, sp2, swap(sp2)) * cs_now)
                s0 = tn(kf0, low(jnp.where(lo, t1, 1.0)))
                s1 = tn(kf1, low(jnp.where(lo, 1.0, t2)))
                pair = 2 * j + p
                io.state[pair * LANES : (pair + 1) * LANES, :] = low(
                    jnp.where(lo_state, s0, s1)
                )
                totals = jnp.where(lane_state == 2 * pair, swap(s0), totals)
                totals = jnp.where(lane_state == 2 * pair + 1, s1, totals)
        io.state[PAIRS * LANES :, :] = low(totals.T[:16])
        io.done("kept")

    outs = Box(
        packed=("v", shape(rows, 3 * D, dtype=BF)),
        xt=("h", shape(D, rows, dtype=BF)),
        state=("v", shape(STATE_ROWS, LANES, dtype=BF)),
    )
    outs.kept = ("h", shape(rows, 3 * D, dtype=BF))
    outs.update(fetches)
    return run(
        body,
        Box(spot=("s", spot), x=(x_mode, x), wq=wq, cs=("d", cs), **vecs),
        outs,
        deps,
        flops=2 * rows * D * 3 * D,
        nbytes=2 * D * 3 * D,
    )


def inside(spot, packed, cm, long, fetches, deps):
    rows = packed.shape[0]

    def body(io):
        lo = lane_of(rows) < HEAD_DIM
        for pair in range(PAIRS):
            at = pair * 3 * LANES
            t0, t1, t2 = (
                up(io.packed[:, at + i * LANES : at + (i + 1) * LANES]) for i in range(3)
            )
            sp0, sp1, sp2 = softplus(t0), softplus(t1), softplus(t2)
            a0 = nt(low(jnp.where(lo, sp0, 0.0)), low(swap(sp0)))
            a1 = nt(low(jnp.where(lo, 0.0, sp1)), low(swap(sp2)))
            mask = io.cm[...]
            n0 = nn(low(a0 * mask), low(jnp.where(lo, t1, 1.0)))
            n1 = nn(low(a1 * mask), low(jnp.where(lo, 1.0, t2)))
            here = slice(pair * LANES, (pair + 1) * LANES)
            io.num[:, here] = jnp.where(lo, n0, n1)
            io.den[:, here] = swap(jnp.where(lo, n1, n0))
            sq = low(jnp.where(lo, sp0, sp1))
            io.sq[:, here] = sq
            if long:
                io.sq_kept[:, here] = sq

    outs = Box(
        num=("v", shape(rows, D)),
        den=("v", shape(rows, D)),
        sq=("v", shape(rows, D, dtype=BF)),
    )
    if long:
        outs.sq_kept = ("h", shape(rows, D, dtype=BF))

    def body_all(io):
        body(io)
        if long:
            io.done("sq_kept")

    outs.update(fetches)
    return run(
        body_all,
        Box(spot=("s", spot), packed=("v", packed), cm=("d", cm)),
        outs,
        deps,
        flops=4 * HEADS * rows * rows * LANES,
        nbytes=rows * D * 16,
    )


def sum_states(io, count):
    total = up(io.recv0[...])
    for at in range(1, count):
        total = total + up(io["recv%d" % at][...])
    return total


def vector(io, name, layer):
    return up(io[name][...])[layer : layer + 1]


def state_totals(total):
    return jnp.concatenate(
        [total[PAIRS * LANES :], jnp.zeros((LANES - 16, LANES), F32)], axis=0
    ).T


def totals_column(totals, head):
    return jnp.broadcast_to(totals[:, head : head + 1], (LANES, LANES))


def diagonal(a, b):
    zero = jnp.zeros((LANES, LANES), BF)
    return above(beside(a, zero), beside(zero, b))


def second_norm_back(io, gs, n2, r2, gain):
    gz2 = norm_back(gs, n2, r2, gain)
    gb2 = low(gz2)
    io.gz2[...] = gz2
    io.gb2[...] = gb2
    io.gb2t[...] = low(gz2.T)
    io.sums_a[...] = jnp.zeros((8, D), F32)
    io.sums_a[0:1, :] = column_sum(up(gb2))
    io.sums_a[1:2, :] = column_sum(gs)
    io.sums_a[2:3, :] = column_sum(gs * n2)
    io.done("sums_a")


def second_norm_outs(rows):
    return Box(
        gz2=("v", shape(rows, D)),
        gb2=("v", shape(rows, D, dtype=BF)),
        gb2t=("v", shape(D, rows, dtype=BF)),
        sums_a=("h", shape(8, D)),
    )


def layer_forward(layer, recv, x, x_mode, inner, weights, vecs, cs, cotangent, deps):
    rows = x.shape[0]
    last = cotangent is not None

    def body(io):
        lane = lane_of(rows)
        lo = lane < HEAD_DIM
        lo_state = lane_of(LANES) < HEAD_DIM
        before = sum_states(io, len(recv))
        io.before[...] = low(before)
        io.done("before")
        totals = state_totals(before)
        for pair in range(PAIRS):
            here = slice(pair * LANES, (pair + 1) * LANES)
            sq = up(io.sq[:, here])
            other = swap(sq)
            state = before[here]
            cs_now = io.cs[...]
            feats = beside(
                low(jnp.where(lo, sq, other) * cs_now), low(jnp.where(lo, other, sq) * cs_now)
            )
            both = nn(
                feats,
                diagonal(
                    low(jnp.where(lo_state, state, totals_column(totals, 2 * pair))),
                    low(jnp.where(lo_state, totals_column(totals, 2 * pair + 1), state)),
                ),
            )
            n0 = both[:, :LANES]
            n1 = both[:, LANES:]
            num = io.num[:, here] + jnp.where(lo, n0, n1)
            inv = 1.0 / (io.den[:, here] + swap(jnp.where(lo, n1, n0)))
            mixed = num * inv
            io.inv[:, here] = inv
            io.mixed[:, here] = low(mixed)
            io.mixt[here, :] = low(mixed.T)
        io.done("inv")
        io.done("mixed")
        io.done("mixt")
        shifts = up(io.shifts[layer])
        gains = up(io.gains[layer])
        bias = vector(io, "ffn_bias", layer)
        branch = nn(io.mixed[...], io.part("wo", 0)[...]) + shifts[0:1]
        middle, n1, r1 = norm_apply(up(io.x[...]) + branch, gains[0:1], shifts[2:3])
        io.n1[...] = n1
        io.done("n1")
        io.r1[...] = jnp.broadcast_to(r1, (rows, LANES))
        io.done("r1")
        io.midt[...] = low(middle.T)
        io.done("midt")
        mid = low(middle)
        total = middle + shifts[1:2]
        for j in range(FF // D):
            here = slice(D * j, D * (j + 1))
            pre = nn(mid, io.part("w1", j)[...]) + bias[:, here]
            cdf = 0.5 * (1.0 + lax.erf(pre * (1.0 / math.sqrt(2.0))))
            hid = low(pre * cdf)
            io.hid[:, here] = hid
            io.slope[:, here] = low(
                cdf + pre * jnp.exp(-0.5 * pre * pre) * (1.0 / math.sqrt(2.0 * math.pi))
            )
            total = total + nn(hid, io.part("w2", j)[...])
        io.done("hid")
        io.done("slope")
        s_next, n2, r2 = norm_apply(total, gains[1:2], shifts[3:4])
        if last:
            io.output[...] = low(s_next)
            io.done("output")
            second_norm_back(io, up(io.cot[...]), n2, r2, gains[1:2])
        else:
            io.s_next[...] = s_next
            io.n2[...] = n2
            io.done("n2")
            io.r2[...] = jnp.broadcast_to(r2, (rows, LANES))
            io.done("r2")

    ins = Box({"recv%d" % i: ("v", recv[i]) for i in range(len(recv))})
    ins.update(
        Box(
            x=(x_mode, x),
            num=("v", inner.num),
            den=("v", inner.den),
            sq=("v", inner.sq),
            wo=("v", weights.wo),
            w1=("v", weights.w1),
            w2=("v", weights.w2),
            cs=("d", cs),
            **vecs,
        )
    )
    if last:
        ins.cot = ("d", cotangent)
    mode = "v" if last else "h"
    outs = Box(
        before=("h", shape(STATE_ROWS, LANES, dtype=BF)),
        mixed=(mode, shape(rows, D, dtype=BF)),
        mixt=("h", shape(D, rows, dtype=BF)),
        inv=(mode, shape(rows, D)),
        n1=(mode, shape(rows, D)),
        r1=(mode, shape(rows, LANES)),
        midt=(mode, shape(D, rows, dtype=BF)),
        hid=(mode, shape(rows, FF, dtype=BF)),
        slope=(mode, shape(rows, FF, dtype=BF)),
    )
    if last:
        outs.output = ("h", shape(rows, D, dtype=BF))
        outs.update(second_norm_outs(rows))
    else:
        outs.s_next = ("v", shape(rows, D))
        outs.n2 = ("h", shape(rows, D))
        outs.r2 = ("h", shape(rows, LANES))
    return run(
        body,
        ins,
        outs,
        deps,
        limit=20,
        flops=2 * rows * D * (D + 2 * FF),
        nbytes=2 * D * (D + 2 * FF),
    )


def layer_back(layer, spot, top, kept, mode, weights, vecs, cs, fetches, deps, after=None):
    rows = top.gz2.shape[0]

    def body(io):
        lane = lane_of(rows)
        lo = lane < HEAD_DIM
        lane_state = lane_of(LANES)
        lo_state = lane_state < HEAD_DIM
        left_rows = lax.broadcasted_iota(jnp.int32, (LANES, LANES), 0) < HEAD_DIM
        same = low(jnp.where(lo_state == left_rows, 1.0, 0.0))
        gb2 = io.gb2[...]
        gmid = io.gz2[...]
        sums = io.sums_b
        sums[...] = jnp.zeros((8, D), F32)
        for j in range(FF // D):
            here = slice(D * j, D * (j + 1))
            gpre = low(nt(gb2, io.part("w2", j)[...]) * up(io.slope[:, here]))
            io.gpre[:, here] = gpre
            sums[j : j + 1, :] = column_sum(up(gpre))
            gmid = gmid + nt(gpre, io.part("w1", j)[...])
        n1 = io.n1[...]
        gz1 = norm_back(gmid, n1, io.r1[:, :1], up(io.gains[layer])[0:1])
        gb1 = low(gz1)
        io.gz1[...] = gz1
        io.gb1[...] = gb1
        sums[4:5, :] = column_sum(up(gb1))
        sums[5:6, :] = column_sum(gmid)
        sums[6:7, :] = column_sum(gmid * n1)
        io.done("sums_b")
        gmixed = up(low(nt(gb1, io.part("wo", 0)[...])))
        totals = jnp.zeros((LANES, LANES), F32)
        for pair in range(PAIRS):
            here = slice(pair * LANES, (pair + 1) * LANES)
            u = gmixed[:, here] * io.inv[:, here]
            dd = -nn(low(u * up(io.mixed[:, here])), same)
            io.u[:, here] = low(u)
            io.dd[:, here] = low(dd)
            ds = swap(dd)
            sq = up(io.sq[:, here])
            other = swap(sq)
            cs_now = io.cs[...]
            s0 = tn(low(jnp.where(lo, sq, other) * cs_now), low(jnp.where(lo, u, ds)))
            s1 = tn(low(jnp.where(lo, other, sq) * cs_now), low(jnp.where(lo, ds, u)))
            io.state[here, :] = low(jnp.where(lo_state, s0, s1))
            totals = jnp.where(lane_state == 2 * pair, swap(s0), totals)
            totals = jnp.where(lane_state == 2 * pair + 1, s1, totals)
        io.state[PAIRS * LANES :, :] = low(totals.T[:16])

    ins = Box(
        gz2=("v", top.gz2),
        gb2=("v", top.gb2),
        wo=("v", weights.wo),
        w1=("v", weights.w1),
        w2=("v", weights.w2),
    )
    for name in ("slope", "n1", "r1", "inv", "mixed", "sq"):
        ins[name] = (mode, kept[name])
    if after is not None:
        ins.after = ("r", after)
    ins.spot = ("s", spot)
    ins.gains = vecs.gains
    ins.cs = ("d", cs)
    outs = Box(
        gpre=("v", shape(rows, FF, dtype=BF)),
        gb1=("v", shape(rows, D, dtype=BF)),
        gz1=("v", shape(rows, D)),
        u=("v", shape(rows, D, dtype=BF)),
        dd=("v", shape(rows, D, dtype=BF)),
        state=("v", shape(STATE_ROWS, LANES, dtype=BF)),
        sums_b=("h", shape(8, D)),
    )
    outs.update(fetches)
    return run(
        body,
        ins,
        outs,
        deps,
        limit=20,
        flops=2 * rows * D * (D + 2 * FF),
        nbytes=2 * D * (D + 2 * FF),
    )


def mix_back(layer, recv, spot, low_part, kept, cs, cm, wq, below, fetches, deps):
    rows = low_part.u.shape[0]

    def body(io):
        lane = lane_of(rows)
        lo = lane < HEAD_DIM
        lane_state = lane_of(LANES)
        lo_state = lane_state < HEAD_DIM
        one_left = jnp.where(lane == 0, 1.0, 0.0)
        one_right = jnp.where(lane == HEAD_DIM, 1.0, 0.0)
        later = sum_states(io, len(recv))
        later_totals = state_totals(later)
        before = up(io.before[...])
        before_totals = state_totals(before)

        def halves(state, totals, pair):
            first = jnp.where(
                lo_state,
                state,
                jnp.where(lane_state == HEAD_DIM, totals_column(totals, 2 * pair), 0.0),
            )
            second = jnp.where(
                lo_state,
                jnp.where(lane_state == 0, totals_column(totals, 2 * pair + 1), 0.0),
                state,
            )
            return diagonal(low(first), low(second))

        def fold(v, cs_now):
            first = v[:, :LANES] * cs_now
            second = v[:, LANES:] * cs_now
            return jnp.where(lo, first + swap(first), second + swap(second))

        io.cmt[...] = io.cm[...].T
        for pair in range(PAIRS):
            here = slice(pair * LANES, (pair + 1) * LANES)
            at = pair * 3 * LANES
            t0, t1, t2 = (
                up(io.packed[:, at + i * LANES : at + (i + 1) * LANES]) for i in range(3)
            )
            cs_now = io.cs[...]
            mask = io.cm[...]
            sp0, sp1, sp2 = softplus(t0), softplus(t1), softplus(t2)
            sw0 = swap(sp0)
            sw2 = swap(sp2)
            q0 = low(jnp.where(lo, sp0, 0.0))
            k0 = low(jnp.where(lo, sw0, 0.0))
            q1 = low(jnp.where(lo, 0.0, sp1))
            k1 = low(jnp.where(lo, 0.0, sw2))
            kf = beside(
                low(jnp.where(lo, sw0, sp0) * cs_now), low(jnp.where(lo, sp2, sw2) * cs_now)
            )
            v0 = low(jnp.where(lo, t1, one_right))
            v1 = low(jnp.where(lo, one_left, t2))
            uf = up(io.u[:, here])
            ds = swap(up(io.dd[:, here]))
            u0 = low(jnp.where(lo, uf, ds))
            u1 = low(jnp.where(lo, ds, uf))
            ua = low(jnp.where(lo, uf, 0.0))
            ub = low(jnp.where(lo, 0.0, uf))
            mask_t = io.cmt[...]
            pt = beside(low(nt(k0, q0) * mask_t), low(nt(k1, q1) * mask_t))
            d = beside(low(nt(u0, v0) * mask), low(nt(u1, v1) * mask))
            dt = beside(low(nt(v0, u0) * mask_t), low(nt(v1, u1) * mask_t))
            after = later[here]
            eq = nt(beside(u0, u1), halves(before[here], before_totals, pair))
            ek = nt(beside(v0, v1), halves(after, later_totals, pair))
            after_split = above(
                low(jnp.where(lo_state, after, 0.0)), low(jnp.where(lo_state, 0.0, after))
            )
            dq = fold(eq, cs_now) + nn(d, above(k0, k1))
            dk = fold(ek, cs_now) + nn(dt, above(q0, q1))
            dv = nn(beside(kf, pt), jnp.concatenate([after_split, ua, ub], axis=0))
            dks = swap(dk)
            gpk = io.gpk
            gpk[:, at : at + LANES] = low(jnp.where(lo, dq, dks) * sigmoid(t0))
            gpk[:, at + LANES : at + 2 * LANES] = low(jnp.where(lo, dv, dq * sigmoid(t1)))
            gpk[:, at + 2 * LANES : at + 3 * LANES] = low(jnp.where(lo, dks * sigmoid(t2), dv))
        grad = io.gz1[...]
        io.sums_c[...] = jnp.zeros((8, D), F32)
        for j in range(3):
            gpk = io.gpk[:, D * j : D * (j + 1)]
            io.sums_c[j : j + 1, :] = column_sum(up(gpk))
            grad = grad + nt(gpk, io.part("wq", j)[...])
        io.done("sums_c")
        if below is None:
            io.grad[...] = grad
            io.done("grad")
        else:
            gain = up(io.gains[layer - 1])[1:2]
            second_norm_back(io, grad, io.n2[...], io.r2[:, :1], gain)
        near = io.spot[3]
        far = io.spot[4]
        gpk = up(io.gpk[...])
        gb1 = up(io.gb1[...])
        for low_bit in range(2):
            slot = low_bit ^ near
            for source, start in ((gb1, 0), (gpk, D // 2)):
                width = source.shape[1] // 4
                first = source[:, low_bit * width : (low_bit + 1) * width]
                second = source[:, (low_bit + 2) * width : (low_bit + 3) * width]
                both = beside(
                    jnp.where(far == 0, first, second), jnp.where(far == 0, second, first)
                )
                io.gcol[slot, :, start : start + 2 * width] = low(both)

    ins = Box({"recv%d" % i: ("v", recv[i]) for i in range(len(recv))})
    ins.update(
        Box(
            spot=("s", spot),
            u=("v", low_part.u),
            dd=("v", low_part.dd),
            gb1=("v", low_part.gb1),
            gz1=("v", low_part.gz1),
            packed=("d", kept.packed),
            cs=("d", cs),
            cm=("d", cm),
            before=("d", kept.before),
            wq=wq,
        )
    )
    outs = Box(
        gcol=("v", shape(2, rows, 2 * D, dtype=BF)),
        sums_c=("h", shape(8, D)),
    )
    if below is None:
        outs.grad = ("h", shape(rows, D))
    else:
        ins.n2 = ("d", below.n2)
        ins.r2 = ("d", below.r2)
        ins.gains = below.vecs.gains
        outs.update(second_norm_outs(rows))
    outs.update(fetches)
    return run(
        body,
        ins,
        outs,
        deps,
        scratch=Box(gpk=pltpu.VMEM((rows, 3 * D), BF), cmt=pltpu.VMEM((rows, rows), F32)),
        limit=20,
        flops=2 * rows * D * 3 * D + 12 * HEADS * rows * rows * LANES,
        nbytes=2 * D * 3 * D,
    )


def owners(spot, core):
    return [
        ((spot[1] ^ along) * 2 + (spot[2] ^ across)) * 2 + core
        for across in range(2)
        for along in range(2)
    ]


def out_terms(io, core, put):
    near, far = io.spot[3], io.spot[4]
    for at, block in enumerate(owners(io.spot, core)):
        lanes = pl.ds(pl.multiple_of(block * (FF // 8), LANES), FF // 8)
        io.rhs[:, at * (FF // 8) : (at + 1) * (FF // 8)] = io.hid[:, lanes]
    lhs = io.gb2t[...]
    for half in range(2):
        grad = nn(lhs, io.rhs[:, half * D : (half + 1) * D])
        for sub in range(2):
            at = 2 * half + sub
            for n in range(4):
                lanes = pl.ds(pl.multiple_of(((n // 2) ^ far) * (D // 2), LANES), D // 2)
                put(
                    at,
                    (n % 2) ^ near,
                    None,
                    lanes,
                    grad[n * 192 : (n + 1) * 192, sub * (D // 2) : (sub + 1) * (D // 2)],
                )


def pair_terms(io, core, put):
    near, far = io.spot[3], io.spot[4]
    tokens = io.hid.shape[1]
    width = FF // 8
    io.lhs[:, :tokens] = io.gb2t[...]
    io.lhs[:, tokens:] = io.gb2t_got[...]
    for across in range(2):
        block = (io.spot[2] ^ across) * 2 + core
        lanes = pl.ds(pl.multiple_of(block * width, LANES), width)
        io.rhs[:tokens, across * width : (across + 1) * width] = io.hid[0, :, lanes]
        io.rhs[tokens:, across * width : (across + 1) * width] = io.hid_got[0, :, lanes]
    grad = nn(io.lhs[...], io.rhs[...])
    for across in range(2):
        for n in range(4):
            lanes = pl.ds(pl.multiple_of(((n // 2) ^ far) * width, LANES), width)
            put(
                across,
                (n % 2) ^ near,
                None,
                lanes,
                grad[n * 192 : (n + 1) * 192, across * width : (across + 1) * width],
            )


def gather_rows(io, name, target, core):
    for at, block in enumerate(owners(io.spot, core)):
        io[target][at * 96 : (at + 1) * 96, :] = io[name][
            pl.ds(pl.multiple_of(block * 96, 16), 96), :
        ]


def in_terms(io, core, put):
    near, far = io.spot[3], io.spot[4]
    gather_rows(io, "midt", "lhs", core)
    for n in range(4):
        grad = nn(io.lhs[...], io.gpre[:, n * D : (n + 1) * D])
        for at in range(4):
            put(at, (n % 2) ^ near, (n // 2) ^ far, slice(None), grad[at * 96 : (at + 1) * 96])


def mix_terms(io, core, put):
    gather_rows(io, "mixt", "lhs", core)
    gather_rows(io, "xt", "lhs_two", core)
    for slot in range(2):
        for lhs, start, stop in (("lhs", 0, D // 2), ("lhs_two", D // 2, 2 * D)):
            grad = nn(io[lhs][...], io.gcol[slot, :, start:stop])
            for at in range(4):
                put(
                    at,
                    slot,
                    None,
                    slice(start, stop),
                    grad[at * 96 : (at + 1) * 96],
                )


def part_rows(part, count):
    if part is None:
        return slice(None)
    return pl.ds(pl.multiple_of(part * count, 16), count)


TERMS = Box(pair=pair_terms, out=out_terms, inner=in_terms, mix=mix_terms)


def grad_setup(kind, spot, operands):
    ins = Box(spot=("s", spot))
    if kind == "out":
        gb2t, hid = operands
        tokens = gb2t.shape[1]
        ins.gb2t = ("v", gb2t)
        ins.hid = ("v", hid)
        return ins, Box(rhs=pltpu.VMEM((tokens, FF // 2), BF)), (192, D), tokens
    if kind == "pair":
        for name, array in zip(("gb2t", "gb2t_got", "hid", "hid_got"), operands):
            ins[name] = ("v", array)
        tokens = 2 * operands[0].shape[1]
        both = Box(lhs=pltpu.VMEM((D, tokens), BF), rhs=pltpu.VMEM((tokens, D), BF))
        return ins, both, (192, D), tokens
    lhs = pltpu.VMEM((D // 2, operands[0].shape[1]), BF)
    if kind == "inner":
        midt, gpre = operands
        ins.midt = ("v", midt)
        ins.gpre = ("v", gpre)
        return ins, Box(lhs=lhs), (192, D), midt.shape[1]
    mixt, xt, gcol = operands
    ins.mixt = ("v", mixt)
    ins.xt = ("v", xt)
    ins.gcol = ("v", gcol)
    return ins, Box(lhs=lhs, lhs_two=lhs), (96, 2 * D), xt.shape[1]


def grad_send(kind, spot, operands, deps):
    ins, scratch, block, tokens = grad_setup(kind, spot, operands)

    def body(io):
        def put(at, slot, part, lanes, value):
            io.send[at, slot, part_rows(part, value.shape[0]), lanes] = low(value)

        TERMS[kind](io, 1 - io.spot[0], put)

    outs, token = run(
        body,
        ins,
        Box(send=("v", shape(2 if kind == "pair" else 4, 2, *block, dtype=BF))),
        deps,
        scratch=scratch,
        flops=2 * tokens * 8 * block[0] * block[1],
        nbytes=4 * 2 * 2 * block[0] * block[1],
    )
    return outs.send, token


def grad_keep(kind, spot, operands, got, order, deps):
    ins, scratch, block, tokens = grad_setup(kind, spot, operands)
    ins.got = ("v", got)
    rows_all = block[0]
    if order == "both":
        half = (rows_all // 2, block[1])
    else:
        half = block

    def body(io):
        def put(at, slot, part, lanes, value):
            count = value.shape[0]
            rows = part_rows(part, count)
            value = low(value + up(io.got[at, slot, rows, lanes]))
            across, along = at // 2, at % 2
            if kind == "pair":
                io["send0" if at else "keep0"][slot, rows, lanes] = value
            elif order == "x":
                io["send0" if across else "keep0"][along, slot, rows, lanes] = value
            elif order == "y":
                io["send0" if along else "keep0"][across, slot, rows, lanes] = value
            else:
                rows = part_rows(part, count // 2)
                first, second = value[: count // 2], value[count // 2 :]
                io["send0" if across else "keep0"][along, slot, rows, lanes] = first
                io["send1" if along else "keep1"][across, slot, rows, lanes] = second

        TERMS[kind](io, io.spot[0], put)

    names = ["send0", "keep0"] + (["send1", "keep1"] if order == "both" else [])
    return run(
        body,
        ins,
        {
            name: ("v", shape(*((2,) if kind == "pair" else (2, 2)), *half, dtype=BF))
            for name in names
        },
        deps,
        scratch=scratch,
        flops=2 * tokens * 8 * block[0] * block[1],
        nbytes=4 * 2 * 4 * block[0] * block[1],
    )


def grad_pass(groups, deps):
    pairs = [
        (group["keep%d" % at], group["got%d" % at]) for group in groups for at in halves_of(group)
    ]
    ins, outs = Box(), Box()
    for at, (keep, got) in enumerate(pairs):
        ins["keep%d" % at] = ("v", keep)
        ins["got%d" % at] = ("v", got)
        outs["next%d" % at] = ("v", shape(*keep.shape[1:], dtype=BF))

    def body(io):
        for at in range(len(pairs)):
            io["next%d" % at][...] = low(
                up(io["keep%d" % at][1]) + up(io["got%d" % at][1])
            )

    outs, token = run(body, ins, outs, deps)
    return [outs["next%d" % at] for at in range(len(pairs))], token


def halves_of(group):
    return [at for at in range(2) if "keep%d" % at in group]


def group_ins(groups):
    ins = Box()
    for which, group in enumerate(groups):
        for at in halves_of(group):
            for name in ("keep", "got", "come"):
                if "%s%d" % (name, at) in group:
                    ins["%s%d_%d" % (name, which, at)] = ("v", group["%s%d" % (name, at)])
    return ins


def group_sum(io, which, at, slot):
    if "come%d_%d" % (which, at) not in io.refs:
        return up(io["keep%d_%d" % (which, at)][slot]) + up(io["got%d_%d" % (which, at)][slot])
    return (
        up(io["keep%d_%d" % (which, at)][0, slot])
        + up(io["got%d_%d" % (which, at)][0, slot])
        + up(io["come%d_%d" % (which, at)][slot])
    )


def grad_near(groups, deps):
    ins = group_ins(groups)
    places = [(which, at) for which, group in enumerate(groups) for at in halves_of(group)]
    sizes = [groups[which]["keep%d" % at].shape[-2:] for which, at in places]
    total = sum(rows * lanes // D for rows, lanes in sizes)

    def body(io):
        start = 0
        for which, at in places:
            rows, lanes = groups[which]["keep%d" % at].shape[-2:]
            for slot, target in ((1, io.near), (0, io.stay)):
                value = low(group_sum(io, which, at, slot))
                for part in range(lanes // D):
                    here = slice(start + part * rows, start + (part + 1) * rows)
                    target[here, :] = value[:, part * D : (part + 1) * D]
            start += rows * lanes // D

    return run(
        body,
        ins,
        Box(
            near=("v", shape(total, D, dtype=BF)),
            stay=("v", shape(total, D, dtype=BF)),
        ),
        deps,
    )


def grad_collect(kinds, groups, deps):
    ins = group_ins(groups)
    ins.spot = ("s", groups[0].spot)

    def body(io):
        near, far = io.spot[3], io.spot[4]
        for which, kind in enumerate(kinds):
            for slot in range(2):
                full = [group_sum(io, which, at, slot) for at in halves_of(groups[which])]
                if kind == "mix":
                    both = full[0]
                    quarter = D // 4
                    parts = [
                        beside(both[:, :quarter], both[:, 2 * quarter : 5 * quarter]),
                        beside(both[:, quarter : 2 * quarter], both[:, 5 * quarter :]),
                    ]
                elif kind == "inner":
                    parts = [full[0][:96], full[0][96:]]
                else:
                    parts = [
                        beside(full[0][:96, : D // 2], full[0][96:, : D // 2]),
                        beside(full[0][:96, D // 2 :], full[0][96:, D // 2 :]),
                    ]
                for half in range(2):
                    owner = (slot ^ near) + 2 * (half ^ far)
                    io.blocks[owner, which * 96 : (which + 1) * 96, :] = low(parts[half])

    outs, token = run(
        body, ins, Box(blocks=("v", shape(4, 96 * len(kinds), D, dtype=BF))), deps
    )
    return outs.blocks, token


def grad_far(kinds, pairs, deps):
    count = len(kinds)
    ins = Box()
    for at, (stay, near) in enumerate(pairs):
        ins["stay%d" % at] = ("v", stay)
        ins["near%d" % at] = ("v", near)

    def body(io):
        sums = [
            up(io["stay%d" % at][...]) + up(io["near%d" % at][...]) for at in range(len(pairs))
        ]
        full = jnp.concatenate(sums, axis=0)
        for at, kind in enumerate(kinds):
            part = full[192 * at : 192 * (at + 1)]
            here = slice(96 * at, 96 * (at + 1))
            if kind in ("mix", "mix both"):
                if kind == "mix":
                    both = beside(part[:96], part[96:])
                else:
                    both = above(beside(part[:48], part[48:96]), beside(part[96:144], part[144:]))
                quarter = D // 4
                io.own[here, :] = beside(both[:, :quarter], both[:, 2 * quarter : 5 * quarter])
                io.far[here, :] = low(
                    beside(both[:, quarter : 2 * quarter], both[:, 5 * quarter : 8 * quarter])
                )
            elif kind == "out":
                io.own[here, :] = beside(part[:96, : D // 2], part[96:, : D // 2])
                io.far[here, :] = low(beside(part[:96, D // 2 :], part[96:, D // 2 :]))
            else:
                io.own[here, :] = above(part[:48], part[96:144])
                io.far[here, :] = low(above(part[48:96], part[144:]))

    return run(
        body,
        ins,
        Box(
            own=("v", shape(count * 96, D)),
            far=("v", shape(count * 96, D, dtype=BF)),
        ),
        deps,
    )


def grad_last(kind, terms, starts, deps):
    size = 96 if kind == "mix" else 192
    ins = Box()
    for layer in range(LAYERS):
        for at, term in enumerate(terms[layer]):
            ins["term%d_%d" % (layer, at)] = ("v", term)
    if kind == "mix":
        outs = Box(
            first=("h", shape(LAYERS, 96, 3 * D // 4)),
            second=("h", shape(LAYERS, 96, D // 4)),
        )
    else:
        outs = Box(
            first=("h", shape(LAYERS, 96, D)),
            second=("h", shape(LAYERS, FF // 8, D // 4)),
        )

    def body(io):
        for layer in range(LAYERS):
            here = slice(starts[layer], starts[layer] + size)
            full = 0.0
            for at, term in enumerate(terms[layer]):
                ref = io["term%d_%d" % (layer, at)]
                if len(term.shape) == 2:
                    full = full + up(ref[here, :])
                else:
                    full = full + sum(up(ref[part]) for part in range(term.shape[0]))
            if kind == "mix":
                io.first[layer] = full[:, D // 4 :]
                io.second[layer] = full[:, : D // 4]
            else:
                io.first[layer] = full[:96]
                io.second[layer, :, :96] = full[96:, : D // 2].T
                io.second[layer, :, 96:] = full[96:, D // 2 :].T
        io.done("first")
        io.done("second")

    return run(body, ins, outs, deps)


def wide_swap(v, bit):
    size = lax.axis_size("wide")
    return lax.ppermute(v, "wide", [(i, i ^ bit) for i in range(size)])


def narrow_swap(v, bit):
    size = lax.axis_size("narrow")
    return lax.ppermute(v, "narrow", [(i, i ^ bit) for i in range(size)])


CORE, ACROSS, ALONG = 1, 2, 4
NEAR, FAR = 1, 2


def reduce_plain(left, right):
    term = low(tn(left, right))
    part = lax.psum_scatter(term, "narrow", scatter_dimension=1, tiled=True)
    return lax.psum_scatter(up(part), "wide", scatter_dimension=0, tiled=True)


def move(v, shift):
    size = lax.axis_size("narrow")
    pairs = [(i, i + shift) for i in range(size) if 0 <= i + shift < size]
    return lax.ppermute(v, "narrow", pairs)


def travel(state, step):
    return [move(state, step * shift) for shift in range(1, lax.axis_size("narrow"))]


SUM_ROWS = (3, 7, 3)


def collect_sums(parts, after, deps):
    def body(io):
        io.sums[...] = jnp.zeros((32, D), F32)
        start = 0
        for at in range(len(parts)):
            rows = SUM_ROWS[at % 3]
            io.sums[start : start + rows, :] = io["part%d" % at][:rows, :]
            start += rows

    outs, token = run(
        body,
        Box({"part%d" % at: ("d", part) for at, part in enumerate(parts)}, after=("r", after)),
        Box(sums=("v", shape(32, D))),
        deps,
    )
    return outs.sums, token


def add_up(a, b, deps):
    def body(io):
        io.sum[...] = (up(io.a[...]) + up(io.b[...])).astype(a.dtype)

    outs, token = run(
        body,
        Box(a=("v", a), b=("v", b)),
        Box(sum=("v", shape(*a.shape, dtype=a.dtype))),
        deps,
    )
    return outs.sum, token


def shards(
    tokens,
    cotangent,
    horizons,
    qkv_weight,
    out_weight,
    ffn_in_weight,
    ffn_out_weight,
    qkv_bias,
    ffn_in_bias,
    model_biases,
    norm_gains,
):
    Counter.at = 0
    rows = tokens.shape[0]
    wide = lax.axis_size("wide")
    narrow = lax.axis_size("narrow")
    wide_at = lax.axis_index("wide")
    narrow_at = lax.axis_index("narrow")
    fast = wide == 8 and narrow == 4
    place = [wide_at % 2, (wide_at // 4) % 2, (wide_at // 2) % 2, narrow_at % 2, narrow_at // 2]
    if not fast:
        place = [wide_at * 0] * 5
    place.append(narrow_at)
    spot = jnp.stack(place).astype(jnp.int32)
    step = 0.5 * math.pi / up(horizons[0])
    places = up(narrow_at * rows + jnp.arange(rows)) * step
    cs = beside(
        jnp.broadcast_to(jnp.cos(places)[:, None], (rows, HEAD_DIM)),
        jnp.broadcast_to(jnp.sin(places)[:, None], (rows, HEAD_DIM)),
    )

    def mask(step):
        apart = jnp.arange(rows)[:, None] - jnp.arange(rows)[None, :]
        return jnp.where(apart >= 0, jnp.cos(up(apart) * step), 0.0)

    vecs = Box(
        ffn_bias=("d", ffn_in_bias),
        shifts=("d", model_biases),
        gains=("d", norm_gains),
    )
    wq_cuts = [("d", qkv_weight, columns_of(layer, 3)) for layer in range(LAYERS)]

    def weight_fetch(layer):
        return Box(
            wo=("f", out_weight) + layer_of(layer, (D, D)),
            w1=("f", ffn_in_weight) + columns_of(layer, 4),
            w2=("f", ffn_out_weight) + rows_of(layer, 4),
        )

    x = tokens
    wq = wq_cuts[0]
    saved = []
    deps = ()
    for layer in range(LAYERS):
        last = layer == LAYERS - 1
        hidden = last and fast
        fetches = Box(hid_send=("f", saved[0].hid) + half_of(rows, False)) if hidden else Box()
        x_mode = "v" if layer else "d"
        bias = Box(qkv_bias=("d", qkv_bias))
        first, token = project(layer, spot, x, x_mode, wq, bias, cs, fetches, deps)
        hid_got = wide_swap(first.hid_send, ALONG) if hidden else None
        if not layer:
            cm = mask(step + token[0, 0])
        recv = travel(first.state, 1)
        fetches = weight_fetch(layer)
        if not last:
            fetches.wq = ("f", qkv_weight) + columns_of(layer + 1, 3)
        inner, token = inside(spot, first.packed, cm, not last, fetches, (token,))
        weights = inner
        kept, token = layer_forward(
            layer,
            recv,
            x,
            "v" if layer else "d",
            inner,
            weights,
            vecs,
            cs,
            cotangent if last else None,
            (token,),
        )
        kept.packed = first.kept
        kept.xt = first.xt
        kept.sq = inner.sq if last else inner.sq_kept
        kept.vecs = vecs
        saved.append(kept)
        deps = (token,)
        if not last:
            x = kept.s_next
            wq = ("v", inner.wq)

    output = saved[1].output
    one, zero = saved[1], saved[0]
    if not fast:
        grads = [None] * LAYERS
        sums = [None] * LAYERS
        top = one
        for layer in (1, 0):
            kept = saved[layer]
            fetch = Box() if layer == 1 else Box()
            back, token = layer_back(
                layer, spot, top, kept, "v" if layer else "d", weights, vecs, cs, fetch, (token,)
            )
            recv = travel(back.state, -1)
            below = saved[0] if layer == 1 else None
            fetch = weight_fetch(0) if layer == 1 else Box()
            mix, token = mix_back(
                layer, recv, spot, back, kept, cs, cm, wq_cuts[layer], below, fetch, (token,)
            )
            gcol = mix.gcol
            gpk = jnp.concatenate(
                [gcol[n % 2, :, 384 + 576 * (n // 2) : 960 + 576 * (n // 2)] for n in range(4)],
                axis=1,
            )
            grads[layer] = (
                reduce_plain(kept.xt.T, gpk),
                reduce_plain(kept.mixt.T, back.gb1),
                reduce_plain(kept.midt.T, back.gpre),
                reduce_plain(kept.hid, top.gb2),
            )
            sums[layer] = jnp.concatenate(
                [top.sums_a[:3], back.sums_b[:7], mix.sums_c[:3]], axis=0
            )
            top = mix
            weights = mix
        sums = lax.psum(jnp.stack(sums), ("wide", "narrow"))
        grad_qkv, grad_o, grad_in, grad_out = (
            jnp.stack([grads[l][k] for l in range(LAYERS)]) for k in range(4)
        )
        input_grad = mix.grad
    else:
        group = Box()
        ops = Box()

        def send(name, kind, operands, token):
            ops[name] = (kind, operands)
            sent, token = grad_send(kind, spot, operands, (token,))
            ops[name] += (wide_swap(sent, CORE),)
            return token

        def keep(name, order, token):
            kind, operands, got = ops[name]
            found, token = grad_keep(kind, spot, operands, got, order, (token,))
            axes = Box(x=(ACROSS,), y=(ALONG,), both=(ACROSS, ALONG))[order]
            for at, axis in enumerate(axes):
                found["got%d" % at] = wide_swap(found["send%d" % at], axis)
            found.axes = axes
            group[name] = found
            return token

        def forward(names, token):
            sent, token = grad_pass([group[name] for name in names], (token,))
            for name in names:
                for at in halves_of(group[name]):
                    axis = ACROSS + ALONG - group[name].axes[at]
                    group[name]["come%d" % at] = wide_swap(sent.pop(0), axis)
            return token

        def near(names, token):
            found, token = grad_near([group[name] for name in names], (token,))
            return (found.stay, narrow_swap(found.near, NEAR)), token

        def far(kinds, pairs, token):
            found, token = grad_far(kinds, pairs, (token,))
            return (found.own, narrow_swap(found.far, FAR)), token

        def gather(kinds, names, token, *after):
            for name in names:
                group[name].spot = spot
            groups = [group[name] for name in names]
            blocks, token = grad_collect(kinds, groups, (token, *after))
            parts = lax.all_to_all(blocks, "narrow", split_axis=0, concat_axis=0, tiled=True)
            return (parts,), token

        token = send("o1", "out", (one.gb2t, one.hid), token)
        back1, token = layer_back(
            1, spot, one, one, "v", weights, vecs, cs, Box(), (token,), hid_got
        )
        later1 = travel(back1.state, -1)
        token = send("i1", "inner", (one.midt, back1.gpre), token)
        token = keep("o1", "y", token)
        token = keep("i1", "x", token)
        def features(kept):
            return Box(
                mixt=("f", kept.mixt, [whole_cut], (D, rows)),
                xt=("f", kept.xt, [whole_cut], (D, rows)),
            )

        def mix_operands(mix):
            return mix.mixt.reshape(D, rows), mix.xt.reshape(D, rows), mix.gcol

        fetch = weight_fetch(0)
        fetch.update(features(one))
        mix1, token = mix_back(
            1, later1, spot, back1, one, cs, cm, wq_cuts[1], zero, fetch, (token,)
        )
        token = send("m1", "mix", mix_operands(mix1), token)
        token = forward(["o1"], token)
        token = forward(["i1"], token)
        gb2t_got = wide_swap(mix1.gb2t, ALONG)
        fetch = Box(
            hid=("f", zero.hid) + half_of(rows, True),
            hid_got=("f", hid_got, [lambda ref: ref.at[0]], (rows, FF // 2)),
            midt=("f", zero.midt, [whole_cut], (D, rows)),
        )
        weights = mix1
        back0, token = layer_back(0, spot, mix1, zero, "d", weights, vecs, cs, fetch, (token,))
        later0 = [move(back0.state, -1)]
        token = keep("m1", "both", token)
        pair = (mix1.gb2t, gb2t_got, back0.hid, back0.hid_got)
        token = send("o0", "pair", pair, token)
        both, token = add_up(back0.state, later0[0], (token,))
        later0.append(move(both, -2))
        f1, token = gather(["inner", "out"], ["i1", "o1"], token)
        token = send("i0", "inner", (back0.midt.reshape(D, rows), back0.gpre), token)
        token = forward(["m1"], token)
        token = keep("o0", "x", token)
        token = keep("i0", "both", token)
        mix0, token = mix_back(
            0, later0, spot, back0, zero, cs, cm, wq_cuts[0], None, features(zero), (token,)
        )
        input_grad = mix0.grad
        parts = (mix1.sums_a, back0.sums_b, mix0.sums_c, one.sums_a, back1.sums_b, mix1.sums_c)
        token = send("m0", "mix", mix_operands(mix0), token)
        near_a, token = near(["o0", "m1"], token)
        token = forward(["i0"], token)
        token = keep("m0", "both", token)
        near_b, token = near(["i0"], token)
        sums, token = collect_sums(parts, f1[0], (token,))
        come = wide_swap(sums, CORE)
        sums, token = add_up(sums, come, (token,))
        come = wide_swap(sums, ACROSS)
        token = forward(["m0"], token)
        sums, token = add_up(sums, come, (token,))
        come = wide_swap(sums, ALONG)
        far_f0, token = far(["inner both", "out", "mix both"], [near_b, near_a], token)
        sums, token = add_up(sums, come, (token,))
        come = narrow_swap(sums, NEAR)
        near_m0, token = near(["m0"], token)
        sums, token = add_up(sums, come, (token,))
        come = narrow_swap(sums, FAR)
        far_m0, token = far(["mix both"], [near_m0], token)
        ffn_grads, token = grad_last("ffn", [far_f0, f1], (0, 0), (token,))
        sums, token = add_up(sums, come, (token,))
        mix_grads, token = grad_last("mix", [far_m0, far_f0], (0, 192), (token,))
        sums = sums[:26].reshape(LAYERS, 13, D)
        grad_qkv, grad_o = mix_grads.first, mix_grads.second
        grad_in, grad_out = ffn_grads.first, ffn_grads.second

    def columns(v):
        width = v.shape[-1] // narrow
        return lax.dynamic_slice_in_dim(v, narrow_at * width, width, axis=v.ndim - 1)

    return (
        output,
        input_grad,
        grad_qkv,
        grad_o,
        grad_in,
        grad_out,
        columns(sums[:, 10:13].reshape(LAYERS, 3 * D)),
        columns(sums[:, 3:7].reshape(LAYERS, FF)),
        columns(jnp.stack([sums[:, 7], sums[:, 0], sums[:, 8], sums[:, 1]], axis=1)),
        columns(jnp.stack([sums[:, 9], sums[:, 2]], axis=1)),
    )


def solution(mesh):
    rows = P(("wide", "narrow"), None)
    placed = (rows, rows, P("wide")) + (P(),) * 8
    return jax.shard_map(
        shards,
        mesh=mesh,
        in_specs=placed,
        out_specs=(rows, rows)
        + (P(None, "wide", "narrow"),) * 4
        + (P(None, "narrow"),) * 2
        + (P(None, None, "narrow"),) * 2,
        check_vma=False,
    )
```
